32 devices in a mesh: dp: 16 (over z, y, core), tensor: 2 (over x).
Axes of the slice: x: 2, y: 2, z: 4, core: 2. Of those that a mesh axis runs over, the one named last changes fastest.
Arguments:
- inputs: bfloat16 [38912, 432], P(('dp', 'tensor')), may hold values from -6 to 6
- patch_cells: int32 [38912], P(('dp', 'tensor')), may hold values from 0 to 195, as said below
- ln1_gain: float32 [432], replicated, may hold values from 0.25 to 1.75
- ln1_bias: float32 [432], replicated, may hold values from -3 to 3
- w_query: bfloat16 [432, 432], replicated, may hold values from -0.3125 to 0.3125
- w_key: bfloat16 [432, 432], replicated, may hold values from -0.3125 to 0.3125
- w_value: bfloat16 [432, 432], replicated, may hold values from -0.3125 to 0.3125
- w_proj: bfloat16 [432, 432], replicated, may hold values from -1.25 to 1.25
- proj_bias: float32 [432], replicated, may hold values from -3 to 3
- pos_weight: float32 [3, 9], replicated, may hold values from -0.6 to 0.6
- gate_param: float32 [9], replicated, may hold values from -1.5 to 1.5
- ln2_gain: float32 [432], replicated, may hold values from 0.25 to 1.75
- ln2_bias: float32 [432], replicated, may hold values from -3 to 3
- fc1_weight: bfloat16 [432, 1728], P(None, 'tensor'), may hold values from -0.3125 to 0.3125
- fc1_bias: bfloat16 [1728], P('tensor'), may hold values from -3 to 3
- fc2_weight: bfloat16 [1728, 432], P('tensor'), may hold values from -0.21875 to 0.21875
- fc2_bias: float32 [432], replicated, may hold values from -3 to 3
- cotangent: float32 [38912, 432], P(('dp', 'tensor')), may hold values from -6 to 6
Outputs:
- output: bfloat16 [38912, 432], P(('dp', 'tensor'))
- grad_inputs: float32 [38912, 432], P(('dp', 'tensor'))
- grad_ln1_gain: float32 [432], replicated
- grad_ln1_bias: float32 [432], replicated
- grad_query: float32 [432, 432], replicated
- grad_key: float32 [432, 432], replicated
- grad_value: float32 [432, 432], replicated
- grad_proj: float32 [432, 432], replicated
- grad_proj_bias: float32 [432], replicated
- grad_pos_weight: float32 [3, 9], replicated
- grad_gate: float32 [9], replicated
- grad_ln2_gain: float32 [432], replicated
- grad_ln2_bias: float32 [432], replicated
- grad_fc1: float32 [432, 1728], P(None, 'tensor')
- grad_fc1_bias: float32 [1728], P('tensor')
- grad_fc2: float32 [1728, 432], P('tensor')
- grad_fc2_bias: float32 [432], replicated
The draws below stay inside these ranges and needn't reach their ends.
Inputs may be any that keep to these rules, and one draw needn't show every extreme that they name: `patch_cells`: each image's 608 entries are 2 crops of 196 entries and then 6 crops of 36; each crop's entries are a permutation of its grid's cell numbers, row times side plus column.
All inputs are finite; a program needn't handle non-finite values.
Results may differ from the reference program's by a relative error of at most 0.019.
Values may be sent and summed in bfloat16 or wider, within the bound.
A program may use at most 192 MiB of HBM per device.

```python
import jax
import jax.numpy as jnp
from jax import lax

D = 432
HEADS = 9
HEAD_DIM = 48
FF = 1728
BIG_SIDE = 14
SMALL_SIDE = 6
BIG_CROPS = 2
SMALL_CROPS = 6
PER_IMAGE = 608
TOKENS = 38912


def crop_orders(key, crops, cells):
    subkeys = jax.random.split(key, crops)
    return jax.vmap(lambda subkey: jax.random.permutation(subkey, cells))(subkeys).astype(jnp.int32)


def draw_patch_cells(key, part):
    key = jax.random.fold_in(key, 7)
    images = TOKENS // PER_IMAGE
    big = crop_orders(jax.random.fold_in(key, 1), images * BIG_CROPS, BIG_SIDE * BIG_SIDE)
    small = crop_orders(jax.random.fold_in(key, 2), images * SMALL_CROPS, SMALL_SIDE * SMALL_SIDE)
    joined = jnp.concatenate([big.reshape(images, -1), small.reshape(images, -1)], axis=1)
    return joined.reshape(-1)


def draw_pos_weight(key, part):
    key = jax.random.fold_in(key, 11)
    first, second = jax.random.split(key)
    linear = jnp.clip(0.25 * jax.random.normal(first, (2, HEADS), jnp.float32), -0.6, 0.6)
    reach = -jnp.exp(jax.random.uniform(second, (1, HEADS), jnp.float32, jnp.log(0.005), jnp.log(0.05)))
    return jnp.concatenate([linear, reach], axis=0)


def block_levels(stream_key, extent, cuts, least, top_value):
    loudness = 1.0
    for dim, parts in cuts:
        heights = jax.random.uniform(jax.random.fold_in(jax.random.fold_in(stream_key, 6), dim), (parts,), jnp.float32, least / len(cuts), top_value / len(cuts))
        loudness = loudness * jnp.repeat(jnp.exp(heights), extent[dim] // parts).reshape((-1,) + (1,) * (len(extent) - 1 - dim))
    return loudness


def bell_draw(rng, dims, scale, most, pieces=(), dtype=jnp.bfloat16):
    loudness = block_levels(rng, dims, pieces, -0.22, 0.18) if pieces else 1.0
    entries = jax.random.normal(rng, dims, jnp.float32) * scale * loudness
    return jnp.minimum(jnp.maximum(entries, -most), most).astype(dtype)


def setup_inputs(seed: int = 0) -> dict:
    keys = jax.random.split(jax.random.key(seed), 19)
    return {
        "inputs": bell_draw(keys[0], (TOKENS, D), 1.0, 6.0, ((0, 32),)),
        "patch_cells": draw_patch_cells(jax.random.fold_in(keys[18], 71), 0),
        "ln1_gain": jnp.clip(1.0 + 0.15 * jax.random.normal(keys[2], (D,), jnp.float32), 0.25, 1.75),
        "ln1_bias": bell_draw(keys[3], (D,), 0.3, 3.0, (), jnp.float32),
        "w_query": bell_draw(keys[4], (D, D), D ** -0.5, 0.3125),
        "w_key": bell_draw(keys[5], (D, D), D ** -0.5, 0.3125),
        "w_value": bell_draw(keys[6], (D, D), D ** -0.5, 0.3125),
        "w_proj": bell_draw(keys[7], (D, D), (D // 16) ** -0.5, 1.25),
        "proj_bias": bell_draw(keys[8], (D,), 0.3, 3.0, (), jnp.float32),
        "pos_weight": draw_pos_weight(jax.random.fold_in(keys[18], 71), 0),
        "gate_param": jnp.clip(jax.random.uniform(keys[10], (HEADS,), jnp.float32, -1.5, 1.5), -1.5, 1.5),
        "ln2_gain": jnp.clip(1.0 + 0.15 * jax.random.normal(keys[11], (D,), jnp.float32), 0.25, 1.75),
        "ln2_bias": bell_draw(keys[12], (D,), 0.3, 3.0, (), jnp.float32),
        "fc1_weight": bell_draw(keys[13], (D, FF), D ** -0.5, 0.3125, ((1, 2),)),
        "fc1_bias": bell_draw(keys[14], (FF,), 0.5, 3.0, ((0, 2),)),
        "fc2_weight": bell_draw(keys[15], (FF, D), (FF // 2) ** -0.5, 0.21875, ((0, 2),)),
        "fc2_bias": bell_draw(keys[16], (D,), 0.3, 3.0, (), jnp.float32),
        "cotangent": bell_draw(keys[17], (TOKENS, D), 1.0, 6.0, ((0, 32),), jnp.float32),
    }


@jax.custom_vjp
def low(v):
    return lax.optimization_barrier(v.astype(jnp.bfloat16)).astype(jnp.float32)

@jax.custom_vjp
def low_back(v):
    return v

def low_keep(v):
    return (low(v), None)

def low_pass(kept, grad):
    return (grad,)

def back_keep(v):
    return (v, None)

def back_low(kept, grad):
    return (low(grad),)
low.defvjp(low_keep, low_pass)
low_back.defvjp(back_keep, back_low)
EPS = 1e-06

def matmul(left_mat, right_mat):
    return jnp.dot(left_mat, right_mat, precision=lax.Precision.HIGHEST, preferred_element_type=jnp.float32)

def layer_norm(values, gain_vec, shift_vec):
    center = values - lax.optimization_barrier(jnp.mean(values, axis=-1, keepdims=True))
    spread = lax.optimization_barrier(jnp.mean(center * center, axis=-1, keepdims=True))
    return center * lax.rsqrt(spread + EPS) * gain_vec + shift_vec

def split_groups(array_in):
    images = array_in.shape[0] // PER_IMAGE
    tail = array_in.shape[1:]
    per_image = array_in.reshape((images, PER_IMAGE) + tail)
    boundary = BIG_CROPS * BIG_SIDE * BIG_SIDE
    big = per_image[:, :boundary].reshape((images * BIG_CROPS, BIG_SIDE * BIG_SIDE) + tail)
    small = per_image[:, boundary:].reshape((images * SMALL_CROPS, SMALL_SIDE * SMALL_SIDE) + tail)
    return (big, small)

def join_groups(big, small):
    images = big.shape[0] // BIG_CROPS
    tail = big.shape[2:]
    joined = jnp.concatenate([big.reshape((images, -1) + tail), small.reshape((images, -1) + tail)], axis=1)
    return joined.reshape((-1,) + tail)

def offsets(cells, grid_side):
    row_at = (cells // grid_side).astype(jnp.float32)
    col_at = (cells % grid_side).astype(jnp.float32)
    col_off = col_at[:, None, :] - col_at[:, :, None]
    row_off = row_at[:, None, :] - row_at[:, :, None]
    return (col_off, row_off, col_off * col_off + row_off * row_off)

def position_logits(cells, grid_side, pos_weight):
    col_off, row_off, dist_sq = offsets(cells, grid_side)
    return pos_weight[0][None, :, None, None] * col_off[:, None] + pos_weight[1][None, :, None, None] * row_off[:, None] + pos_weight[2][None, :, None, None] * dist_sq[:, None]

def heads_view(rows):
    return rows.reshape(rows.shape[:-1] + (HEADS, HEAD_DIM))

def group_attend(queries, keys_in, values_in, cells, grid_side, pos_weight, gate_param):
    scores = low_back(jnp.einsum('clhe,cmhe->chlm', queries, keys_in, precision=lax.Precision.HIGHEST) * HEAD_DIM ** (-0.5))
    content = jax.nn.softmax(scores, axis=-1)
    position = jax.nn.softmax(position_logits(cells, grid_side, pos_weight), axis=-1)
    gating = jax.nn.sigmoid(gate_param)[None, :, None, None]
    mixture = low((1.0 - gating) * content + gating * position)
    attended = jnp.einsum('chlm,cmhe->clhe', mixture, values_in, precision=lax.Precision.HIGHEST)
    return attended.reshape(attended.shape[:2] + (HEADS * HEAD_DIM,))

def project_heads(rows, weight):
    return low_back(low(matmul(rows, weight)))

def image_attention(image_rows, image_cells, w_query, w_key, w_value, pos_weight, gate_param):
    query_parts = split_groups(project_heads(image_rows, w_query))
    key_parts = split_groups(project_heads(image_rows, w_key))
    value_parts = split_groups(project_heads(image_rows, w_value))
    cell_parts = split_groups(image_cells)
    sides = (BIG_SIDE, SMALL_SIDE)
    results = []
    for group_index in range(2):
        results.append(group_attend(heads_view(query_parts[group_index]), heads_view(key_parts[group_index]), heads_view(value_parts[group_index]), cell_parts[group_index], sides[group_index], pos_weight, gate_param))
    return low_back(low(join_groups(results[0], results[1])))

def forward(inputs, patch_cells, ln1_gain, ln1_bias, w_query, w_key, w_value, w_proj, proj_bias, pos_weight, gate_param, ln2_gain, ln2_bias, fc1_weight, fc1_bias, fc2_weight, fc2_bias):
    normed_one = low(layer_norm(inputs, ln1_gain, ln1_bias))
    images = inputs.shape[0] // PER_IMAGE
    per_rows = normed_one.reshape(images, PER_IMAGE, normed_one.shape[1])
    per_cells = patch_cells.reshape(images, PER_IMAGE)

    def one_image(pair):
        return image_attention(pair[0], pair[1], w_query, w_key, w_value, pos_weight, gate_param)
    attended = lax.map(jax.checkpoint(one_image), (per_rows, per_cells)).reshape(inputs.shape)
    middle = inputs + low_back(matmul(attended, w_proj) + proj_bias)
    normed_two = low(layer_norm(middle, ln2_gain, ln2_bias))
    before = low_back(matmul(normed_two, fc1_weight) + fc1_bias)
    hidden = low(jax.nn.gelu(before, approximate=False))
    return middle + low_back(matmul(hidden, fc2_weight) + fc2_bias)

def reference(inputs, patch_cells, ln1_gain, ln1_bias, w_query, w_key, w_value, w_proj, proj_bias, pos_weight, gate_param, ln2_gain, ln2_bias, fc1_weight, fc1_bias, fc2_weight, fc2_bias, cotangent):
    floats = [array_in.astype(jnp.float32) for array_in in (inputs, ln1_gain, ln1_bias, w_query, w_key, w_value, w_proj, proj_bias, pos_weight, gate_param, ln2_gain, ln2_bias, fc1_weight, fc1_bias, fc2_weight, fc2_bias)]

    def closed(*params):
        return forward(params[0], patch_cells, *params[1:])
    result, pullback = jax.vjp(closed, *floats)
    grads = pullback(cotangent.astype(jnp.float32))
    return (result.astype(jnp.bfloat16), grads[0], grads[1], grads[2], grads[3], grads[4], grads[5], grads[6], grads[7], grads[8], grads[9], grads[10], grads[11], grads[12], grads[13], grads[14], grads[15])
```

```python
import functools

import jax
import jax.numpy as jnp
from jax import lax
from jax.experimental import pallas as pl
from jax.experimental.pallas import tpu as pltpu
from jax.sharding import PartitionSpec as P

MESH = pl.DeviceIdType.MESH

HEADS = 9
HEAD_DIM = 48
BIG_SIDE = 14
SMALL_SIDE = 6
BIG_CROPS = 2
SMALL_CROPS = 6
PER_IMAGE = 608
BIG = BIG_SIDE * BIG_SIDE
SMALL = SMALL_SIDE * SMALL_SIDE
GROUPS = 3

EPS = 1e-06
F32 = jnp.float32
BF16 = jnp.bfloat16
LOG2E = 1.4426950408889634
SCALE = HEAD_DIM ** (-0.5)
FAR = -1e30

NN = (((1,), (0,)), ((), ()))
NT = (((1,), (1,)), ((), ()))
TN = (((0,), (0,)), ((), ()))

LANES = 128
TOK = 256
KEYS_BIG = 208
STRIDE = 40
KEYS_SMALL = SMALL_CROPS * STRIDE
WIDE = 384
CHUNK = 256
TILE = (16, LANES)
SMALL_ROWS = 32


def dot(left, right, dims=NN):
    return lax.dot_general(left, right, dims, preferred_element_type=F32)


def round_up(count, unit):
    return (count + unit - 1) // unit * unit


def iota(shape, dim):
    return lax.broadcasted_iota(jnp.int32, shape, dim)


def lane_crop():
    token = iota((1, TOK), 1).astype(F32)
    return jnp.floor((token + 0.5) * (1.0 / STRIDE))


def grid_place(cell, side):
    row = jnp.floor((cell + 0.5) * (1.0 / side))
    return row, cell - side * row


def offsets(big):
    keys = KEYS_BIG if big else STRIDE
    side = BIG_SIDE if big else SMALL_SIDE
    key = iota((keys, TOK), 0).astype(F32)
    query = iota((keys, TOK), 1).astype(F32)
    if not big:
        query = query - STRIDE * lane_crop()
    row_j, col_j = grid_place(key, side)
    row_i, col_i = grid_place(query, side)
    col_off = col_j - col_i
    row_off = row_j - row_i
    return col_off, row_off, col_off * col_off + row_off * row_off, key < side * side


def extra_rows(big):
    feature = iota((16, TOK), 0)
    cell = iota((1, TOK), 1).astype(F32)
    if not big:
        cell = cell - STRIDE * lane_crop()
    query = jnp.where(feature == 0, 1.0, 0.0)
    key = jnp.where((feature == 0) & (cell > (BIG if big else SMALL) - 0.5), FAR, 0.0)
    return query.astype(BF16), key.astype(BF16)


def own_crop(full):
    crop = lane_crop()
    result = full[:STRIDE]
    for c in range(1, SMALL_CROPS):
        result = jnp.where(crop == c, full[c * STRIDE : (c + 1) * STRIDE], result)
    return result


def all_crops(own):
    crop = lane_crop()
    return jnp.concatenate([jnp.where(crop == c, own, 0.0) for c in range(SMALL_CROPS)], axis=0)


def whole(values):
    return values


def norm_columns(values):
    center = values - jnp.mean(values, axis=0, keepdims=True)
    inverse = lax.rsqrt(jnp.mean(center * center, axis=0, keepdims=True) + EPS)
    return center * inverse, inverse


def norm_back(grad_normed, scaled, inverse, gain):
    e = grad_normed * gain
    return inverse * (
        e
        - jnp.mean(e, axis=0, keepdims=True)
        - scaled * jnp.mean(e * scaled, axis=0, keepdims=True)
    )


class Plan:
    def __init__(self, dp, tensor, rows, width, share):
        self.dp, self.tensor = dp, tensor
        self.solo = dp == 1
        self.rows, self.width, self.share = rows, width, share
        self.images = rows // PER_IMAGE
        self.windows = 3 * self.images
        self.lanes = round_up(rows, CHUNK)
        self.padded = round_up(share, LANES)
        self.tiles = self.padded // LANES
        self.mains = self.padded // CHUNK
        self.tails = (self.padded % CHUNK) // LANES * ((tensor + 1) // 2)
        self.steps = tensor * self.mains + self.tails
        self.hidden = CHUNK * self.steps
        self.tall = width + 16
        self.tile_rows = self.tall // 16
        self.cores = 1 if self.solo else 2
        self.pairs = 1 if self.solo else 2
        self.quads = dp // (self.cores * self.pairs)
        self.mlp_blocks = round_up(self.tiles * self.tile_rows, self.pairs * self.quads)
        self.width_tiles = width // LANES
        self.left_over = width % LANES
        self.full_blocks = self.width_tiles * (width // 16)
        self.fold = round_up(width // 2, 16)
        whole = self.full_blocks + self.fold // 16
        self.att_blocks = round_up(whole, self.cores * self.pairs * self.quads)
        piece = self.att_blocks // (self.cores * self.pairs * self.quads)
        self.att_arrived = self.att_blocks + tensor * piece
        around = tensor - 1 + 1 + self.quads - 1
        self.sem_weights = 4 * tensor
        self.sem_steps = 2 * self.steps + (tensor - 1) * self.tiles
        self.sem_mlp = 2 + 2 * self.quads
        self.sem_att = 2 * (1 + around)
        self.sem_small = 1 + around
        self.semaphores = (
            self.sem_weights + self.sem_steps + self.sem_mlp + 4 * self.sem_att + self.sem_small
        )


class Links:
    def __init__(self, plan, send, recv):
        self.plan, self.send, self.recv = plan, send, recv
        self.next = 0
        self.started = []
        if plan.solo:
            self.d = self.t = self.core = self.pair = self.quad = 0
        else:
            self.d = lax.axis_index("dp")
            self.t = lax.axis_index("tensor")
            self.core = self.d % 2
            self.pair = (self.d // 2) % 2
            self.quad = self.d // 4

    def take(self, count):
        first = self.next
        self.next += count
        return first

    def group(self, name):
        plan, d, t = self.plan, self.d, self.t
        if name == "core":
            return plan.cores, self.core, lambda k: (d - self.core + k, t)
        if name == "tensor":
            return plan.tensor, t, lambda k: (d, k)
        if name == "pair":
            return plan.pairs, self.pair, lambda k: (d + 2 * (k - self.pair), t)
        return plan.quads, self.quad, lambda k: (d + 4 * (k - self.quad), t)

    def barrier(self):
        if self.plan.solo:
            return
        semaphore = pltpu.get_barrier_semaphore()
        count = 0
        for name in ("core", "tensor", "pair", "quad"):
            size, me, peer = self.group(name)
            for step in range(1, size):
                pl.semaphore_signal(
                    semaphore,
                    inc=1,
                    device_id=peer(lax.rem(me + step, size)),
                    device_id_type=MESH,
                )
                count += 1
        pl.semaphore_wait(semaphore, count)

    def copy(self, source, target, number, device):
        return pltpu.make_async_remote_copy(
            src_ref=source,
            dst_ref=target,
            send_sem=self.send.at[number],
            recv_sem=self.recv.at[number],
            device_id=device,
            device_id_type=MESH,
        )

    def put(self, make):
        self.copy(*make()).start()
        self.started.append(make)

    def drain(self):
        for make in self.started:
            self.copy(*make()).wait_send()


class Reduction:
    def __init__(self, links, part, length, arrived, full, full_start, groups, gathers, shared=None, stage=None, stage_sem=None):
        self.links, self.part, self.arrived, self.full = links, part, arrived, full
        self.full_start, self.stage, self.stage_sem = full_start, stage, stage_sem
        self.terms = []
        self.length = length
        self.used = 0
        self.queue = []
        groups = [name for name in groups if links.group(name)[0] > 1]
        gathers = [name for name in gathers if links.group(name)[0] > 1]
        if shared and links.group(shared)[0] == 1:
            shared = None
        for at, name in enumerate(groups):
            self.queue.append(functools.partial(self.scatter, name))
            self.queue.append(functools.partial(self.add, name, at == len(groups) - 1 and not shared))
        if shared:
            self.queue.append(functools.partial(self.share, shared))
            self.queue.append(functools.partial(self.shared, shared))
        for name in gathers:
            self.queue.append(functools.partial(self.gather, name))
            self.queue.append(functools.partial(self.gathered, name))

    def start(self):
        if self.queue:
            self.queue.pop(0)()

    def advance(self):
        self.start()
        self.start()

    def place(self):
        return sum(me * piece for me, piece in self.terms)

    def scatter(self, name):
        size, me, peer = self.links.group(name)
        piece = self.length // size
        self.first = first = self.links.take(size - 1)
        terms, used = tuple(self.terms), self.used

        def make(step):
            to = lax.rem(me + step, size)
            offset = sum(who * part for who, part in terms) + to * piece
            return (
                self.part.at[pl.ds(offset, piece)],
                self.arrived.at[pl.ds(used + (step - 1) * piece, piece)],
                first + step - 1,
                peer(to),
            )

        for step in range(1, size):
            self.links.put(functools.partial(make, step))

    def add(self, name, last):
        size, me, peer = self.links.group(name)
        piece = self.length // size
        self.terms.append((me, piece))
        mine = pl.ds(self.place(), piece)
        total = self.part[mine].astype(F32)
        for step in range(1, size):
            slot = pl.ds(self.used + (step - 1) * piece, piece)
            ref = self.arrived.at[slot]
            self.links.copy(
                ref, ref, self.first + step - 1, peer(lax.rem(me + step, size))
            ).wait_recv()
            total += self.arrived[slot].astype(F32)
        self.used += (size - 1) * piece
        self.length = piece
        if last and self.stage is not None:
            self.stage[...] = total.astype(BF16)
            target = self.full.at[pl.ds(self.full_start + self.place(), piece)]
            copy = pltpu.make_async_copy(self.stage, target, self.stage_sem)
            copy.start()
            copy.wait()
        elif last:
            self.full[pl.ds(self.full_start + self.place(), piece)] = total.astype(BF16)
        else:
            self.part[mine] = total.astype(BF16)

    def share(self, name):
        size, me, peer = self.links.group(name)
        self.first = first = self.links.take(size - 1)
        length, used = self.length, self.used
        mine = pl.ds(used + me * length, length)
        self.arrived[mine] = self.part[pl.ds(self.place(), length)]

        def make(step):
            ref = self.arrived.at[pl.ds(used + me * length, length)]
            return ref, ref, first + step - 1, peer(lax.rem(me + step, size))

        for step in range(1, size):
            self.links.put(functools.partial(make, step))

    def shared(self, name):
        size, me, peer = self.links.group(name)
        for step in range(1, size):
            source = lax.rem(me + size - step, size)
            ref = self.arrived.at[pl.ds(self.used + source * self.length, self.length)]
            self.links.copy(ref, ref, self.first + step - 1, peer(source)).wait_recv()
        total = self.arrived[pl.ds(self.used, self.length)].astype(F32)
        for other in range(1, size):
            total += self.arrived[pl.ds(self.used + other * self.length, self.length)].astype(F32)
        self.full[pl.ds(self.full_start + self.place(), self.length)] = total.astype(BF16)

    def gather(self, name):
        size, me, peer = self.links.group(name)
        self.first = first = self.links.take(size - 1)
        terms, length = tuple(self.terms), self.length

        def make(step):
            offset = self.full_start + sum(who * part for who, part in terms)
            mine = self.full.at[pl.ds(offset, length)]
            return mine, mine, first + step - 1, peer(lax.rem(me + step, size))

        for step in range(1, size):
            self.links.put(functools.partial(make, step))

    def gathered(self, name):
        size, me, peer = self.links.group(name)
        self.terms = [term for term in self.terms if term[0] is not me]
        for step in range(1, size):
            source = lax.rem(me + size - step, size)
            offset = self.full_start + self.place() + source * self.length
            ref = self.full.at[pl.ds(offset, self.length)]
            self.links.copy(ref, ref, self.first + step - 1, peer(source)).wait_recv()
        self.length = self.length * size


def block_kernel(
    stop,
    plan,
    x_ref,
    cells_ref,
    cot_ref,
    wq_ref,
    wk_ref,
    wv_ref,
    wp_ref,
    fc1_ref,
    fb1_ref,
    fc2_ref,
    g1_ref,
    b1_ref,
    pb_ref,
    g2_ref,
    b2_ref,
    fb2_ref,
    posw_ref,
    gate_ref,
    out_ref,
    gi_ref,
    mlp_ref,
    att_ref,
    small_ref,
    x_s,
    cot_s,
    w_s,
    w_t,
    share_s,
    fc_s,
    fc_t,
    vec_s,
    hot,
    norm_s,
    ncan,
    qkv,
    att_t,
    pos_b,
    pos_s,
    con_b,
    con_s,
    att_s,
    mid_s,
    n2_s,
    cb_s,
    hid,
    dbef,
    gm_s,
    acc,
    mlp_part,
    mlp_core,
    mlp_tensor,
    mlp_sum,
    mlp_arrived,
    att_part,
    att_arrived,
    stage_s,
    small_s,
    small_arrived,
    local_sem,
    send_sem,
    recv_sem,
):
    D, rows, lanes = plan.width, plan.rows, plan.lanes
    windows = plan.windows
    links = Links(plan, send_sem, recv_sem)
    t, core = links.t, links.core
    other_core = (links.d + 1 - 2 * core, t)

    def local(source, target, number):
        return pltpu.make_async_copy(source, target, local_sem.at[number])

    loads = [
        local(x_ref, x_s, 0),
        local(fc1_ref, share_s.at[0], 1),
        local(fc2_ref, share_s.at[1], 2),
        local(wq_ref, w_s.at[0], 3),
        local(wk_ref, w_s.at[1], 4),
        local(wv_ref, w_s.at[2], 5),
        local(wp_ref, w_s.at[3], 6),
        local(cot_ref, cot_s, 7),
    ]
    for load in loads:
        load.start()
    links.barrier()

    parts = [part for part in ("main", "tail") if (plan.mains if part == "main" else plan.tails)]

    def hidden_lanes(owner, holder, part):
        turn = lax.rem(owner - holder - 1 + plan.tensor, plan.tensor)
        if part == "main":
            count = plan.mains * CHUNK
            start = turn * count + jnp.where(turn == plan.tensor - 1, plan.tails * CHUNK, 0)
        else:
            count = LANES
            start = (plan.tensor - 1) * plan.mains * CHUNK + owner * LANES
        return pl.ds(pl.multiple_of(start, LANES), count)

    first_weight = links.take(4 * plan.tensor)
    loads[1].wait()
    loads[2].wait()
    for part in parts:
        to = hidden_lanes(t, t, part)
        low = 0 if part == "main" else plan.mains * CHUNK
        high = min(plan.share, low + (plan.mains * CHUNK if part == "main" else LANES))
        for kind in range(2):
            values = share_s[kind, :, low:high]
            if kind == 0:
                bias = fb1_ref[:, low:high].astype(F32)
            else:
                bias = jnp.zeros((1, high - low), F32)
            bias = jnp.where(iota((16, high - low), 0) == 0, bias, 0.0).astype(BF16)
            values = jnp.concatenate([values, bias], axis=0)
            if to.size > high - low:
                fill = jnp.zeros((plan.tall, to.size - high + low), BF16)
                values = jnp.concatenate([values, fill], axis=1)
            fc_s[kind, :, to] = values

    def send_weights(step, at):
        to = lax.rem(t + step, plan.tensor)
        return (
            fc_s.at[core, :, hidden_lanes(t, t, parts[at])],
            fc_s.at[core, :, hidden_lanes(t, to, parts[at])],
            first_weight + 2 * step + at,
            (links.d, to),
        )

    def arrived_weights(step, at, kind):
        source = lax.rem(t + plan.tensor - step, plan.tensor)
        ref = fc_s.at[kind, :, hidden_lanes(source, t, parts[at])]
        return ref, ref, first_weight + 2 * step + at, (links.d, source)

    def handed_weights(step, at, kind):
        ref, _, number, _ = arrived_weights(step, at, kind)
        return links.copy(ref, ref, number + 2 * plan.tensor, other_core)

    weight_copies = [(step, at) for step in range(1, plan.tensor) for at in range(len(parts))]
    for step, at in weight_copies:
        links.put(functools.partial(send_weights, step, at))

    def pass_weights():
        for step, at in weight_copies:
            links.copy(*arrived_weights(step, at, core)).wait_recv()
            handed_weights(step, at, core).start()

    def wait_weights():
        for step, at in weight_copies:
            handed_weights(step, at, 1 - core).wait_recv()
            handed_weights(step, at, core).wait_send()

    for number, ref in enumerate((g1_ref, b1_ref, pb_ref, g2_ref, b2_ref, fb2_ref)):
        for tile in range(round_up(D, LANES) // LANES):
            low, high = tile * LANES, min(D, tile * LANES + LANES)
            spread = jnp.broadcast_to(ref[:, low:high], (LANES, high - low))
            vec_s[number, low:high, :] = jnp.transpose(spread)
    GAIN1, BIAS1, PBIAS, GAIN2, BIAS2, FBIAS2 = range(6)

    def position(h, carry):
        w0, w1, w2 = posw_ref[0, h], posw_ref[1, h], posw_ref[2, h]
        sig = 1.0 / (1.0 + jnp.exp(-jnp.full((1, TOK), gate_ref[0, h], F32)))
        for big, store in ((True, pos_b), (False, pos_s)):
            col_off, row_off, dist, live = offsets(big)
            logits = jnp.where(live, w0 * col_off + w1 * row_off + w2 * dist, FAR)
            top = jnp.max(logits, axis=0, keepdims=True)
            e = jnp.exp(logits - top)
            store[h] = e * (sig / jnp.sum(e, axis=0, keepdims=True))
        return carry

    lax.fori_loop(0, HEADS, position, 0)
    acc[...] = jnp.zeros(acc.shape, F32)
    small_s[...] = jnp.zeros(small_s.shape, F32)
    for number in range(3, 7):
        loads[number].wait()
    for number in range(4):
        w_t[number] = jnp.transpose(w_s[number])
    if stop == 1:
        return

    loads[0].wait()

    def for_blocks(body):
        def one(b, carry):
            body(pl.ds(pl.multiple_of(b * LANES, LANES), LANES), LANES)
            return carry

        lax.fori_loop(0, rows // LANES, one, 0)
        if rows % LANES:
            body(pl.ds(rows // LANES * LANES, rows % LANES), rows % LANES)

    def norm_one(at, count):
        scaled, _ = norm_columns(x_s[:, at].astype(F32))
        normed = scaled * vec_s[GAIN1, :, :count] + vec_s[BIAS1, :, :count]
        norm_s[:, at] = normed.astype(BF16)

    for_blocks(norm_one)
    if rows < lanes:
        norm_s[:, rows:] = jnp.zeros((D, lanes - rows), BF16)

    def window_start(w):
        first = (w // 3) * PER_IMAGE + (w % 3) * BIG
        return first, pl.multiple_of(first // LANES * LANES, LANES)

    def project(w, carry):
        first, start = window_start(w)
        at = iota((1, WIDE), 1) + start
        inside = at - first
        crop = jnp.floor((inside.astype(F32) + 0.5) * (1.0 / SMALL)).astype(jnp.int32)
        is_small = w % 3 == 2
        count = jnp.where(is_small, SMALL_CROPS * SMALL, BIG)
        token = cells_ref[:, pl.ds(start, WIDE)] + jnp.where(is_small, crop * STRIDE, 0)
        token = jnp.where((inside >= 0) & (inside < count), token, -1)
        one_hot = jnp.where(iota((TOK, WIDE), 0) == token, 1.0, 0.0).astype(BF16)
        hot[w] = one_hot
        canonical = dot(norm_s[:, pl.ds(start, WIDE)], one_hot, NT).astype(BF16)
        ncan[w] = canonical
        for part in range(3):
            qkv[w, part * D : part * D + D, :] = dot(w_t[part], canonical).astype(BF16)
        return carry

    lax.fori_loop(0, windows, project, 0)
    if stop == 2:
        return

    extra_b = extra_rows(True)
    extra_s = extra_rows(False)

    def head_rows(part, h):
        return pl.ds(pl.multiple_of(part * D + h * HEAD_DIM, 16), HEAD_DIM)

    def window_kind(w):
        image, slot = w // 3, w % 3
        if slot < 2:
            return KEYS_BIG, pos_b, con_b, image * BIG_CROPS + slot, extra_b, whole, whole
        return KEYS_SMALL, pos_s, con_s, image, extra_s, own_crop, all_crops

    def forward_head(h, carry):
        sig = 1.0 / (1.0 + jnp.exp(-jnp.full((1, TOK), gate_ref[0, h], F32)))
        for w in range(windows):
            keys, pos, con, place, (extra_q, extra_k), pick, spread = window_kind(w)
            q = jnp.concatenate([qkv[w, head_rows(0, h), :], extra_q], axis=0)
            k = jnp.concatenate([qkv[w, head_rows(1, h), :], extra_k], axis=0)
            v = qkv[w, head_rows(2, h), :]
            s = pick(dot(k[:, :keys], q, TN))
            top = jnp.max(s, axis=0, keepdims=True)
            e = jnp.exp2((s - top) * (SCALE * LOG2E))
            content = e * (1.0 / jnp.sum(e, axis=0, keepdims=True))
            con[h, place] = content.astype(BF16)
            mixture = spread((1.0 - sig) * content + pos[h]).astype(BF16)
            att_t[w, head_rows(0, h), :] = dot(v[:, :keys], mixture).astype(BF16)
        if not plan.solo:
            pl.when(h == HEADS - 3)(pass_weights)
        return carry

    lax.fori_loop(0, HEADS, forward_head, 0)
    if stop == 3:
        return

    def scatter_back(target, w, values):
        _, start = window_start(w)
        at = pl.ds(start, WIDE)
        target[:, at] += sum(dot(value, hot[w]) for value in values)

    att_s[...] = jnp.zeros(att_s.shape, F32)

    def attended_back(w, carry):
        scatter_back(att_s, w, [att_t[w]])
        return carry

    lax.fori_loop(0, windows, attended_back, 0)

    if not plan.solo:
        wait_weights()

    def turn_weights(b, carry):
        at = pl.ds(pl.multiple_of(b * LANES, LANES), LANES)
        for kind in range(2):
            fc_t[kind, at, :] = jnp.transpose(fc_s[kind, :, at])
        return carry

    lax.fori_loop(0, plan.hidden // LANES, turn_weights, 0)

    loads[7].wait()
    def norm_two(at, count):
        values = dot(w_t[3], att_s[:, at].astype(BF16))
        middle = x_s[:, at].astype(F32) + values + vec_s[PBIAS, :, :count]
        mid_s[:, at] = middle
        scaled, _ = norm_columns(middle)
        n2_s[:D, at] = (scaled * vec_s[GAIN2, :, :count] + vec_s[BIAS2, :, :count]).astype(BF16)
        rounded = cot_s[:, at].astype(BF16)
        cb_s[:D, at] = rounded
        acc[3, :D, :count] += rounded.astype(F32)
        att_s[:, at] = middle + vec_s[FBIAS2, :, :count]

    for_blocks(norm_two)
    gm_s[...] = jnp.zeros(gm_s.shape, F32)
    n2_s[D:, :] = jnp.where(iota((16, rows), 0) == 0, 1.0, 0.0).astype(BF16)
    cb_s[D:, :] = jnp.zeros((16, rows), BF16)
    if stop == 4:
        return

    spans = [(low, min(CHUNK, rows - low)) for low in range(0, rows, CHUNK)]

    def activate(s, slot):
        cs = pl.ds(pl.multiple_of(s * CHUNK, CHUNK), CHUNK)
        for low, count in spans:
            at = pl.ds(low, count)
            before = dot(fc_t[0, cs, :], n2_s[:, at])
            dh = dot(fc_t[1, cs, :], cb_s[:, at])
            cdf = 0.5 * (1.0 + lax.erf(before * 0.7071067811865476))
            density = jnp.exp(-0.5 * before * before) * 0.3989422804014327
            hid[slot, :, at] = (before * cdf).astype(BF16)
            dbef[slot, :, at] = (dh * (cdf + before * density)).astype(BF16)

    def consume(s, slot):
        cs = pl.ds(pl.multiple_of(s * CHUNK, CHUNK), CHUNK)
        for kind, left, right in ((0, n2_s, dbef), (1, cb_s, hid)):
            grad = dot(left[...], right[slot], NT).astype(BF16)
            for half in range(2):
                blocks = grad[:, half * LANES : half * LANES + LANES]
                mlp_part[kind, s, half] = blocks.reshape((plan.tile_rows,) + TILE)
        for low, count in spans:
            at = pl.ds(low, count)
            att_s[:, at] += dot(fc_s[1, :D, cs], hid[slot, :, at])
            gm_s[:, at] += dot(fc_s[0, :D, cs], dbef[slot, :, at])

    first_core = links.take(plan.steps)
    first_tensor = links.take((plan.tensor - 1) * plan.tiles)
    others = (plan.tensor - 1) * plan.mains
    own = others + plan.tails

    def core_copy(s):
        return links.copy(mlp_part.at[1 - core, s], mlp_core.at[s], first_core + s, other_core)

    def core_send(s):
        core_copy(s).start()

    def core_sum(s):
        links.copy(mlp_core.at[s], mlp_core.at[s], first_core + s, other_core).wait_recv()
        total = mlp_part[core, s].astype(F32) + mlp_core[s].astype(F32)
        mlp_part[core, s] = total.astype(BF16)

    def tensor_copy(s, half, tile, turn):
        to = lax.rem(t + 1 + turn, plan.tensor)
        return (
            mlp_part.at[core, s, half],
            mlp_tensor.at[turn, tile],
            first_tensor + turn * plan.tiles + tile,
            (links.d, to),
        )

    def tensor_send_main(s):
        turn, pair = s // plan.mains, s % plan.mains
        for half in range(2):
            links.copy(*tensor_copy(s, half, 2 * pair + half, turn)).start()

    def tensor_send_tail(s):
        for half in range(2):
            owner = 2 * (s - others) + half
            turn = lax.rem(owner - t - 1 + plan.tensor, plan.tensor)

            def send(turn=turn, half=half):
                links.copy(*tensor_copy(s, half, plan.tiles - 1, turn)).start()

            pl.when(turn < plan.tensor - 1)(send)

    def exchange(s):
        core_sum(s)
        if others:
            pl.when(s < others)(lambda: tensor_send_main(s))
        if plan.tails and plan.tensor > 1:
            pl.when((s >= others) & (s < own))(lambda: tensor_send_tail(s))

    activate(0, 0)

    def mlp_step(s, carry):
        consume(s - 1, (s - 1) % 2)
        activate(s, s % 2)
        if not plan.solo:
            core_send(s - 1)
            pl.when(s >= 2)(lambda: exchange(s - 2))
        return carry

    lax.fori_loop(1, plan.steps, mlp_step, 0)
    last = plan.steps - 1
    consume(last, last % 2)
    if not plan.solo:
        core_send(last)
        exchange(last - 1)
    if stop == 5:
        return

    def norm_two_back(at, count):
        n2_s[:D, at] = att_s[:, at].astype(BF16)
        grad = gm_s[:, at]
        scaled, inverse = norm_columns(mid_s[:, at])
        back = norm_back(grad, scaled, inverse, vec_s[GAIN2, :, :count])
        grad_middle = cot_s[:, at] + back
        cot_s[:, at] = grad_middle
        branch = grad_middle.astype(BF16)
        norm_s[:, at] = branch
        acc[0, :D, :count] += grad * scaled
        acc[1, :D, :count] += grad
        acc[2, :D, :count] += branch.astype(F32)

    for_blocks(norm_two_back)
    store_out = local(n2_s.at[pl.ds(0, D)], out_ref, 8)
    store_out.start()

    mlp_sums = []

    def start_mlp_sums():
        exchange(last)
        for turn in range(plan.tensor - 1):
            for tile in range(plan.tiles):
                ref = mlp_tensor.at[turn, tile]
                number = first_tensor + turn * plan.tiles + tile
                source = lax.rem(t - turn - 1 + plan.tensor, plan.tensor)
                links.copy(ref, ref, number, (links.d, source)).wait_recv()
        for tile in range(plan.tiles):
            if tile < 2 * plan.mains:
                step, half = own + tile // 2, tile % 2
            else:
                step, half = others + t // 2, t % 2
            total = mlp_part[core, step, half].astype(F32)
            for turn in range(plan.tensor - 1):
                total += mlp_tensor[turn, tile].astype(F32)
            at = pl.ds(tile * plan.tile_rows, plan.tile_rows)
            mlp_sum[at] = total.astype(BF16)
        spare = plan.mlp_blocks - plan.tiles * plan.tile_rows
        if spare:
            mlp_sum[plan.mlp_blocks - spare :] = jnp.zeros((spare,) + TILE, BF16)
        reduction = Reduction(
            links,
            mlp_sum,
            plan.mlp_blocks,
            mlp_arrived,
            mlp_ref,
            core * plan.mlp_blocks,
            ("pair", "quad"),
            ("quad", "pair", "core"),
            stage=stage_s,
            stage_sem=local_sem.at[10],
        )
        mlp_sums.append(reduction)
        reduction.start()

    wide = pl.ds(round_up(D, LANES), D)
    gm_s[:, wide] = jnp.zeros((D, D), F32)

    def project_back(w, carry):
        _, start = window_start(w)
        canonical = dot(norm_s[:, pl.ds(start, WIDE)], hot[w], NT).astype(BF16)
        gm_s[:, wide] += dot(att_t[w], canonical, NT)
        att_t[w] = dot(w_s[3], canonical).astype(BF16)
        return carry

    lax.fori_loop(0, windows, project_back, 0)
    if not plan.solo:
        start_mlp_sums()
    if stop == 6:
        return

    def att_start(number, total):
        gm_s[:, :D] = total
        for tile in range(plan.width_tiles):
            blocks = gm_s[:, tile * LANES : tile * LANES + LANES].astype(BF16)
            at = tile * (D // 16)
            att_part[number, at : at + D // 16] = blocks.reshape((D // 16,) + TILE)
        edge = gm_s[:, plan.width_tiles * LANES : plan.width_tiles * LANES + LANES]
        low = D - plan.fold
        lane = iota((low, LANES), 1)
        folded = jnp.where(
            lane < plan.left_over, edge[:low], pltpu.roll(edge[plan.fold :], plan.left_over, 1)
        )
        at = plan.full_blocks
        att_part[number, at : at + low // 16] = folded.astype(BF16).reshape((low // 16,) + TILE)
        if low < plan.fold:
            rows_left = edge[low : plan.fold].astype(BF16)
            att_part[number, at + low // 16 : at + plan.fold // 16] = rows_left.reshape(
                ((plan.fold - low) // 16,) + TILE
            )
        spare = plan.att_blocks - at - plan.fold // 16
        if spare:
            att_part[number, plan.att_blocks - spare :] = jnp.zeros((spare,) + TILE, BF16)

    att_sums = [
        Reduction(
            links,
            att_part.at[number],
            plan.att_blocks,
            att_arrived.at[number],
            att_ref.at[number],
            0,
            ("core", "pair", "quad"),
            ("quad", "pair", "core"),
            "tensor",
        )
        for number in range(GROUPS + 1)
    ]

    att_start(0, gm_s[:, wide])
    att_sums[0].start()

    def weight_grad(g):
        def joined(w):
            parts = [
                qkv[w, pl.ds(pl.multiple_of(part * D + g * (D // GROUPS), 16), D // GROUPS), :]
                for part in range(3)
            ]
            return jnp.concatenate(parts, axis=0)

        total = dot(ncan[0], joined(0), NT)
        for w in range(1, windows):
            total += dot(ncan[w], joined(w), NT)
        att_start(1 + g, total)

    a0, a1, a2, a3 = att_sums
    slots = {
        0: [a0.advance],
        1: [a0.advance, "mlp"],
        2: [a0.advance, "mlp", a1.start],
        3: [a0.advance, "mlp", a1.advance],
        4: [a0.advance, "mlp", a1.advance],
        5: [a0.advance, a1.advance, "mlp", a2.start],
        6: [a0.advance, a1.advance, a2.advance],
        7: [a0.advance, a1.advance, a2.advance],
        8: [a1.advance, a2.advance, a3.start],
    }

    def backward_head(h, carry):
        sig = 1.0 / (1.0 + jnp.exp(-jnp.full((1, TOK), gate_ref[0, h], F32)))
        keep = 1.0 - sig
        sums = [0.0, 0.0]
        gate_row = jnp.zeros((1, TOK), F32)
        for w in range(windows):
            keys, pos, con, place, _, pick, spread = window_kind(w)
            q = qkv[w, head_rows(0, h), :]
            k = qkv[w, head_rows(1, h), :keys]
            v = qkv[w, head_rows(2, h), :keys]
            da = att_t[w, head_rows(0, h), :]
            content = con[h, place].astype(F32)
            grad_mix = pick(dot(v, da, TN))
            mixture = spread(keep * content + pos[h]).astype(BF16)
            row = jnp.sum(content * grad_mix, axis=0, keepdims=True)
            grad_s = spread(content * (grad_mix - row)).astype(BF16)
            sums[w % 3 // 2] += grad_mix
            gate_row -= row
            factor = keep * SCALE
            qkv[w, head_rows(0, h), :] = (dot(k, grad_s) * factor).astype(BF16)
            qkv[w, head_rows(1, h), :keys] = (dot(q, grad_s, NT) * factor[:, :keys]).astype(BF16)
            qkv[w, head_rows(2, h), :keys] = dot(da, mixture, NT).astype(BF16)
        results = [jnp.zeros((1, TOK), F32)] * 3
        for big, pos, grad_mix in ((True, pos_b, sums[0]), (False, pos_s, sums[1])):
            col_off, row_off, dist, _ = offsets(big)
            row = jnp.sum(pos[h] * grad_mix, axis=0, keepdims=True) / sig
            grad_l = pos[h] * (grad_mix - row)
            gate_row += row
            results = [
                old + jnp.sum(grad_l * off, axis=0, keepdims=True)
                for old, off in zip(results, (col_off, row_off, dist))
            ]
        results = jnp.concatenate(results + [gate_row * sig * keep], axis=0)
        column = jnp.sum(results, axis=1, keepdims=True)
        lane = iota((4, LANES), 1)
        small_s[24:28, :] += jnp.where(lane == h, column, 0.0)
        pl.when(h % (HEADS // GROUPS) == HEADS // GROUPS - 1)(
            lambda: weight_grad(h // (HEADS // GROUPS))
        )
        if not plan.solo:
            for at, actions in slots.items():

                def act(actions=actions):
                    for action in actions:
                        if action == "mlp":
                            mlp_sums[0].advance()
                        else:
                            action()

                pl.when(h == at)(act)
        return carry

    lax.fori_loop(0, HEADS, backward_head, 0)
    if stop == 7:
        return

    att_s[...] = jnp.zeros(att_s.shape, F32)

    def norm_grad(w, carry):
        grad = dot(w_s[0], qkv[w, :D, :])
        grad += dot(w_s[1], qkv[w, D : 2 * D, :])
        grad += dot(w_s[2], qkv[w, 2 * D :, :])
        high = grad.astype(BF16)
        low = (grad - high.astype(F32)).astype(BF16)
        scatter_back(att_s, w, [high, low])
        return carry

    for w in range(0, windows, 2):
        lax.fori_loop(w, min(w + 2, windows), norm_grad, 0)
        if not plan.solo:
            a1.advance()
            a2.advance()
            a3.advance()

    def norm_one_back(at, count):
        scaled, inverse = norm_columns(x_s[:, at].astype(F32))
        grad = att_s[:, at]
        cot_s[:, at] += norm_back(grad, scaled, inverse, vec_s[GAIN1, :, :count])
        acc[4, :D, :count] += grad * scaled
        acc[5, :D, :count] += grad

    for_blocks(norm_one_back)
    store_gi = local(cot_s, gi_ref, 9)
    store_gi.start()
    for number in range(6):
        for tile in range(round_up(D, LANES) // LANES):
            turned = jnp.transpose(acc[number, tile * LANES : tile * LANES + LANES, :])
            at = number * 4 + tile
            small_s[at : at + 1, :] = jnp.sum(turned, axis=0, keepdims=True)

    used = 0
    for name in ("core", "tensor", "pair", "quad"):
        size, me, peer = links.group(name)
        if size == 1:
            continue
        first = links.take(size - 1)
        small_arrived[used + me] = small_s[...]

        def make(step, used=used, me=me, size=size, first=first, peer=peer):
            slot = small_arrived.at[used + me]
            return slot, slot, first + step - 1, peer(lax.rem(me + step, size))

        for step in range(1, size):
            links.put(functools.partial(make, step))
        for item in att_sums:
            item.advance()
        for step in range(1, size):
            source = lax.rem(me + size - step, size)
            ref = small_arrived.at[used + source]
            links.copy(ref, ref, first + step - 1, peer(source)).wait_recv()
        total = small_arrived[used]
        for other in range(1, size):
            total += small_arrived[used + other]
        small_s[...] = total
        used += size
    small_ref[...] = small_s[...]
    while any(item.queue for item in att_sums + mlp_sums):
        for item in mlp_sums + att_sums:
            item.advance()
    store_out.wait()
    store_gi.wait()
    if not plan.solo:
        for s in range(plan.steps):
            core_copy(s).wait_send()
        for s in range(others):
            turn, pair = s // plan.mains, s % plan.mains
            for half in range(2):
                links.copy(*tensor_copy(s, half, 2 * pair + half, turn)).wait_send()
        if plan.tails:
            for turn in range(plan.tensor - 1):
                owner = lax.rem(t + 1 + turn, plan.tensor)
                links.copy(
                    *tensor_copy(others + owner // 2, owner % 2, plan.tiles - 1, turn)
                ).wait_send()
    links.drain()


def finish_kernel(
    plan,
    mlp_ref,
    att_ref,
    small_ref,
    dq_ref,
    dk_ref,
    dv_ref,
    dproj_ref,
    dfc1_ref,
    dfb1_ref,
    dfc2_ref,
    pos_ref,
    gate_ref,
    *vector_refs
):
    D = plan.width
    for kind, target in enumerate((dfc1_ref, dfc2_ref)):
        for tile in range(plan.tiles):
            at = kind * plan.mlp_blocks + tile * plan.tile_rows
            values = mlp_ref[at : at + plan.tile_rows].reshape(plan.tall, LANES).astype(F32)
            low, high = tile * LANES, min(plan.share, tile * LANES + LANES)
            target[:, low:high] = values[:D, : high - low]
            if kind == 0:
                dfb1_ref[:, low:high] = values[D : D + 1, : high - low]
    low = D - plan.fold
    part = D // GROUPS
    for number in range(GROUPS + 1):
        tiles = [
            att_ref[number, tile * (D // 16) : (tile + 1) * (D // 16)]
            .reshape(D, LANES)
            .astype(F32)
            for tile in range(plan.width_tiles)
        ]
        at = plan.full_blocks
        folded = att_ref[number, at : at + plan.fold // 16].reshape(plan.fold, LANES).astype(F32)
        lower = pltpu.roll(folded, LANES - plan.left_over, 1)[:low]
        edge = jnp.concatenate([folded, lower], axis=0)[:, : plan.left_over]
        total = jnp.concatenate(tiles + [edge], axis=1)
        if number == 0:
            dproj_ref[...] = total
        else:
            for place, target in enumerate((dq_ref, dk_ref, dv_ref)):
                g = number - 1
                target[:, g * part : g * part + part] = total[:, place * part : place * part + part]
    for number, target in enumerate(vector_refs):
        for tile in range(round_up(D, LANES) // LANES):
            low, high = tile * LANES, min(D, tile * LANES + LANES)
            row = number * 4 + tile
            target[:, low:high] = small_ref[row : row + 1, : high - low]
    pos_ref[...] = small_ref[24:27, :HEADS]
    gate_ref[...] = small_ref[27:28, :HEADS]


def local(
    stop,
    dp,
    tensor,
    inputs,
    patch_cells,
    ln1_gain,
    ln1_bias,
    w_query,
    w_key,
    w_value,
    w_proj,
    proj_bias,
    pos_weight,
    gate_param,
    ln2_gain,
    ln2_bias,
    fc1_weight,
    fc1_bias,
    fc2_weight,
    fc2_bias,
    cotangent,
):
    rows, D = inputs.shape
    share = fc1_weight.shape[1]
    plan = Plan(dp, tensor, rows, D, share)
    windows, lanes, steps = plan.windows, plan.lanes, plan.steps

    def vector(values):
        return values.reshape(1, -1)

    vmem = pl.BlockSpec(memory_space=pltpu.VMEM)
    smem = pl.BlockSpec(memory_space=pltpu.SMEM)
    anywhere = pl.BlockSpec(memory_space=pl.ANY)
    wide = round_up(D, LANES)
    cells = jnp.pad(patch_cells, (0, lanes - rows))
    params = {} if plan.solo else {"collective_id": 0, "has_side_effects": True}
    sizes = [links for links in (plan.cores, plan.tensor, plan.pairs, plan.quads) if links > 1]
    out, gi, mlp, att, small = pl.pallas_call(
        functools.partial(block_kernel, stop, plan),
        out_shape=(
            jax.ShapeDtypeStruct((D, rows), BF16),
            jax.ShapeDtypeStruct((D, rows), F32),
            jax.ShapeDtypeStruct((2 * plan.mlp_blocks,) + TILE, BF16),
            jax.ShapeDtypeStruct((GROUPS + 1, plan.att_blocks) + TILE, BF16),
            jax.ShapeDtypeStruct((SMALL_ROWS, LANES), F32),
        ),
        in_specs=[anywhere, vmem] + [anywhere] * 6 + [vmem] + [anywhere] + [vmem] * 6 + [smem] * 2,
        out_specs=(anywhere, anywhere, anywhere, vmem, vmem),
        scratch_shapes=[
            pltpu.VMEM((D, rows), BF16),
            pltpu.VMEM((D, rows), F32),
            pltpu.VMEM((4, D, D), BF16),
            pltpu.VMEM((4, D, D), BF16),
            pltpu.VMEM((2, D, share), BF16),
            pltpu.VMEM((2, plan.tall, plan.hidden), BF16),
            pltpu.VMEM((2, plan.hidden, plan.tall), BF16),
            pltpu.VMEM((6, D, LANES), F32),
            pltpu.VMEM((windows, TOK, WIDE), BF16),
            pltpu.VMEM((D, lanes), BF16),
            pltpu.VMEM((windows, D, TOK), BF16),
            pltpu.VMEM((windows, 3 * D, TOK), BF16),
            pltpu.VMEM((windows, D, TOK), BF16),
            pltpu.VMEM((HEADS, KEYS_BIG, TOK), F32),
            pltpu.VMEM((HEADS, STRIDE, TOK), F32),
            pltpu.VMEM((HEADS, BIG_CROPS * plan.images, KEYS_BIG, TOK), BF16),
            pltpu.VMEM((HEADS, plan.images, STRIDE, TOK), BF16),
            pltpu.VMEM((D, lanes), F32),
            pltpu.VMEM((D, lanes), F32),
            pltpu.VMEM((plan.tall, rows), BF16),
            pltpu.VMEM((plan.tall, rows), BF16),
            pltpu.VMEM((2, CHUNK, rows), BF16),
            pltpu.VMEM((2, CHUNK, rows), BF16),
            pltpu.VMEM((D, lanes), F32),
            pltpu.VMEM((6, wide, LANES), F32),
            pltpu.VMEM((2, steps, 2, plan.tile_rows) + TILE, BF16),
            pltpu.VMEM((steps, 2, plan.tile_rows) + TILE, BF16),
            pltpu.VMEM((max(1, tensor - 1), plan.tiles, plan.tile_rows) + TILE, BF16),
            pltpu.VMEM((plan.mlp_blocks,) + TILE, BF16),
            pltpu.VMEM((plan.mlp_blocks,) + TILE, BF16),
            pltpu.VMEM((GROUPS + 1, plan.att_blocks) + TILE, BF16),
            pltpu.VMEM((GROUPS + 1, plan.att_arrived) + TILE, BF16),
            pltpu.VMEM((plan.mlp_blocks // (plan.pairs * plan.quads),) + TILE, BF16),
            pltpu.VMEM((SMALL_ROWS, LANES), F32),
            pltpu.VMEM((max(1, sum(sizes)), SMALL_ROWS, LANES), F32),
            pltpu.SemaphoreType.DMA((11,)),
            pltpu.SemaphoreType.DMA((plan.semaphores,)),
            pltpu.SemaphoreType.DMA((plan.semaphores,)),
        ],
        compiler_params=pltpu.CompilerParams(vmem_limit_bytes=63 * 1024 * 1024, **params),
    )(
        inputs.T,
        vector(cells),
        cotangent.T,
        w_query,
        w_key,
        w_value,
        w_proj,
        fc1_weight,
        vector(fc1_bias),
        fc2_weight.T,
        vector(ln1_gain),
        vector(ln1_bias),
        vector(proj_bias),
        vector(ln2_gain),
        vector(ln2_bias),
        vector(fc2_bias),
        pos_weight,
        vector(gate_param),
    )
    square = jax.ShapeDtypeStruct((D, D), F32)
    results = pl.pallas_call(
        functools.partial(finish_kernel, plan),
        out_shape=(square,) * 4
        + (
            jax.ShapeDtypeStruct((D, share), F32),
            jax.ShapeDtypeStruct((1, share), F32),
            jax.ShapeDtypeStruct((D, share), F32),
            jax.ShapeDtypeStruct((3, HEADS), F32),
            jax.ShapeDtypeStruct((1, HEADS), F32),
        )
        + (jax.ShapeDtypeStruct((1, D), F32),) * 6,
        in_specs=[vmem] * 3,
        out_specs=(vmem,) * 15,
        compiler_params=pltpu.CompilerParams(vmem_limit_bytes=32 * 1024 * 1024),
    )(mlp, att, small)
    dq, dk, dv, dproj, dfc1, dfb1, dfc2, pos, gate = results[:9]
    gain2, bias2, pbias, fbias2, gain1, bias1 = (item.reshape(D) for item in results[9:])
    return (
        out.T,
        gi.T,
        gain1,
        bias1,
        dq,
        dk,
        dv,
        dproj,
        pbias,
        pos,
        gate.reshape(HEADS),
        gain2,
        bias2,
        dfc1,
        dfb1.reshape(share),
        dfc2.T,
        fbias2,
    )


def solution(mesh, stop=0):
    both = ("dp", "tensor")
    copied = P()
    in_specs = (
        (P(both, None), P(both))
        + (copied,) * 11
        + (P(None, "tensor"), P("tensor"), P("tensor", None), copied, P(both, None))
    )
    out_specs = (
        (P(both, None), P(both, None))
        + (copied,) * 11
        + (P(None, "tensor"), P("tensor"), P("tensor", None), copied)
    )
    return jax.shard_map(
        functools.partial(local, stop, mesh.shape["dp"], mesh.shape["tensor"]),
        mesh=mesh,
        in_specs=in_specs,
        out_specs=out_specs,
        check_vma=False,
    )
```

```python
import functools

import jax
import jax.numpy as jnp
from jax import lax
from jax.experimental import pallas as pl
from jax.experimental.pallas import tpu as pltpu
from jax.sharding import PartitionSpec as P

MESH = pl.DeviceIdType.MESH

MLP_STEP = 2.1
NORM_TIME = 2.5
PROJECT_TIME = 1.0
HEAD_TIME = 1.4
WINDOW_TIME = 1.1
SENT = 7.0

HEADS = 9
HEAD_DIM = 48
BIG_SIDE = 14
SMALL_SIDE = 6
BIG_CROPS = 2
SMALL_CROPS = 6
PER_IMAGE = 608
BIG = BIG_SIDE * BIG_SIDE
SMALL = SMALL_SIDE * SMALL_SIDE
GROUPS = 3

EPS = 1e-06
F32 = jnp.float32
BF16 = jnp.bfloat16
LOG2E = 1.4426950408889634
SCALE = HEAD_DIM ** (-0.5)
FAR = -1e30

NN = (((1,), (0,)), ((), ()))
NT = (((1,), (1,)), ((), ()))
TN = (((0,), (0,)), ((), ()))

LANES = 128
TOK = 256
KEYS_BIG = 208
STRIDE = 40
KEYS_SMALL = SMALL_CROPS * STRIDE
WIDE = 384
CHUNK = 256
TILE = (16, LANES)
SMALL_ROWS = 32


def dot(left, right, dims=NN):
    return lax.dot_general(left, right, dims, preferred_element_type=F32)


def round_up(count, unit):
    return (count + unit - 1) // unit * unit


def iota(shape, dim):
    return lax.broadcasted_iota(jnp.int32, shape, dim)


def lane_crop():
    token = iota((1, TOK), 1).astype(F32)
    return jnp.floor((token + 0.5) * (1.0 / STRIDE))


def grid_place(cell, side):
    row = jnp.floor((cell + 0.5) * (1.0 / side))
    return row, cell - side * row


def offsets(big):
    keys = KEYS_BIG if big else STRIDE
    side = BIG_SIDE if big else SMALL_SIDE
    key = iota((keys, TOK), 0).astype(F32)
    query = iota((keys, TOK), 1).astype(F32)
    if not big:
        query = query - STRIDE * lane_crop()
    row_j, col_j = grid_place(key, side)
    row_i, col_i = grid_place(query, side)
    col_off = col_j - col_i
    row_off = row_j - row_i
    return col_off, row_off, col_off * col_off + row_off * row_off, key < side * side


def extra_rows(big):
    feature = iota((16, TOK), 0)
    cell = iota((1, TOK), 1).astype(F32)
    if not big:
        cell = cell - STRIDE * lane_crop()
    query = jnp.where(feature == 0, 1.0, 0.0)
    key = jnp.where((feature == 0) & (cell > (BIG if big else SMALL) - 0.5), FAR, 0.0)
    return query.astype(BF16), key.astype(BF16)


def own_crop(full):
    crop = lane_crop()
    result = full[:STRIDE]
    for c in range(1, SMALL_CROPS):
        result = jnp.where(crop == c, full[c * STRIDE : (c + 1) * STRIDE], result)
    return result


def all_crops(own):
    crop = lane_crop()
    return jnp.concatenate([jnp.where(crop == c, own, 0.0) for c in range(SMALL_CROPS)], axis=0)


def whole(values):
    return values


def norm_columns(values):
    center = values - jnp.mean(values, axis=0, keepdims=True)
    inverse = lax.rsqrt(jnp.mean(center * center, axis=0, keepdims=True) + EPS)
    return center * inverse, inverse


def norm_back(grad_normed, scaled, inverse, gain):
    e = grad_normed * gain
    return inverse * (
        e
        - jnp.mean(e, axis=0, keepdims=True)
        - scaled * jnp.mean(e * scaled, axis=0, keepdims=True)
    )


class Plan:
    def __init__(self, dp, tensor, rows, width, share):
        self.dp, self.tensor = dp, tensor
        self.solo = dp == 1
        self.rows, self.width, self.share = rows, width, share
        self.images = rows // PER_IMAGE
        self.windows = 3 * self.images
        self.lanes = round_up(rows, CHUNK)
        self.padded = round_up(share, LANES)
        self.tiles = self.padded // LANES
        self.mains = self.padded // CHUNK
        self.tails = (self.padded % CHUNK) // LANES * ((tensor + 1) // 2)
        self.roles = []
        self.first_main = []
        for j in range(self.mains):
            if j == self.mains - 1:
                self.first_tail = len(self.roles)
                self.roles += [("tail", m, 0) for m in range(self.tails)]
            self.first_main.append(len(self.roles))
            self.roles += [("main", j, turn) for turn in range(tensor)]
        self.steps = len(self.roles)
        self.hidden = CHUNK * self.steps
        self.tall = width + 16
        self.tile_rows = self.tall // 16
        self.cores = 1 if self.solo else 2
        self.pairs = 1 if self.solo else 2
        self.quads = dp // (self.cores * self.pairs)
        self.direct = tensor * dp // self.cores <= 16
        self.pieces = [[2 * j, 2 * j + 1] for j in range(self.mains)]
        if self.tails:
            self.pieces[-1].append(self.tiles - 1)
        self.piece_blocks = [
            round_up(len(piece) * self.tile_rows, self.pairs * self.quads) for piece in self.pieces
        ]
        self.mlp_blocks = sum(self.piece_blocks)
        self.width_tiles = width // LANES
        self.left_over = width % LANES
        self.full_blocks = self.width_tiles * (width // 16)
        self.fold = round_up(width // 2, 16)
        whole = self.full_blocks + self.fold // 16
        self.att_blocks = round_up(whole, self.cores * self.pairs * self.quads)
        piece = self.att_blocks // (self.cores * self.pairs * self.quads)
        self.att_arrived = self.att_blocks + tensor * piece
        around = tensor * dp // self.cores if self.direct else tensor + self.pairs + self.quads
        self.sem_weights = 2 * tensor * (self.mains + 1)
        self.sem_steps = self.steps + (tensor - 1) * self.tiles
        self.semaphores = (
            self.sem_weights
            + self.sem_steps
            + len(self.pieces) * (2 * (self.pairs + dp // self.cores) + 1)
            + 4 * 2 * (1 + around)
            + 1
            + around
        )


class Timeline:
    def __init__(self):
        self.chains = []

    def add(self, ready, actions):
        self.chains.append([ready, list(actions)])

    def due(self, now):
        calls = []
        for chain in list(self.chains):
            if chain[1] and chain[0] <= now:
                call, delay, hook = chain[1].pop(0)
                chain[0] = now + delay
                calls.append(call)
                if hook:
                    hook(now)
        return calls

    def point(self, now, condition=None):
        calls = self.due(now)
        if not calls:
            return

        def act():
            for call in calls:
                call()

        if condition is None:
            act()
        else:
            pl.when(condition)(act)

    def finish(self, now):
        while any(chain[1] for chain in self.chains):
            self.point(now)
            now += 1.0


class Links:
    def __init__(self, plan, send, recv):
        self.plan, self.send, self.recv = plan, send, recv
        self.next = 0
        self.started = []
        if plan.solo:
            self.d = self.t = self.core = self.pair = self.quad = self.chip = self.place = 0
        else:
            self.d = lax.axis_index("dp")
            self.t = lax.axis_index("tensor")
            self.core = self.d % 2
            self.pair = (self.d // 2) % 2
            self.quad = self.d // 4
            self.chip = self.d // 2
            self.place = self.chip * plan.tensor + self.t

    def take(self, count):
        first = self.next
        self.next += count
        return first

    def group(self, name):
        plan, d, t = self.plan, self.d, self.t
        if name == "core":
            return plan.cores, self.core, lambda k: (d - self.core + k, t)
        if name == "tensor":
            return plan.tensor, t, lambda k: (d, k)
        if name == "pair":
            return plan.pairs, self.pair, lambda k: (d + 2 * (k - self.pair), t)
        if name == "quad":
            return plan.quads, self.quad, lambda k: (d + 4 * (k - self.quad), t)
        if name == "plane":
            return plan.dp // plan.cores, self.chip, lambda k: (2 * k + self.core, t)
        count = plan.tensor
        return (
            plan.dp // plan.cores * count,
            self.place,
            lambda k: (2 * (k // count) + self.core, k % count),
        )

    def greet(self):
        if self.plan.solo:
            return
        semaphore = pltpu.get_barrier_semaphore()
        self.greeted = 0
        direct = ("core", "all")
        for name in direct if self.plan.direct else ("core", "tensor", "pair", "quad"):
            size, me, peer = self.group(name)
            for step in range(1, size):
                pl.semaphore_signal(
                    semaphore,
                    inc=1,
                    device_id=peer(lax.rem(me + step, size)),
                    device_id_type=MESH,
                )
                self.greeted += 1

    def await_greetings(self):
        if not self.plan.solo:
            pl.semaphore_wait(pltpu.get_barrier_semaphore(), self.greeted)

    def copy(self, source, target, number, device):
        return pltpu.make_async_remote_copy(
            src_ref=source,
            dst_ref=target,
            send_sem=self.send.at[number],
            recv_sem=self.recv.at[number],
            device_id=device,
            device_id_type=MESH,
        )

    def put(self, make):
        self.copy(*make()).start()
        self.started.append(make)

    def drain(self):
        for make in self.started:
            self.copy(*make()).wait_send()


DELAYS = {"core": 2.0, "pair": 5.5, "quad": 6.0, "tensor": 4.5, "plane": 8.0, "all": 7.5}


class Reduction:
    def __init__(self, links, part, length, arrived, full, full_start, groups, gathers, shared=None, held=()):
        self.links, self.part, self.arrived, self.full = links, part, arrived, full
        self.full_start = full_start
        self.length = length
        self.used = 0
        self.terms = [(name, links.group(name)[1], stride, False) for name, stride in held]
        self.stages = []

        def several(name):
            return name and links.group(name)[0] > 1

        groups = [name for name in groups if several(name)]
        gathers = [name for name in gathers if several(name)]
        for at, name in enumerate(groups):
            last = at == len(groups) - 1 and not several(shared)
            self.stages.append((name, self.scatter, functools.partial(self.add, last=last)))
        if several(shared):
            self.stages.append((shared, self.share, self.shared))
        for name in gathers:
            self.stages.append((name, self.gather, self.gathered))

    def actions(self, before=None, after=None):
        calls = []
        for at in range(len(self.stages) + 1):
            todo = []
            if at == 0 and before:
                todo.append(before)
            if at:
                name, _, end = self.stages[at - 1]
                todo.append(functools.partial(end, name))
            if at < len(self.stages):
                name, start, _ = self.stages[at]
                todo.append(functools.partial(start, name))
                delay = DELAYS[name]
            else:
                delay = 0.0
                if after:
                    todo.append(after)
            calls.append((functools.partial(self.run, todo), delay, None))
        return calls

    @staticmethod
    def run(todo):
        for call in todo:
            call()

    def part_place(self):
        return sum(me * stride for _, me, stride, cut in self.terms if cut)

    def full_place(self, terms):
        return self.full_start + sum(me * stride for _, me, stride, _ in terms)

    def scatter(self, name):
        size, me, peer = self.links.group(name)
        piece = self.length // size
        self.first = first = self.links.take(size - 1)
        terms, used = tuple(self.terms), self.used

        def make(step):
            to = lax.rem(me + step, size)
            offset = sum(who * stride for _, who, stride, cut in terms if cut) + to * piece
            return (
                self.part.at[pl.ds(offset, piece)],
                self.arrived.at[pl.ds(used + (step - 1) * piece, piece)],
                first + step - 1,
                peer(to),
            )

        for step in range(1, size):
            self.links.put(functools.partial(make, step))

    def add(self, name, last):
        size, me, peer = self.links.group(name)
        piece = self.length // size
        self.terms.append((name, me, piece, True))
        mine = pl.ds(self.part_place(), piece)
        total = self.part[mine].astype(F32)
        for step in range(1, size):
            slot = pl.ds(self.used + (step - 1) * piece, piece)
            ref = self.arrived.at[slot]
            self.links.copy(
                ref, ref, self.first + step - 1, peer(lax.rem(me + step, size))
            ).wait_recv()
            total += self.arrived[slot].astype(F32)
        self.used += (size - 1) * piece
        self.length = piece
        if last:
            self.full[pl.ds(self.full_place(self.terms), piece)] = total.astype(BF16)
        else:
            self.part[mine] = total.astype(BF16)

    def share(self, name):
        size, me, peer = self.links.group(name)
        self.first = first = self.links.take(size - 1)
        length, used = self.length, self.used
        self.arrived[pl.ds(used + me * length, length)] = self.part[pl.ds(self.part_place(), length)]

        def make(step):
            ref = self.arrived.at[pl.ds(used + me * length, length)]
            return ref, ref, first + step - 1, peer(lax.rem(me + step, size))

        for step in range(1, size):
            self.links.put(functools.partial(make, step))

    def shared(self, name):
        size, me, peer = self.links.group(name)
        for step in range(1, size):
            source = lax.rem(me + size - step, size)
            ref = self.arrived.at[pl.ds(self.used + source * self.length, self.length)]
            self.links.copy(ref, ref, self.first + step - 1, peer(source)).wait_recv()
        total = self.arrived[pl.ds(self.used, self.length)].astype(F32)
        for other in range(1, size):
            total += self.arrived[pl.ds(self.used + other * self.length, self.length)].astype(F32)
        self.full[pl.ds(self.full_place(self.terms), self.length)] = total.astype(BF16)

    def gather(self, name):
        size, me, peer = self.links.group(name)
        self.first = first = self.links.take(size - 1)
        terms, length = tuple(self.terms), self.length

        def make(step):
            mine = self.full.at[pl.ds(self.full_place(terms), length)]
            return mine, mine, first + step - 1, peer(lax.rem(me + step, size))

        for step in range(1, size):
            self.links.put(functools.partial(make, step))

    def gathered(self, name):
        size, me, peer = self.links.group(name)
        stride = [term for term in self.terms if term[0] == name][0][2]
        self.terms = [term for term in self.terms if term[0] != name]
        for step in range(1, size):
            source = lax.rem(me + size - step, size)
            offset = self.full_place(self.terms) + source * stride
            ref = self.full.at[pl.ds(offset, self.length)]
            self.links.copy(ref, ref, self.first + step - 1, peer(source)).wait_recv()
        self.length = self.length * size


def block_kernel(
    stop,
    plan,
    x_ref,
    cells_ref,
    cot_ref,
    wq_ref,
    wk_ref,
    wv_ref,
    wp_ref,
    fc1_ref,
    fb1_ref,
    fc2_ref,
    g1_ref,
    b1_ref,
    pb_ref,
    g2_ref,
    b2_ref,
    fb2_ref,
    posw_ref,
    gate_ref,
    out_ref,
    gi_ref,
    mlp_ref,
    att_ref,
    small_ref,
    x_s,
    cot_s,
    w_s,
    w_t,
    share_s,
    fc_s,
    fc_t,
    vec_s,
    hot,
    norm_s,
    ncan,
    qkv,
    att_t,
    pos_b,
    pos_s,
    con_b,
    con_s,
    att_s,
    mid_s,
    n2_s,
    cb_s,
    hid,
    dbef,
    gm_s,
    acc,
    mlp_part,
    mlp_core,
    mlp_tensor,
    mlp_sum,
    mlp_arrived,
    att_part,
    att_arrived,
    mlp_full,
    att_full,
    small_s,
    small_arrived,
    local_sem,
    send_sem,
    recv_sem,
):
    D, rows, lanes = plan.width, plan.rows, plan.lanes
    windows = plan.windows
    links = Links(plan, send_sem, recv_sem)
    t, core = links.t, links.core
    other_core = (links.d + 1 - 2 * core, t)

    def local(source, target, number):
        return pltpu.make_async_copy(source, target, local_sem.at[number])

    loads = [
        local(x_ref, x_s, 0),
        local(fc1_ref, share_s.at[0], 1),
        local(fc2_ref, share_s.at[1], 2),
        local(wq_ref, w_s.at[0], 3),
        local(wk_ref, w_s.at[1], 4),
        local(wv_ref, w_s.at[2], 5),
        local(wp_ref, w_s.at[3], 6),
        local(cot_ref, cot_s, 7),
    ]
    for load in loads:
        load.start()
    links.greet()

    parts = list(range(plan.mains)) + (["tail"] if plan.tails else [])

    def hidden_lanes(owner, holder, part):
        turn = lax.rem(owner - holder - 1 + plan.tensor, plan.tensor)
        if part == "tail":
            start = plan.first_tail * CHUNK + owner * LANES
            return pl.ds(pl.multiple_of(start, LANES), LANES)
        start = (plan.first_main[part] + turn) * CHUNK
        return pl.ds(pl.multiple_of(start, CHUNK), CHUNK)

    first_weight = links.take(2 * plan.tensor * len(parts))
    loads[1].wait()
    loads[2].wait()
    for part in parts:
        to = hidden_lanes(t, t, part)
        low = (plan.mains if part == "tail" else part) * CHUNK
        high = min(plan.share, low + to.size)
        for kind in range(2):
            values = share_s[kind, :, low:high]
            if kind == 0:
                bias = fb1_ref[:, low:high].astype(F32)
            else:
                bias = jnp.zeros((1, high - low), F32)
            bias = jnp.where(iota((16, high - low), 0) == 0, bias, 0.0).astype(BF16)
            values = jnp.concatenate([values, bias], axis=0)
            if to.size > high - low:
                fill = jnp.zeros((plan.tall, to.size - high + low), BF16)
                values = jnp.concatenate([values, fill], axis=1)
            fc_s[kind, :, to] = values

    def send_weights(step, at):
        to = lax.rem(t + step, plan.tensor)
        return (
            fc_s.at[core, :, hidden_lanes(t, t, parts[at])],
            fc_s.at[core, :, hidden_lanes(t, to, parts[at])],
            first_weight + len(parts) * step + at,
            (links.d, to),
        )

    def arrived_weights(step, at, kind):
        source = lax.rem(t + plan.tensor - step, plan.tensor)
        ref = fc_s.at[kind, :, hidden_lanes(source, t, parts[at])]
        return ref, ref, first_weight + len(parts) * step + at, (links.d, source)

    def handed_weights(step, at, kind):
        ref, _, number, _ = arrived_weights(step, at, kind)
        return links.copy(ref, ref, number + plan.tensor * len(parts), other_core)

    weight_copies = [(step, at) for step in range(1, plan.tensor) for at in range(len(parts))]
    links.await_greetings()
    for step, at in weight_copies:
        links.put(functools.partial(send_weights, step, at))

    def pass_weights():
        for step, at in weight_copies:
            links.copy(*arrived_weights(step, at, core)).wait_recv()
            handed_weights(step, at, core).start()

    def wait_weights():
        for step, at in weight_copies:
            handed_weights(step, at, 1 - core).wait_recv()
            handed_weights(step, at, core).wait_send()

    for number, ref in enumerate((g1_ref, b1_ref, pb_ref, g2_ref, b2_ref, fb2_ref)):
        for tile in range(round_up(D, LANES) // LANES):
            low, high = tile * LANES, min(D, tile * LANES + LANES)
            spread = jnp.broadcast_to(ref[:, low:high], (LANES, high - low))
            vec_s[number, low:high, :] = jnp.transpose(spread)
    GAIN1, BIAS1, PBIAS, GAIN2, BIAS2, FBIAS2 = range(6)

    def position(h, carry):
        w0, w1, w2 = posw_ref[0, h], posw_ref[1, h], posw_ref[2, h]
        sig = 1.0 / (1.0 + jnp.exp(-jnp.full((1, TOK), gate_ref[0, h], F32)))
        for big, store in ((True, pos_b), (False, pos_s)):
            col_off, row_off, dist, live = offsets(big)
            logits = jnp.where(live, w0 * col_off + w1 * row_off + w2 * dist, FAR)
            top = jnp.max(logits, axis=0, keepdims=True)
            e = jnp.exp(logits - top)
            store[h] = e * (sig / jnp.sum(e, axis=0, keepdims=True))
        return carry

    lax.fori_loop(0, HEADS, position, 0)
    acc[...] = jnp.zeros(acc.shape, F32)
    small_s[...] = jnp.zeros(small_s.shape, F32)
    for number in range(3, 7):
        loads[number].wait()
    for number in range(4):
        w_t[number] = jnp.transpose(w_s[number])
    if stop == 1:
        return

    loads[0].wait()

    def for_blocks(body):
        def one(b, carry):
            body(pl.ds(pl.multiple_of(b * LANES, LANES), LANES), LANES)
            return carry

        lax.fori_loop(0, rows // LANES, one, 0)
        if rows % LANES:
            body(pl.ds(rows // LANES * LANES, rows % LANES), rows % LANES)

    def norm_one(at, count):
        scaled, _ = norm_columns(x_s[:, at].astype(F32))
        normed = scaled * vec_s[GAIN1, :, :count] + vec_s[BIAS1, :, :count]
        norm_s[:, at] = normed.astype(BF16)

    for_blocks(norm_one)
    if rows < lanes:
        norm_s[:, rows:] = jnp.zeros((D, lanes - rows), BF16)

    def window_start(w):
        first = (w // 3) * PER_IMAGE + (w % 3) * BIG
        return first, pl.multiple_of(first // LANES * LANES, LANES)

    def project(w, carry):
        first, start = window_start(w)
        at = iota((1, WIDE), 1) + start
        inside = at - first
        crop = jnp.floor((inside.astype(F32) + 0.5) * (1.0 / SMALL)).astype(jnp.int32)
        is_small = w % 3 == 2
        count = jnp.where(is_small, SMALL_CROPS * SMALL, BIG)
        token = cells_ref[:, pl.ds(start, WIDE)] + jnp.where(is_small, crop * STRIDE, 0)
        token = jnp.where((inside >= 0) & (inside < count), token, -1)
        one_hot = jnp.where(iota((TOK, WIDE), 0) == token, 1.0, 0.0).astype(BF16)
        hot[w] = one_hot
        canonical = dot(norm_s[:, pl.ds(start, WIDE)], one_hot, NT).astype(BF16)
        ncan[w] = canonical
        for part in range(3):
            qkv[w, part * D : part * D + D, :] = dot(w_t[part], canonical).astype(BF16)
        return carry

    lax.fori_loop(0, windows, project, 0)
    if stop == 2:
        return

    extra_b = extra_rows(True)
    extra_s = extra_rows(False)

    def head_rows(part, h):
        return pl.ds(pl.multiple_of(part * D + h * HEAD_DIM, 16), HEAD_DIM)

    def window_kind(w):
        image, slot = w // 3, w % 3
        if slot < 2:
            return KEYS_BIG, pos_b, con_b, image * BIG_CROPS + slot, extra_b, whole, whole
        return KEYS_SMALL, pos_s, con_s, image, extra_s, own_crop, all_crops

    window_groups = [range(windows)]

    def forward_head(h, carry):
        sig = 1.0 / (1.0 + jnp.exp(-jnp.full((1, TOK), gate_ref[0, h], F32)))
        for group in window_groups:
            kinds = [window_kind(w) for w in group]
            scores = []
            for w, kind in zip(group, kinds):
                extra_q, extra_k = kind[4]
                q = jnp.concatenate([qkv[w, head_rows(0, h), :], extra_q], axis=0)
                k = jnp.concatenate([qkv[w, head_rows(1, h), :], extra_k], axis=0)
                scores.append(kind[5](dot(k[:, : kind[0]], q, TN)))
            tops = [jnp.max(s, axis=0, keepdims=True) for s in scores]
            exps = [jnp.exp2((s - top) * (SCALE * LOG2E)) for s, top in zip(scores, tops)]
            totals = [1.0 / jnp.sum(e, axis=0, keepdims=True) for e in exps]
            contents = [e * total for e, total in zip(exps, totals)]
            for kind, content in zip(kinds, contents):
                kind[2][h, kind[3]] = content.astype(BF16)
            mixtures = [
                kind[6]((1.0 - sig) * content + kind[1][h]).astype(BF16)
                for kind, content in zip(kinds, contents)
            ]
            for w, kind, mixture in zip(group, kinds, mixtures):
                v = qkv[w, head_rows(2, h), : kind[0]]
                att_t[w, head_rows(0, h), :] = dot(v, mixture).astype(BF16)
        return carry

    lax.fori_loop(0, HEADS, forward_head, 0)
    if not plan.solo:
        pass_weights()
    if stop == 3:
        return

    def scatter_back(target, w, values):
        _, start = window_start(w)
        at = pl.ds(start, WIDE)
        target[:, at] += sum(dot(value, hot[w]) for value in values)

    att_s[...] = jnp.zeros(att_s.shape, F32)

    def attended_back(w, carry):
        scatter_back(att_s, w, [att_t[w]])
        return carry

    lax.fori_loop(0, windows, attended_back, 0)

    def turn_weights(kind):
        def turn(b, carry):
            at = pl.ds(pl.multiple_of(b * LANES, LANES), LANES)
            fc_t[kind, at, :] = jnp.transpose(fc_s[kind, :, at])
            return carry

        lax.fori_loop(0, plan.hidden // LANES, turn, 0)

    turn_weights(core)

    loads[7].wait()
    def norm_two(at, count):
        values = dot(w_t[3], att_s[:, at].astype(BF16))
        middle = x_s[:, at].astype(F32) + values + vec_s[PBIAS, :, :count]
        mid_s[:, at] = middle
        scaled, _ = norm_columns(middle)
        n2_s[:D, at] = (scaled * vec_s[GAIN2, :, :count] + vec_s[BIAS2, :, :count]).astype(BF16)
        rounded = cot_s[:, at].astype(BF16)
        cb_s[:D, at] = rounded
        acc[3, :D, :count] += rounded.astype(F32)
        att_s[:, at] = middle + vec_s[FBIAS2, :, :count]

    for_blocks(norm_two)
    gm_s[...] = jnp.zeros(gm_s.shape, F32)
    if not plan.solo:
        wait_weights()
    turn_weights(1 - core)
    n2_s[D:, :] = jnp.where(iota((16, rows), 0) == 0, 1.0, 0.0).astype(BF16)
    cb_s[D:, :] = jnp.zeros((16, rows), BF16)
    if stop == 4:
        return

    spans = [(low, min(CHUNK, rows - low)) for low in range(0, rows, CHUNK)]

    def activate(s, slot):
        cs = pl.ds(pl.multiple_of(s * CHUNK, CHUNK), CHUNK)
        for low, count in spans:
            at = pl.ds(low, count)
            before = dot(fc_t[0, cs, :], n2_s[:, at])
            dh = dot(fc_t[1, cs, :], cb_s[:, at])
            cdf = 0.5 * (1.0 + lax.erf(before * 0.7071067811865476))
            density = jnp.exp(-0.5 * before * before) * 0.3989422804014327
            hid[slot, :, at] = (before * cdf).astype(BF16)
            dbef[slot, :, at] = (dh * (cdf + before * density)).astype(BF16)

    def consume(s, slot):
        cs = pl.ds(pl.multiple_of(s * CHUNK, CHUNK), CHUNK)
        for kind, left, right in ((0, n2_s, dbef), (1, cb_s, hid)):
            grad = dot(left[...], right[slot], NT).astype(BF16)
            for half in range(2):
                blocks = grad[:, half * LANES : half * LANES + LANES]
                mlp_part[kind, s, half] = blocks.reshape((plan.tile_rows,) + TILE)
        for low, count in spans:
            at = pl.ds(low, count)
            att_s[:, at] += dot(fc_s[1, :D, cs], hid[slot, :, at])
            gm_s[:, at] += dot(fc_s[0, :D, cs], dbef[slot, :, at])

    first_core = links.take(plan.steps)
    first_tensor = links.take((plan.tensor - 1) * plan.tiles)
    timeline = Timeline()

    def core_copy(s):
        return links.copy(mlp_part.at[1 - core, s], mlp_core.at[s], first_core + s, other_core)

    def tensor_copy(s, half, tile, turn):
        to = lax.rem(t + 1 + turn, plan.tensor)
        return (
            mlp_part.at[core, s, half],
            mlp_tensor.at[turn, tile],
            first_tensor + turn * plan.tiles + tile,
            (links.d, to),
        )

    def step_sum(s):
        links.copy(mlp_core.at[s], mlp_core.at[s], first_core + s, other_core).wait_recv()
        total = mlp_part[core, s].astype(F32) + mlp_core[s].astype(F32)
        mlp_part[core, s] = total.astype(BF16)
        kind, j, turn = plan.roles[s]
        if kind == "main" and turn < plan.tensor - 1:
            for half in range(2):
                links.copy(*tensor_copy(s, half, 2 * j + half, turn)).start()
        if kind == "tail" and plan.tensor > 1:
            for half in range(2):
                turn = lax.rem(2 * j + half - t - 1 + plan.tensor, plan.tensor)

                def send(turn=turn, half=half):
                    links.copy(*tensor_copy(s, half, plan.tiles - 1, turn)).start()

                pl.when(turn < plan.tensor - 1)(send)

    def collect(number):
        start = sum(plan.piece_blocks[:number])
        for at, tile in enumerate(plan.pieces[number]):
            for turn in range(plan.tensor - 1):
                ref = mlp_tensor.at[turn, tile]
                source = lax.rem(t - turn - 1 + plan.tensor, plan.tensor)
                links.copy(
                    ref, ref, first_tensor + turn * plan.tiles + tile, (links.d, source)
                ).wait_recv()
            if tile < 2 * plan.mains:
                step, half = plan.first_main[tile // 2] + plan.tensor - 1, tile % 2
            else:
                step, half = plan.first_tail + t // 2, t % 2
            total = mlp_part[core, step, half].astype(F32)
            for turn in range(plan.tensor - 1):
                total += mlp_tensor[turn, tile].astype(F32)
            low = start + at * plan.tile_rows
            mlp_sum[low : low + plan.tile_rows] = total.astype(BF16)
        low = start + len(plan.pieces[number]) * plan.tile_rows
        high = start + plan.piece_blocks[number]
        if low < high:
            mlp_sum[low:high] = jnp.zeros((high - low,) + TILE, BF16)

    mlp_sums = []
    for number, size in enumerate(plan.piece_blocks):
        start = sum(plan.piece_blocks[:number])
        mlp_sums.append(
            Reduction(
                links,
                mlp_sum.at[pl.ds(start, size)],
                size,
                mlp_arrived.at[pl.ds(start, size)],
                mlp_full,
                start,
                ("pair", "quad"),
                ("quad", "pair", "core"),
                held=(("core", plan.mlp_blocks),),
            )
        )
    summed = {}
    begun = set()

    def needed(number):
        tail = any(tile >= 2 * plan.mains for tile in plan.pieces[number])
        return [
            s
            for s, (kind, j, turn) in enumerate(plan.roles)
            if (kind == "tail" and tail) or (kind == "main" and 2 * j in plan.pieces[number])
        ]

    def step_done(s, now):
        summed[s] = now
        for number in range(len(plan.pieces)):
            steps = needed(number)
            if number in begun or any(step not in summed for step in steps):
                continue
            begun.add(number)
            sent = [
                summed[step]
                for step in steps
                if plan.roles[step][0] == "tail" or plan.roles[step][2] < plan.tensor - 1
            ]
            timeline.add(
                max([now] + [at + SENT for at in sent]),
                mlp_sums[number].actions(before=functools.partial(collect, number)),
            )

    def begin_step(s, now):
        timeline.add(
            now,
            [
                (lambda: core_copy(s).start(), DELAYS["core"], None),
                (lambda: step_sum(s), 0.0, functools.partial(step_done, s)),
            ],
        )

    activate(0, 0)

    def mlp_step(s, carry):
        consume(s - 1, (s - 1) % 2)
        activate(s, s % 2)
        if not plan.solo:
            for k in range(1, plan.steps):
                begin_step(k - 1, MLP_STEP * k + 1)
                timeline.point(MLP_STEP * k + 1, s == k)
        return carry

    lax.fori_loop(1, plan.steps, mlp_step, 0)
    last = plan.steps - 1
    consume(last, last % 2)
    now = MLP_STEP * plan.steps + 1
    if not plan.solo:
        begin_step(last, now)
        timeline.point(now)
    if stop == 5:
        return

    def norm_two_back(at, count):
        n2_s[:D, at] = att_s[:, at].astype(BF16)
        grad = gm_s[:, at]
        scaled, inverse = norm_columns(mid_s[:, at])
        back = norm_back(grad, scaled, inverse, vec_s[GAIN2, :, :count])
        grad_middle = cot_s[:, at] + back
        cot_s[:, at] = grad_middle
        branch = grad_middle.astype(BF16)
        norm_s[:, at] = branch
        acc[0, :D, :count] += grad * scaled
        acc[1, :D, :count] += grad
        acc[2, :D, :count] += branch.astype(F32)

    for_blocks(norm_two_back)
    store_out = local(n2_s.at[pl.ds(0, D)], out_ref, 8)
    store_out.start()

    now += NORM_TIME
    timeline.point(now)

    wide = pl.ds(round_up(D, LANES), D)
    gm_s[:, wide] = jnp.zeros((D, D), F32)

    def project_back(w, carry):
        _, start = window_start(w)
        canonical = dot(norm_s[:, pl.ds(start, WIDE)], hot[w], NT).astype(BF16)
        gm_s[:, wide] += dot(att_t[w], canonical, NT)
        att_t[w] = dot(w_s[3], canonical).astype(BF16)
        for k in range(windows):
            timeline.point(now + PROJECT_TIME * (k + 1), w == k)
        return carry

    lax.fori_loop(0, windows, project_back, 0)
    now += PROJECT_TIME * windows
    if stop == 6:
        return

    def att_start(number, total):
        gm_s[:, :D] = total
        for tile in range(plan.width_tiles):
            blocks = gm_s[:, tile * LANES : tile * LANES + LANES].astype(BF16)
            at = tile * (D // 16)
            att_part[number, at : at + D // 16] = blocks.reshape((D // 16,) + TILE)
        edge = gm_s[:, plan.width_tiles * LANES : plan.width_tiles * LANES + LANES]
        low = D - plan.fold
        lane = iota((low, LANES), 1)
        folded = jnp.where(
            lane < plan.left_over, edge[:low], pltpu.roll(edge[plan.fold :], plan.left_over, 1)
        )
        at = plan.full_blocks
        att_part[number, at : at + low // 16] = folded.astype(BF16).reshape((low // 16,) + TILE)
        if low < plan.fold:
            rows_left = edge[low : plan.fold].astype(BF16)
            att_part[number, at + low // 16 : at + plan.fold // 16] = rows_left.reshape(
                ((plan.fold - low) // 16,) + TILE
            )
        spare = plan.att_blocks - at - plan.fold // 16
        if spare:
            att_part[number, plan.att_blocks - spare :] = jnp.zeros((spare,) + TILE, BF16)

    direct = plan.direct

    att_sums = [
        Reduction(
            links,
            att_part.at[number],
            plan.att_blocks,
            att_arrived.at[number],
            att_full.at[number],
            0,
            ("core", "all") if direct else ("core", "pair", "quad"),
            ("all", "core") if direct else ("quad", "pair", "core"),
            None if direct else "tensor",
        )
        for number in range(GROUPS + 1)
    ]

    def begin_att(number, now):
        timeline.add(now, att_sums[number].actions())

    att_start(0, gm_s[:, wide])
    if not plan.solo:
        begin_att(0, now)
        timeline.point(now)

    def weight_grad(g):
        def joined(w):
            parts = [
                qkv[w, pl.ds(pl.multiple_of(part * D + g * (D // GROUPS), 16), D // GROUPS), :]
                for part in range(3)
            ]
            return jnp.concatenate(parts, axis=0)

        total = dot(ncan[0], joined(0), NT)
        for w in range(1, windows):
            total += dot(ncan[w], joined(w), NT)
        att_start(1 + g, total)

    window_groups = [range(windows)]

    def backward_head(h, carry):
        sig = 1.0 / (1.0 + jnp.exp(-jnp.full((1, TOK), gate_ref[0, h], F32)))
        keep = 1.0 - sig
        factor = keep * SCALE
        sums = [0.0, 0.0]
        gate_row = jnp.zeros((1, TOK), F32)
        for group in window_groups:
            kinds = [window_kind(w) for w in group]
            queries = [qkv[w, head_rows(0, h), :] for w in group]
            keys = [qkv[w, head_rows(1, h), : kind[0]] for w, kind in zip(group, kinds)]
            vals = [qkv[w, head_rows(2, h), : kind[0]] for w, kind in zip(group, kinds)]
            grads = [att_t[w, head_rows(0, h), :] for w in group]
            contents = [kind[2][h, kind[3]].astype(F32) for kind in kinds]
            grad_mixes = [
                kind[5](dot(v, da, TN)) for kind, v, da in zip(kinds, vals, grads)
            ]
            mixtures = [
                kind[6](keep * content + kind[1][h]).astype(BF16)
                for kind, content in zip(kinds, contents)
            ]
            grad_vals = [dot(da, mixture, NT) for da, mixture in zip(grads, mixtures)]
            rows_sum = [
                jnp.sum(content * grad_mix, axis=0, keepdims=True)
                for content, grad_mix in zip(contents, grad_mixes)
            ]
            grad_scores = [
                kind[6](content * (grad_mix - row)).astype(BF16)
                for kind, content, grad_mix, row in zip(kinds, contents, grad_mixes, rows_sum)
            ]
            for w, grad_mix, row in zip(group, grad_mixes, rows_sum):
                sums[w % 3 // 2] += grad_mix
                gate_row -= row
            grad_queries = [dot(k, grad_s) for k, grad_s in zip(keys, grad_scores)]
            grad_keys = [dot(q, grad_s, NT) for q, grad_s in zip(queries, grad_scores)]
            for w, kind, dq, dk, dv in zip(group, kinds, grad_queries, grad_keys, grad_vals):
                qkv[w, head_rows(0, h), :] = (dq * factor).astype(BF16)
                qkv[w, head_rows(1, h), : kind[0]] = (dk * factor[:, : kind[0]]).astype(BF16)
                qkv[w, head_rows(2, h), : kind[0]] = dv.astype(BF16)
        results = [jnp.zeros((1, TOK), F32)] * 3
        for big, pos, grad_mix in ((True, pos_b, sums[0]), (False, pos_s, sums[1])):
            col_off, row_off, dist, _ = offsets(big)
            row = jnp.sum(pos[h] * grad_mix, axis=0, keepdims=True) / sig
            grad_l = pos[h] * (grad_mix - row)
            gate_row += row
            results = [
                old + jnp.sum(grad_l * off, axis=0, keepdims=True)
                for old, off in zip(results, (col_off, row_off, dist))
            ]
        results = jnp.concatenate(results + [gate_row * sig * keep], axis=0)
        column = jnp.sum(results, axis=1, keepdims=True)
        lane = iota((4, LANES), 1)
        small_s[24:28, :] += jnp.where(lane == h, column, 0.0)
        pl.when(h % (HEADS // GROUPS) == HEADS // GROUPS - 1)(
            lambda: weight_grad(h // (HEADS // GROUPS))
        )
        if not plan.solo:
            for k in range(HEADS):
                time = now + HEAD_TIME * (k + 1)
                if k % (HEADS // GROUPS) == HEADS // GROUPS - 1:
                    begin_att(1 + k // (HEADS // GROUPS), time)
                timeline.point(time, h == k)
        return carry

    lax.fori_loop(0, HEADS, backward_head, 0)
    now += HEAD_TIME * HEADS
    if stop == 7:
        return

    att_s[...] = jnp.zeros(att_s.shape, F32)

    def norm_grad(w, carry):
        grad = dot(w_s[0], qkv[w, :D, :])
        grad += dot(w_s[1], qkv[w, D : 2 * D, :])
        grad += dot(w_s[2], qkv[w, 2 * D :, :])
        high = grad.astype(BF16)
        low = (grad - high.astype(F32)).astype(BF16)
        scatter_back(att_s, w, [high, low])
        for k in range(windows):
            timeline.point(now + WINDOW_TIME * (k + 1), w == k)
        return carry

    lax.fori_loop(0, windows, norm_grad, 0)
    now += WINDOW_TIME * windows

    def norm_one_back(at, count):
        scaled, inverse = norm_columns(x_s[:, at].astype(F32))
        grad = att_s[:, at]
        cot_s[:, at] += norm_back(grad, scaled, inverse, vec_s[GAIN1, :, :count])
        acc[4, :D, :count] += grad * scaled
        acc[5, :D, :count] += grad

    for_blocks(norm_one_back)
    store_gi = local(cot_s, gi_ref, 9)
    store_gi.start()
    for number in range(6):
        for tile in range(round_up(D, LANES) // LANES):
            turned = jnp.transpose(acc[number, tile * LANES : tile * LANES + LANES, :])
            at = number * 4 + tile
            small_s[at : at + 1, :] = jnp.sum(turned, axis=0, keepdims=True)

    now += NORM_TIME
    small_places = {}

    def small_begin(name):
        size, me, peer = links.group(name)
        first = links.take(size - 1)
        used = sum(size for size, _ in small_places.values())
        small_places[name] = size, first
        small_arrived[used + me] = small_s[...]

        def make(step):
            slot = small_arrived.at[used + me]
            return slot, slot, first + step - 1, peer(lax.rem(me + step, size))

        for step in range(1, size):
            links.put(functools.partial(make, step))

    def small_end(name):
        size, me, peer = links.group(name)
        _, first = small_places[name]
        used = sum(size for size, _ in small_places.values()) - size
        for step in range(1, size):
            source = lax.rem(me + size - step, size)
            ref = small_arrived.at[used + source]
            links.copy(ref, ref, first + step - 1, peer(source)).wait_recv()
        total = small_arrived[used]
        for other in range(1, size):
            total += small_arrived[used + other]
        small_s[...] = total

    names = ("core", "all") if direct else ("core", "tensor", "pair", "quad")
    names = [name for name in names if links.group(name)[0] > 1]
    if names:
        actions = [(functools.partial(small_begin, names[0]), DELAYS[names[0]], None)]
        for before, name in zip(names, names[1:]):

            def turn(before=before, name=name):
                small_end(before)
                small_begin(name)

            actions.append((turn, DELAYS[name], None))
        actions.append((functools.partial(small_end, names[-1]), 0.0, None))
        timeline.add(now, actions)
    timeline.finish(now)
    small_ref[...] = small_s[...]
    stores = [local(mlp_full, mlp_ref, 10), local(att_full, att_ref, 11)]
    for store in stores:
        store.start()
    store_out.wait()
    store_gi.wait()
    if not plan.solo:
        for s in range(plan.steps):
            core_copy(s).wait_send()
        for s, (kind, j, turn) in enumerate(plan.roles):
            if kind == "main" and turn < plan.tensor - 1:
                for half in range(2):
                    links.copy(*tensor_copy(s, half, 2 * j + half, turn)).wait_send()
        if plan.tails:
            for turn in range(plan.tensor - 1):
                owner = lax.rem(t + 1 + turn, plan.tensor)
                links.copy(
                    *tensor_copy(plan.first_tail + owner // 2, owner % 2, plan.tiles - 1, turn)
                ).wait_send()
    links.drain()
    for store in stores:
        store.wait()


def finish_kernel(
    plan,
    mlp_ref,
    att_ref,
    small_ref,
    dq_ref,
    dk_ref,
    dv_ref,
    dproj_ref,
    dfc1_ref,
    dfb1_ref,
    dfc2_ref,
    pos_ref,
    gate_ref,
    *vector_refs
):
    D = plan.width
    for kind, target in enumerate((dfc1_ref, dfc2_ref)):
        for tile in range(plan.tiles):
            at = kind * plan.mlp_blocks + tile * plan.tile_rows
            values = mlp_ref[at : at + plan.tile_rows].reshape(plan.tall, LANES).astype(F32)
            low, high = tile * LANES, min(plan.share, tile * LANES + LANES)
            target[:, low:high] = values[:D, : high - low]
            if kind == 0:
                dfb1_ref[:, low:high] = values[D : D + 1, : high - low]
    low = D - plan.fold
    part = D // GROUPS
    for number in range(GROUPS + 1):
        tiles = [
            att_ref[number, tile * (D // 16) : (tile + 1) * (D // 16)]
            .reshape(D, LANES)
            .astype(F32)
            for tile in range(plan.width_tiles)
        ]
        at = plan.full_blocks
        folded = att_ref[number, at : at + plan.fold // 16].reshape(plan.fold, LANES).astype(F32)
        lower = pltpu.roll(folded, LANES - plan.left_over, 1)[:low]
        edge = jnp.concatenate([folded, lower], axis=0)[:, : plan.left_over]
        total = jnp.concatenate(tiles + [edge], axis=1)
        if number == 0:
            dproj_ref[...] = total
        else:
            for place, target in enumerate((dq_ref, dk_ref, dv_ref)):
                g = number - 1
                target[:, g * part : g * part + part] = total[:, place * part : place * part + part]
    for number, target in enumerate(vector_refs):
        for tile in range(round_up(D, LANES) // LANES):
            low, high = tile * LANES, min(D, tile * LANES + LANES)
            row = number * 4 + tile
            target[:, low:high] = small_ref[row : row + 1, : high - low]
    pos_ref[...] = small_ref[24:27, :HEADS]
    gate_ref[...] = small_ref[27:28, :HEADS]


def local(
    stop,
    dp,
    tensor,
    inputs,
    patch_cells,
    ln1_gain,
    ln1_bias,
    w_query,
    w_key,
    w_value,
    w_proj,
    proj_bias,
    pos_weight,
    gate_param,
    ln2_gain,
    ln2_bias,
    fc1_weight,
    fc1_bias,
    fc2_weight,
    fc2_bias,
    cotangent,
):
    rows, D = inputs.shape
    share = fc1_weight.shape[1]
    plan = Plan(dp, tensor, rows, D, share)
    windows, lanes, steps = plan.windows, plan.lanes, plan.steps

    def vector(values):
        return values.reshape(1, -1)

    vmem = pl.BlockSpec(memory_space=pltpu.VMEM)
    smem = pl.BlockSpec(memory_space=pltpu.SMEM)
    anywhere = pl.BlockSpec(memory_space=pl.ANY)
    wide = round_up(D, LANES)
    cells = jnp.pad(patch_cells, (0, lanes - rows))
    params = {} if plan.solo else {"collective_id": 0, "has_side_effects": True}
    slots = plan.cores + plan.tensor + plan.pairs + plan.quads
    if plan.direct:
        slots = plan.cores + tensor * dp // plan.cores
    out, gi, mlp, att, small = pl.pallas_call(
        functools.partial(block_kernel, stop, plan),
        out_shape=(
            jax.ShapeDtypeStruct((D, rows), BF16),
            jax.ShapeDtypeStruct((D, rows), F32),
            jax.ShapeDtypeStruct((2 * plan.mlp_blocks,) + TILE, BF16),
            jax.ShapeDtypeStruct((GROUPS + 1, plan.att_blocks) + TILE, BF16),
            jax.ShapeDtypeStruct((SMALL_ROWS, LANES), F32),
        ),
        in_specs=[anywhere, vmem] + [anywhere] * 6 + [vmem] + [anywhere] + [vmem] * 6 + [smem] * 2,
        out_specs=(anywhere, anywhere, anywhere, anywhere, vmem),
        scratch_shapes=[
            pltpu.VMEM((D, rows), BF16),
            pltpu.VMEM((D, rows), F32),
            pltpu.VMEM((4, D, D), BF16),
            pltpu.VMEM((4, D, D), BF16),
            pltpu.VMEM((2, D, share), BF16),
            pltpu.VMEM((2, plan.tall, plan.hidden), BF16),
            pltpu.VMEM((2, plan.hidden, plan.tall), BF16),
            pltpu.VMEM((6, D, LANES), F32),
            pltpu.VMEM((windows, TOK, WIDE), BF16),
            pltpu.VMEM((D, lanes), BF16),
            pltpu.VMEM((windows, D, TOK), BF16),
            pltpu.VMEM((windows, 3 * D, TOK), BF16),
            pltpu.VMEM((windows, D, TOK), BF16),
            pltpu.VMEM((HEADS, KEYS_BIG, TOK), F32),
            pltpu.VMEM((HEADS, STRIDE, TOK), F32),
            pltpu.VMEM((HEADS, BIG_CROPS * plan.images, KEYS_BIG, TOK), BF16),
            pltpu.VMEM((HEADS, plan.images, STRIDE, TOK), BF16),
            pltpu.VMEM((D, lanes), F32),
            pltpu.VMEM((D, lanes), F32),
            pltpu.VMEM((plan.tall, rows), BF16),
            pltpu.VMEM((plan.tall, rows), BF16),
            pltpu.VMEM((2, CHUNK, rows), BF16),
            pltpu.VMEM((2, CHUNK, rows), BF16),
            pltpu.VMEM((D, lanes), F32),
            pltpu.VMEM((6, wide, LANES), F32),
            pltpu.VMEM((2, steps, 2, plan.tile_rows) + TILE, BF16),
            pltpu.VMEM((steps, 2, plan.tile_rows) + TILE, BF16),
            pltpu.VMEM((max(1, tensor - 1), plan.tiles, plan.tile_rows) + TILE, BF16),
            pltpu.VMEM((plan.mlp_blocks,) + TILE, BF16),
            pltpu.VMEM((plan.mlp_blocks,) + TILE, BF16),
            pltpu.VMEM((GROUPS + 1, plan.att_blocks) + TILE, BF16),
            pltpu.VMEM((GROUPS + 1, plan.att_arrived) + TILE, BF16),
            pltpu.VMEM((2 * plan.mlp_blocks,) + TILE, BF16),
            pltpu.VMEM((GROUPS + 1, plan.att_blocks) + TILE, BF16),
            pltpu.VMEM((SMALL_ROWS, LANES), F32),
            pltpu.VMEM((slots, SMALL_ROWS, LANES), F32),
            pltpu.SemaphoreType.DMA((12,)),
            pltpu.SemaphoreType.DMA((plan.semaphores,)),
            pltpu.SemaphoreType.DMA((plan.semaphores,)),
        ],
        compiler_params=pltpu.CompilerParams(vmem_limit_bytes=63 * 1024 * 1024, **params),
    )(
        inputs.T,
        vector(cells),
        cotangent.T,
        w_query,
        w_key,
        w_value,
        w_proj,
        fc1_weight,
        vector(fc1_bias),
        fc2_weight.T,
        vector(ln1_gain),
        vector(ln1_bias),
        vector(proj_bias),
        vector(ln2_gain),
        vector(ln2_bias),
        vector(fc2_bias),
        pos_weight,
        vector(gate_param),
    )
    square = jax.ShapeDtypeStruct((D, D), F32)
    results = pl.pallas_call(
        functools.partial(finish_kernel, plan),
        out_shape=(square,) * 4
        + (
            jax.ShapeDtypeStruct((D, share), F32),
            jax.ShapeDtypeStruct((1, share), F32),
            jax.ShapeDtypeStruct((D, share), F32),
            jax.ShapeDtypeStruct((3, HEADS), F32),
            jax.ShapeDtypeStruct((1, HEADS), F32),
        )
        + (jax.ShapeDtypeStruct((1, D), F32),) * 6,
        in_specs=[vmem] * 3,
        out_specs=(vmem,) * 15,
        compiler_params=pltpu.CompilerParams(vmem_limit_bytes=32 * 1024 * 1024),
    )(mlp, att, small)
    dq, dk, dv, dproj, dfc1, dfb1, dfc2, pos, gate = results[:9]
    gain2, bias2, pbias, fbias2, gain1, bias1 = (item.reshape(D) for item in results[9:])
    return (
        out.T,
        gi.T,
        gain1,
        bias1,
        dq,
        dk,
        dv,
        dproj,
        pbias,
        pos,
        gate.reshape(HEADS),
        gain2,
        bias2,
        dfc1,
        dfb1.reshape(share),
        dfc2.T,
        fbias2,
    )


def solution(mesh, stop=0):
    both = ("dp", "tensor")
    copied = P()
    in_specs = (
        (P(both, None), P(both))
        + (copied,) * 11
        + (P(None, "tensor"), P("tensor"), P("tensor", None), copied, P(both, None))
    )
    out_specs = (
        (P(both, None), P(both, None))
        + (copied,) * 11
        + (P(None, "tensor"), P("tensor"), P("tensor", None), copied)
    )
    return jax.shard_map(
        functools.partial(local, stop, mesh.shape["dp"], mesh.shape["tensor"]),
        mesh=mesh,
        in_specs=in_specs,
        out_specs=out_specs,
        check_vma=False,
    )
```

```python
import functools

import jax
import jax.numpy as jnp
from jax import lax
from jax.experimental import pallas as pl
from jax.experimental.pallas import tpu as pltpu
from jax.sharding import PartitionSpec as P

MESH = pl.DeviceIdType.MESH

MLP_STEP = 2.1
NORM_TIME = 2.5
PROJECT_TIME = 1.0
HEAD_TIME = 1.4
WINDOW_TIME = 1.1
SENT = 7.0

HEADS = 9
HEAD_DIM = 48
BIG_SIDE = 14
SMALL_SIDE = 6
BIG_CROPS = 2
SMALL_CROPS = 6
PER_IMAGE = 608
BIG = BIG_SIDE * BIG_SIDE
SMALL = SMALL_SIDE * SMALL_SIDE
GROUPS = 3

EPS = 1e-06
F32 = jnp.float32
BF16 = jnp.bfloat16
LOG2E = 1.4426950408889634
SCALE = HEAD_DIM ** (-0.5)
FAR = -1e30

NN = (((1,), (0,)), ((), ()))
NT = (((1,), (1,)), ((), ()))
TN = (((0,), (0,)), ((), ()))

LANES = 128
TOK = 256
KEYS_BIG = 208
STRIDE = 40
KEYS_SMALL = SMALL_CROPS * STRIDE
WIDE = 384
CHUNK = 256
BLOCK = 256
TILE = (16, LANES)
SMALL_ROWS = 32


def dot(left, right, dims=NN):
    return lax.dot_general(left, right, dims, preferred_element_type=F32)


def round_up(count, unit):
    return (count + unit - 1) // unit * unit


def iota(shape, dim):
    return lax.broadcasted_iota(jnp.int32, shape, dim)


def lane_crop():
    token = iota((1, TOK), 1).astype(F32)
    return jnp.floor((token + 0.5) * (1.0 / STRIDE))


def grid_place(cell, side):
    row = jnp.floor((cell + 0.5) * (1.0 / side))
    return row, cell - side * row


def offsets(big):
    keys = KEYS_BIG if big else STRIDE
    side = BIG_SIDE if big else SMALL_SIDE
    key = iota((keys, TOK), 0).astype(F32)
    query = iota((keys, TOK), 1).astype(F32)
    if not big:
        query = query - STRIDE * lane_crop()
    row_j, col_j = grid_place(key, side)
    row_i, col_i = grid_place(query, side)
    col_off = col_j - col_i
    row_off = row_j - row_i
    return col_off, row_off, col_off * col_off + row_off * row_off, key < side * side


def extra_rows(big):
    feature = iota((16, TOK), 0)
    cell = iota((1, TOK), 1).astype(F32)
    if not big:
        cell = cell - STRIDE * lane_crop()
    query = jnp.where(feature == 0, 1.0, 0.0)
    key = jnp.where((feature == 0) & (cell > (BIG if big else SMALL) - 0.5), FAR, 0.0)
    return query.astype(BF16), key.astype(BF16)


def own_crop(full):
    crop = lane_crop()
    result = full[:STRIDE]
    for c in range(1, SMALL_CROPS):
        result = jnp.where(crop == c, full[c * STRIDE : (c + 1) * STRIDE], result)
    return result


def all_crops(own):
    crop = lane_crop()
    return jnp.concatenate([jnp.where(crop == c, own, 0.0) for c in range(SMALL_CROPS)], axis=0)


def whole(values):
    return values


def gelu_parts(before):
    cdf = 0.5 * (1.0 + lax.erf(before * 0.7071067811865476))
    density = jnp.exp(-0.5 * before * before) * 0.3989422804014327
    return before * cdf, cdf + before * density


def norm_columns(values):
    center = values - jnp.mean(values, axis=0, keepdims=True)
    inverse = lax.rsqrt(jnp.mean(center * center, axis=0, keepdims=True) + EPS)
    return center * inverse, inverse


def norm_back(grad_normed, scaled, inverse, gain):
    e = grad_normed * gain
    return inverse * (
        e
        - jnp.mean(e, axis=0, keepdims=True)
        - scaled * jnp.mean(e * scaled, axis=0, keepdims=True)
    )


class Plan:
    def __init__(self, dp, tensor, rows, width, share):
        self.dp, self.tensor = dp, tensor
        self.solo = dp == 1
        self.rows, self.width, self.share = rows, width, share
        self.images = rows // PER_IMAGE
        self.windows = 3 * self.images
        self.lanes = round_up(rows, CHUNK)
        self.padded = round_up(share, LANES)
        self.tiles = self.padded // LANES
        self.mains = self.padded // CHUNK
        self.tails = (self.padded % CHUNK) // LANES * ((tensor + 1) // 2)
        self.own_first = self.mains - 1
        self.roles = [("main", j, tensor - 1) for j in range(self.own_first)]
        self.own_step = list(range(self.own_first))
        self.other_step = []
        for j in range(self.mains):
            if j == self.mains - 1:
                self.first_tail = len(self.roles)
                self.roles += [("tail", m, 0) for m in range(self.tails)]
            self.other_step.append(len(self.roles))
            self.roles += [("main", j, turn) for turn in range(tensor - 1)]
        self.own_step.append(len(self.roles))
        self.roles.append(("main", self.mains - 1, tensor - 1))
        self.steps = len(self.roles)
        self.hidden = CHUNK * self.steps
        self.tall = width + 16
        self.tile_rows = self.tall // 16
        self.cores = 1 if self.solo else 2
        self.pairs = 1 if self.solo else 2
        self.quads = dp // (self.cores * self.pairs)
        self.direct = tensor * dp // self.cores <= 16
        self.pieces = [[2 * j, 2 * j + 1] for j in range(self.mains)]
        if self.tails:
            self.pieces[-1].append(self.tiles - 1)
        self.pair_rows = self.tile_rows // self.pairs
        self.piece_blocks = [
            self.pairs * round_up(len(piece) * self.pair_rows, self.quads) for piece in self.pieces
        ]
        self.mlp_blocks = sum(self.piece_blocks)
        self.width_tiles = width // LANES
        self.left_over = width % LANES
        self.full_blocks = self.width_tiles * (width // 16)
        self.fold = round_up(width // 2, 16)
        whole = self.full_blocks + self.fold // 16
        self.att_blocks = round_up(whole, self.cores * self.pairs * self.quads)
        piece = self.att_blocks // (self.cores * self.pairs * self.quads)
        self.att_arrived = self.att_blocks + tensor * piece
        around = tensor * dp // self.cores if self.direct else tensor + self.pairs + self.quads
        self.sem_weights = 2 * tensor * (self.mains + 1)
        self.sem_steps = 2 * self.steps + (tensor - 1) * self.tiles
        self.semaphores = (
            self.sem_weights
            + self.sem_steps
            + len(self.pieces) * (2 * (self.pairs + dp // self.cores) + 1)
            + 4 * 2 * (1 + around)
            + 1
            + around
        )


class Timeline:
    def __init__(self):
        self.chains = []

    def add(self, ready, actions, label=""):
        self.chains.append([ready, list(actions), label, 0])

    def due(self, now):
        calls = []
        for chain in list(self.chains):
            if chain[1] and chain[0] <= now:
                call, delay, hook = chain[1].pop(0)
                chain[0] = now + delay
                calls.append((call, f"{chain[2]}_{chain[3]}"))
                chain[3] += 1
                if hook:
                    hook(now)
        return calls

    def point(self, now, condition=None):
        calls = self.due(now)
        if not calls:
            return

        def act():
            for call, _ in calls:
                call()

        if condition is None:
            act()
        else:
            pl.when(condition)(act)

    def finish(self, now):
        while any(chain[1] for chain in self.chains):
            self.point(now)
            now += 1.0


class Links:
    def __init__(self, plan, send, recv):
        self.plan, self.send, self.recv = plan, send, recv
        self.next = 0
        self.started = []
        if plan.solo:
            self.d = self.t = self.core = self.pair = self.quad = self.chip = self.place = self.crossed = 0
        else:
            self.d = lax.axis_index("dp")
            self.t = lax.axis_index("tensor")
            self.core = self.d % 2
            self.pair = (self.d // 2) % 2
            self.quad = self.d // 4
            self.chip = self.d // 2
            self.place = self.chip * plan.tensor + self.t
            self.crossed = self.pair * plan.tensor + self.t

    def take(self, count):
        first = self.next
        self.next += count
        return first

    def group(self, name):
        plan, d, t = self.plan, self.d, self.t
        if name == "core":
            return plan.cores, self.core, lambda k: (d - self.core + k, t)
        if name == "tensor":
            return plan.tensor, t, lambda k: (d, k)
        if name == "pair":
            return plan.pairs, self.pair, lambda k: (d + 2 * (k - self.pair), t)
        if name == "quad":
            return plan.quads, self.quad, lambda k: (d + 4 * (k - self.quad), t)
        if name == "cross":
            return (
                plan.pairs * plan.tensor,
                self.crossed,
                lambda k: (d + 2 * (k // plan.tensor - self.pair), k % plan.tensor),
            )
        count = plan.tensor
        return (
            plan.dp // plan.cores * count,
            self.place,
            lambda k: (2 * (k // count) + self.core, k % count),
        )

    def greet(self):
        if self.plan.solo:
            return
        semaphore = pltpu.get_barrier_semaphore()
        self.greeted = 0
        direct = ("core", "all")
        for name in direct if self.plan.direct else ("core", "tensor", "pair", "quad"):
            size, me, peer = self.group(name)
            for step in range(1, size):
                pl.semaphore_signal(
                    semaphore,
                    inc=1,
                    device_id=peer(lax.rem(me + step, size)),
                    device_id_type=MESH,
                )
                self.greeted += 1

    def await_greetings(self):
        if not self.plan.solo:
            pl.semaphore_wait(pltpu.get_barrier_semaphore(), self.greeted)

    def copy(self, source, target, number, device):
        return pltpu.make_async_remote_copy(
            src_ref=source,
            dst_ref=target,
            send_sem=self.send.at[number],
            recv_sem=self.recv.at[number],
            device_id=device,
            device_id_type=MESH,
        )

    def put(self, make):
        self.copy(*make()).start()
        self.started.append(make)

    def drain(self):
        for make in self.started:
            self.copy(*make()).wait_send()


DELAYS = {"core": 1.5, "pair": 4.5, "quad": 4.5, "tensor": 4.5, "cross": 5.0, "all": 6.5}


class Reduction:
    def __init__(self, links, part, length, arrived, full, full_start, groups, gathers, shared=None, held=()):
        self.links, self.part, self.arrived, self.full = links, part, arrived, full
        self.full_start = full_start
        self.length = length
        self.used = 0
        self.terms = [(name, links.group(name)[1], stride, False) for name, stride in held]
        self.stages = []

        def several(name):
            return name and links.group(name)[0] > 1

        groups = [name for name in groups if several(name)]
        gathers = [name for name in gathers if several(name)]
        for at, name in enumerate(groups):
            last = at == len(groups) - 1 and not several(shared)
            self.stages.append((name, self.scatter, functools.partial(self.add, last=last)))
        if several(shared):
            self.stages.append((shared, self.share, self.shared))
        for name in gathers:
            self.stages.append((name, self.gather, self.gathered))

    def actions(self, before=None, after=None):
        calls = []
        for at in range(len(self.stages) + 1):
            todo = []
            if at == 0 and before:
                todo.append(before)
            if at:
                name, _, end = self.stages[at - 1]
                todo.append(functools.partial(end, name))
            if at < len(self.stages):
                name, start, _ = self.stages[at]
                todo.append(functools.partial(start, name))
                delay = DELAYS[name]
            else:
                delay = 0.0
                if after:
                    todo.append(after)
            calls.append((functools.partial(self.run, todo), delay, None))
        return calls

    @staticmethod
    def run(todo):
        for call in todo:
            call()

    def part_place(self):
        return sum(me * stride for _, me, stride, cut in self.terms if cut)

    def full_place(self, terms):
        return self.full_start + sum(me * stride for _, me, stride, _ in terms)

    def scatter(self, name):
        size, me, peer = self.links.group(name)
        piece = self.length // size
        self.first = first = self.links.take(size - 1)
        terms, used = tuple(self.terms), self.used

        def make(step):
            to = lax.rem(me + step, size)
            offset = sum(who * stride for _, who, stride, cut in terms if cut) + to * piece
            return (
                self.part.at[pl.ds(offset, piece)],
                self.arrived.at[pl.ds(used + (step - 1) * piece, piece)],
                first + step - 1,
                peer(to),
            )

        for step in range(1, size):
            self.links.put(functools.partial(make, step))

    def add(self, name, last):
        size, me, peer = self.links.group(name)
        piece = self.length // size
        self.terms.append((name, me, piece, True))
        mine = pl.ds(self.part_place(), piece)
        total = self.part[mine].astype(F32)
        for step in range(1, size):
            slot = pl.ds(self.used + (step - 1) * piece, piece)
            ref = self.arrived.at[slot]
            self.links.copy(
                ref, ref, self.first + step - 1, peer(lax.rem(me + step, size))
            ).wait_recv()
            total += self.arrived[slot].astype(F32)
        self.used += (size - 1) * piece
        self.length = piece
        if last:
            self.full[pl.ds(self.full_place(self.terms), piece)] = total.astype(BF16)
        else:
            self.part[mine] = total.astype(BF16)

    def share(self, name):
        size, me, peer = self.links.group(name)
        self.first = first = self.links.take(size - 1)
        length, used = self.length, self.used
        self.arrived[pl.ds(used + me * length, length)] = self.part[pl.ds(self.part_place(), length)]

        def make(step):
            ref = self.arrived.at[pl.ds(used + me * length, length)]
            return ref, ref, first + step - 1, peer(lax.rem(me + step, size))

        for step in range(1, size):
            self.links.put(functools.partial(make, step))

    def shared(self, name):
        size, me, peer = self.links.group(name)
        for step in range(1, size):
            source = lax.rem(me + size - step, size)
            ref = self.arrived.at[pl.ds(self.used + source * self.length, self.length)]
            self.links.copy(ref, ref, self.first + step - 1, peer(source)).wait_recv()
        total = self.arrived[pl.ds(self.used, self.length)].astype(F32)
        for other in range(1, size):
            total += self.arrived[pl.ds(self.used + other * self.length, self.length)].astype(F32)
        self.full[pl.ds(self.full_place(self.terms), self.length)] = total.astype(BF16)

    def gather(self, name):
        size, me, peer = self.links.group(name)
        self.first = first = self.links.take(size - 1)
        terms, length = tuple(self.terms), self.length

        def make(step):
            mine = self.full.at[pl.ds(self.full_place(terms), length)]
            return mine, mine, first + step - 1, peer(lax.rem(me + step, size))

        for step in range(1, size):
            self.links.put(functools.partial(make, step))

    def gathered(self, name):
        size, me, peer = self.links.group(name)
        stride = [term for term in self.terms if term[0] == name][0][2]
        self.terms = [term for term in self.terms if term[0] != name]
        for step in range(1, size):
            source = lax.rem(me + size - step, size)
            offset = self.full_place(self.terms) + source * stride
            ref = self.full.at[pl.ds(offset, self.length)]
            self.links.copy(ref, ref, self.first + step - 1, peer(source)).wait_recv()
        self.length = self.length * size


def block_kernel(
    stop,
    plan,
    x_ref,
    cells_ref,
    cot_ref,
    wq_ref,
    wk_ref,
    wv_ref,
    wp_ref,
    fc1_ref,
    fb1_ref,
    fc2_ref,
    g1_ref,
    b1_ref,
    pb_ref,
    g2_ref,
    b2_ref,
    fb2_ref,
    posw_ref,
    gate_ref,
    out_ref,
    gi_ref,
    mlp_ref,
    att_ref,
    small_ref,
    x_s,
    cot_s,
    w_s,
    w_t,
    share_s,
    fc_s,
    vec_s,
    cells_s,
    hot,
    norm_s,
    ncan,
    qkv,
    att_t,
    gcan,
    pos_b,
    pos_s,
    con_b,
    con_s,
    att_s,
    mid_s,
    n2_s,
    cb_s,
    hid,
    dbef,
    gm_s,
    acc,
    mlp_part,
    mlp_core,
    mlp_pair,
    mlp_tensor,
    mlp_sum,
    mlp_arrived,
    att_part,
    att_arrived,
    mlp_full,
    att_full,
    small_s,
    small_arrived,
    local_sem,
    send_sem,
    recv_sem,
):
    D, rows, lanes = plan.width, plan.rows, plan.lanes
    windows = plan.windows
    links = Links(plan, send_sem, recv_sem)
    t, core = links.t, links.core
    other_core = (links.d + 1 - 2 * core, t)

    def local(source, target, number):
        return pltpu.make_async_copy(source, target, local_sem.at[number])

    loads = [
        local(x_ref, x_s, 0),
        local(fc1_ref, share_s.at[0], 1),
        local(fc2_ref, share_s.at[1], 2),
        local(wq_ref, w_s.at[0], 3),
        local(wk_ref, w_s.at[1], 4),
        local(wv_ref, w_s.at[2], 5),
        local(wp_ref, w_s.at[3], 6),
        local(cot_ref, cot_s, 7),
    ]
    for load in loads:
        load.start()
    links.greet()

    def position(g, carry):
        heads = [g * (HEADS // GROUPS) + i for i in range(HEADS // GROUPS)]
        sigs = [1.0 / (1.0 + jnp.exp(-jnp.full((1, TOK), gate_ref[0, h], F32))) for h in heads]
        for big, store in ((True, pos_b), (False, pos_s)):
            col_off, row_off, dist, live = offsets(big)
            logits = [
                jnp.where(
                    live,
                    posw_ref[0, h] * col_off + posw_ref[1, h] * row_off + posw_ref[2, h] * dist,
                    FAR,
                )
                for h in heads
            ]
            tops = [jnp.max(item, axis=0, keepdims=True) for item in logits]
            exps = [jnp.exp(item - top) for item, top in zip(logits, tops)]
            totals = [sig / jnp.sum(e, axis=0, keepdims=True) for sig, e in zip(sigs, exps)]
            for h, e, total in zip(heads, exps, totals):
                store[h] = e * total
        return carry

    lax.fori_loop(0, GROUPS, position, 0)
    parts = list(range(plan.mains)) + (["tail"] if plan.tails else [])

    def hidden_lanes(owner, holder, part):
        turn = lax.rem(owner - holder - 1 + plan.tensor, plan.tensor)
        if part == "tail":
            start = plan.first_tail * CHUNK + owner * LANES
            return pl.ds(pl.multiple_of(start, LANES), LANES)
        own = turn == plan.tensor - 1
        step = jnp.where(own, plan.own_step[part], plan.other_step[part] + turn)
        return pl.ds(pl.multiple_of(step * CHUNK, CHUNK), CHUNK)

    first_weight = links.take(2 * plan.tensor * len(parts))
    loads[1].wait()
    loads[2].wait()
    for part in parts:
        to = hidden_lanes(t, t, part)
        low = (plan.mains if part == "tail" else part) * CHUNK
        high = min(plan.share, low + to.size)
        for kind in range(2):
            values = share_s[kind, :, low:high]
            if kind == 0:
                bias = fb1_ref[low:high].astype(F32).reshape(1, high - low)
            else:
                bias = jnp.zeros((1, high - low), F32)
            bias = jnp.where(iota((16, high - low), 0) == 0, bias, 0.0).astype(BF16)
            values = jnp.concatenate([values, bias], axis=0)
            if to.size > high - low:
                fill = jnp.zeros((plan.tall, to.size - high + low), BF16)
                values = jnp.concatenate([values, fill], axis=1)
            fc_s[kind, :, to] = values

    def send_weights(step, at):
        to = lax.rem(t + step, plan.tensor)
        return (
            fc_s.at[core, :, hidden_lanes(t, t, parts[at])],
            fc_s.at[core, :, hidden_lanes(t, to, parts[at])],
            first_weight + len(parts) * step + at,
            (links.d, to),
        )

    def arrived_weights(step, at, kind):
        source = lax.rem(t + plan.tensor - step, plan.tensor)
        ref = fc_s.at[kind, :, hidden_lanes(source, t, parts[at])]
        return ref, ref, first_weight + len(parts) * step + at, (links.d, source)

    def handed_weights(step, at, kind):
        ref, _, number, _ = arrived_weights(step, at, kind)
        return links.copy(ref, ref, number + plan.tensor * len(parts), other_core)

    weight_copies = [(step, at) for step in range(1, plan.tensor) for at in range(len(parts))]
    links.await_greetings()
    for step, at in weight_copies:
        links.put(functools.partial(send_weights, step, at))

    def pass_weights():
        for step, at in weight_copies:
            links.copy(*arrived_weights(step, at, core)).wait_recv()
            handed_weights(step, at, core).start()

    def wait_weights():
        for step, at in weight_copies:
            handed_weights(step, at, 1 - core).wait_recv()
            handed_weights(step, at, core).wait_send()

    for number, ref in enumerate((g1_ref, b1_ref, pb_ref, g2_ref, b2_ref, fb2_ref)):
        for tile in range(round_up(D, LANES) // LANES):
            low, high = tile * LANES, min(D, tile * LANES + LANES)
            spread = jnp.broadcast_to(ref[:, low:high], (LANES, high - low))
            vec_s[number, low:high, :] = jnp.transpose(spread)
    GAIN1, BIAS1, PBIAS, GAIN2, BIAS2, FBIAS2 = range(6)

    acc[...] = jnp.zeros(acc.shape, F32)
    small_s[...] = jnp.zeros(small_s.shape, F32)
    for number in range(3, 7):
        loads[number].wait()
    for number in range(4):
        w_t[number] = jnp.transpose(w_s[number])
    if stop == 1:
        return

    loads[0].wait()

    def for_blocks(body):
        def one(b, carry):
            body(pl.ds(pl.multiple_of(b * BLOCK, BLOCK), BLOCK), BLOCK)
            return carry

        lax.fori_loop(0, rows // BLOCK, one, 0)
        if rows % BLOCK:
            body(pl.ds(rows // BLOCK * BLOCK, rows % BLOCK), rows % BLOCK)

    def spread(number, count):
        vector = vec_s[number]
        return jnp.concatenate([vector] * (round_up(count, LANES) // LANES), axis=1)[:, :count]

    def gather_up(number, values):
        for low in range(0, values.shape[1], LANES):
            part = values[:, low : low + LANES]
            acc[number, :D, : part.shape[1]] += part

    def norm_one(at, count):
        scaled, _ = norm_columns(x_s[:, at].astype(F32))
        normed = scaled * spread(GAIN1, count) + spread(BIAS1, count)
        norm_s[:, at] = normed.astype(BF16)

    for_blocks(norm_one)
    if rows < lanes:
        norm_s[:, rows:] = jnp.zeros((D, lanes - rows), BF16)

    def window_span(w):
        first = (w // 3) * PER_IMAGE + (w % 3) * BIG
        count = BIG if w % 3 < 2 else SMALL_CROPS * SMALL
        start = first // LANES * LANES
        return first, count, start, round_up(first + count, LANES) - start

    def window_lanes(w):
        _, _, start, width = window_span(w)
        return pl.ds(start, width)

    def one_hot(w):
        first, count, start, width = window_span(w)
        inside = iota((1, width), 1) + (start - first)
        token = cells_s[:, window_lanes(w)]
        if w % 3 == 2:
            crop = jnp.floor((inside.astype(F32) + 0.5) * (1.0 / SMALL)).astype(jnp.int32)
            token = token + crop * STRIDE
        token = jnp.where((inside >= 0) & (inside < count), token, -1)
        return jnp.where(iota((TOK, width), 0) == token, 1.0, 0.0).astype(BF16)

    cells_s[...] = jnp.full(cells_s.shape, -1, jnp.int32)
    cells_s[:, :rows] = cells_ref[...].reshape(1, rows)
    for w in range(windows):
        hot[w, :, : window_span(w)[3]] = one_hot(w)

    def to_grid(w):
        return dot(norm_s[:, window_lanes(w)], hot[w, :, : window_span(w)[3]], NT).astype(BF16)

    def from_grid(values, w):
        return dot(values, hot[w, :, : window_span(w)[3]])

    for w in range(windows):
        ncan[w] = to_grid(w)

    def project(w, carry):
        canonical = ncan[w]
        for part in range(3):
            qkv[w, part * D : part * D + D, :] = dot(w_t[part], canonical).astype(BF16)
        return carry

    lax.fori_loop(0, windows, project, 0)
    if stop == 2:
        return

    extra_b = extra_rows(True)
    extra_s = extra_rows(False)

    def head_rows(part, h):
        return pl.ds(pl.multiple_of(part * D + h * HEAD_DIM, 16), HEAD_DIM)

    def window_kind(w):
        image, slot = w // 3, w % 3
        if slot < 2:
            return KEYS_BIG, pos_b, con_b, image * BIG_CROPS + slot, extra_b, whole, whole
        return KEYS_SMALL, pos_s, con_s, image, extra_s, own_crop, all_crops

    window_groups = [range(windows)]

    def forward_head(h, carry):
        sig = 1.0 / (1.0 + jnp.exp(-jnp.full((1, TOK), gate_ref[0, h], F32)))
        for group in window_groups:
            kinds = [window_kind(w) for w in group]
            scores = []
            for w, kind in zip(group, kinds):
                extra_q, extra_k = kind[4]
                q = jnp.concatenate([qkv[w, head_rows(0, h), :], extra_q], axis=0)
                k = jnp.concatenate([qkv[w, head_rows(1, h), :], extra_k], axis=0)
                scores.append(kind[5](dot(k[:, : kind[0]], q, TN)))
            tops = [jnp.max(s, axis=0, keepdims=True) for s in scores]
            exps = [jnp.exp2((s - top) * (SCALE * LOG2E)) for s, top in zip(scores, tops)]
            totals = [1.0 / jnp.sum(e, axis=0, keepdims=True) for e in exps]
            contents = [e * total for e, total in zip(exps, totals)]
            for kind, content in zip(kinds, contents):
                kind[2][h, kind[3]] = content.astype(BF16)
            mixtures = [
                kind[6]((1.0 - sig) * content + kind[1][h]).astype(BF16)
                for kind, content in zip(kinds, contents)
            ]
            for w, kind, mixture in zip(group, kinds, mixtures):
                v = qkv[w, head_rows(2, h), : kind[0]]
                att_t[w, head_rows(0, h), :] = dot(v, mixture).astype(BF16)
        return carry

    lax.fori_loop(0, HEADS, forward_head, 0)
    if stop == 3:
        return

    att_s[...] = jnp.zeros(att_s.shape, F32)
    for w in range(windows):
        att_s[:, window_lanes(w)] += from_grid(att_t[w], w)

    loads[7].wait()
    def norm_two(at, count):
        values = dot(w_t[3], att_s[:, at].astype(BF16))
        middle = x_s[:, at].astype(F32) + values + spread(PBIAS, count)
        mid_s[:, at] = middle
        scaled, _ = norm_columns(middle)
        n2_s[:D, at] = (scaled * spread(GAIN2, count) + spread(BIAS2, count)).astype(BF16)
        rounded = cot_s[:, at].astype(BF16)
        cb_s[:D, at] = rounded
        gather_up(3, rounded.astype(F32))
        att_s[:, at] = middle + spread(FBIAS2, count)

    for_blocks(norm_two)
    gm_s[...] = jnp.zeros(gm_s.shape, F32)
    if not plan.solo and plan.own_first < 2:
        pass_weights()
        wait_weights()
    n2_s[D:, :] = jnp.where(iota((16, rows), 0) == 0, 1.0, 0.0).astype(BF16)
    cb_s[D:, :] = jnp.zeros((16, rows), BF16)
    if stop == 4:
        return

    spans = [(low, min(CHUNK, rows - low)) for low in range(0, rows, CHUNK)]

    def activate(s, slot):
        cs = pl.ds(pl.multiple_of(s * CHUNK, CHUNK), CHUNK)
        up = jnp.transpose(fc_s[0, :, cs])
        down = jnp.transpose(fc_s[1, :, cs])
        for low, count in spans:
            at = pl.ds(low, count)
            before = dot(up, n2_s[:, at])
            dh = dot(down, cb_s[:, at])
            active, slope = gelu_parts(before)
            hid[slot, :, at] = active.astype(BF16)
            dbef[slot, :, at] = (dh * slope).astype(BF16)

    def consume(s, slot):
        cs = pl.ds(pl.multiple_of(s * CHUNK, CHUNK), CHUNK)
        for kind, left, right in ((0, n2_s, dbef), (1, cb_s, hid)):
            grad = dot(left[...], right[slot], NT).astype(BF16)
            for half in range(2):
                blocks = grad[:, half * LANES : half * LANES + LANES]
                mlp_part[kind, s, half] = blocks.reshape((plan.tile_rows,) + TILE)
        for low, count in spans:
            at = pl.ds(low, count)
            att_s[:, at] += dot(fc_s[1, :D, cs], hid[slot, :, at])
            gm_s[:, at] += dot(fc_s[0, :D, cs], dbef[slot, :, at])

    first_core = links.take(plan.steps)
    first_pair = links.take(plan.steps)
    first_tensor = links.take((plan.tensor - 1) * plan.tiles)
    timeline = Timeline()

    def core_copy(s):
        return links.copy(mlp_part.at[1 - core, s], mlp_core.at[s], first_core + s, other_core)

    rows_here = pl.ds(links.pair * plan.pair_rows, plan.pair_rows)
    rows_there = pl.ds((1 - links.pair) * plan.pair_rows, plan.pair_rows)
    other_pair = (links.d + 2 - 4 * links.pair, t)

    def pair_copy(s):
        source = mlp_part.at[core, s, :, rows_there]
        return links.copy(source, mlp_pair.at[s], first_pair + s, other_pair)

    def tensor_copy(s, half, tile, turn):
        to = lax.rem(t + 1 + turn, plan.tensor)
        return (
            mlp_part.at[core, s, half, rows_here],
            mlp_tensor.at[turn, tile],
            first_tensor + turn * plan.tiles + tile,
            (links.d, to),
        )

    def core_sum(s):
        links.copy(mlp_core.at[s], mlp_core.at[s], first_core + s, other_core).wait_recv()
        total = mlp_part[core, s].astype(F32) + mlp_core[s].astype(F32)
        mlp_part[core, s] = total.astype(BF16)
        pair_copy(s).start()

    def pair_sum(s):
        links.copy(mlp_pair.at[s], mlp_pair.at[s], first_pair + s, other_pair).wait_recv()
        total = mlp_part[core, s, :, rows_here].astype(F32) + mlp_pair[s].astype(F32)
        mlp_part[core, s, :, rows_here] = total.astype(BF16)
        kind, j, turn = plan.roles[s]
        if kind == "main" and turn < plan.tensor - 1:
            for half in range(2):
                links.copy(*tensor_copy(s, half, 2 * j + half, turn)).start()
        if kind == "tail" and plan.tensor > 1:
            for half in range(2):
                turn = lax.rem(2 * j + half - t - 1 + plan.tensor, plan.tensor)

                def send(turn=turn, half=half):
                    links.copy(*tensor_copy(s, half, plan.tiles - 1, turn)).start()

                pl.when(turn < plan.tensor - 1)(send)

    def collect(number):
        start = sum(plan.piece_blocks[:number]) // plan.pairs
        for at, tile in enumerate(plan.pieces[number]):
            for turn in range(plan.tensor - 1):
                ref = mlp_tensor.at[turn, tile]
                source = lax.rem(t - turn - 1 + plan.tensor, plan.tensor)
                links.copy(
                    ref, ref, first_tensor + turn * plan.tiles + tile, (links.d, source)
                ).wait_recv()
            if tile < 2 * plan.mains:
                step, half = plan.own_step[tile // 2], tile % 2
            else:
                step, half = plan.first_tail + t // 2, t % 2
            total = mlp_part[core, step, half, rows_here].astype(F32)
            for turn in range(plan.tensor - 1):
                total += mlp_tensor[turn, tile].astype(F32)
            low = start + at * plan.pair_rows
            mlp_sum[low : low + plan.pair_rows] = total.astype(BF16)
        low = start + len(plan.pieces[number]) * plan.pair_rows
        high = start + plan.piece_blocks[number] // plan.pairs
        if low < high:
            mlp_sum[low:high] = jnp.zeros((high - low,) + TILE, BF16)

    mlp_sums = []
    for number, size in enumerate(plan.piece_blocks):
        start = sum(plan.piece_blocks[:number])
        share = pl.ds(start // plan.pairs, size // plan.pairs)
        mlp_sums.append(
            Reduction(
                links,
                mlp_sum.at[share],
                size // plan.pairs,
                mlp_arrived.at[share],
                mlp_full,
                start,
                ("quad",),
                ("quad", "pair", "core"),
                held=(("pair", size // plan.pairs), ("core", plan.mlp_blocks)),
            )
        )
    summed = {}
    begun = set()

    def needed(number):
        tail = any(tile >= 2 * plan.mains for tile in plan.pieces[number])
        return [
            s
            for s, (kind, j, turn) in enumerate(plan.roles)
            if (kind == "tail" and tail) or (kind == "main" and 2 * j in plan.pieces[number])
        ]

    def step_done(s, now):
        summed[s] = now
        for number in range(len(plan.pieces)):
            steps = needed(number)
            if number in begun or any(step not in summed for step in steps):
                continue
            begun.add(number)
            sent = [
                summed[step]
                for step in steps
                if plan.roles[step][0] == "tail" or plan.roles[step][2] < plan.tensor - 1
            ]
            timeline.add(
                max([now] + [at + SENT for at in sent]),
                mlp_sums[number].actions(before=functools.partial(collect, number)),
                f"mlp{number}",
            )

    def begin_step(s, now):
        timeline.add(
            now,
            [
                (lambda: core_copy(s).start(), DELAYS["core"], None),
                (lambda: core_sum(s), DELAYS["pair"], None),
                (lambda: pair_sum(s), 0.0, functools.partial(step_done, s)),
            ],
            f"step{s}",
        )

    activate(0, 0)
    if not plan.solo and plan.own_first >= 2:
        pass_weights()

    def mlp_step(s, carry):
        consume(s - 1, (s - 1) % 2)
        activate(s, s % 2)
        if not plan.solo:
            if plan.own_first >= 2:
                pl.when(s == plan.own_first - 1)(wait_weights)
            for k in range(1, plan.steps):
                begin_step(k - 1, MLP_STEP * k + 1)
                timeline.point(MLP_STEP * k + 1, s == k)
        return carry

    lax.fori_loop(1, plan.steps, mlp_step, 0)
    last = plan.steps - 1
    consume(last, last % 2)
    now = MLP_STEP * plan.steps + 1
    if not plan.solo:
        begin_step(last, now)
        timeline.point(now)
    if stop == 5:
        return

    def norm_two_back(at, count):
        n2_s[:D, at] = att_s[:, at].astype(BF16)
        grad = gm_s[:, at]
        scaled, inverse = norm_columns(mid_s[:, at])
        back = norm_back(grad, scaled, inverse, spread(GAIN2, count))
        grad_middle = cot_s[:, at] + back
        cot_s[:, at] = grad_middle
        branch = grad_middle.astype(BF16)
        norm_s[:, at] = branch
        gather_up(0, grad * scaled)
        gather_up(1, grad)
        gather_up(2, branch.astype(F32))

    for_blocks(norm_two_back)
    store_out = local(n2_s.at[pl.ds(0, D)], out_ref, 8)
    store_out.start()

    now += NORM_TIME
    timeline.point(now)

    wide = pl.ds(round_up(D, LANES), D)
    for w in range(windows):
        gcan[w] = to_grid(w)
    gm_s[:, wide] = sum(dot(att_t[w], gcan[w], NT) for w in range(windows))

    def project_back(w, carry):
        att_t[w] = dot(w_s[3], gcan[w]).astype(BF16)
        return carry

    lax.fori_loop(0, windows, project_back, 0)
    timeline.point(now + PROJECT_TIME * windows)
    now += PROJECT_TIME * windows
    if stop == 6:
        return

    def att_start(number, total):
        gm_s[:, :D] = total
        for tile in range(plan.width_tiles):
            blocks = gm_s[:, tile * LANES : tile * LANES + LANES].astype(BF16)
            at = tile * (D // 16)
            att_part[number, at : at + D // 16] = blocks.reshape((D // 16,) + TILE)
        edge = gm_s[:, plan.width_tiles * LANES : plan.width_tiles * LANES + LANES]
        low = D - plan.fold
        lane = iota((low, LANES), 1)
        folded = jnp.where(
            lane < plan.left_over, edge[:low], pltpu.roll(edge[plan.fold :], plan.left_over, 1)
        )
        at = plan.full_blocks
        att_part[number, at : at + low // 16] = folded.astype(BF16).reshape((low // 16,) + TILE)
        if low < plan.fold:
            rows_left = edge[low : plan.fold].astype(BF16)
            att_part[number, at + low // 16 : at + plan.fold // 16] = rows_left.reshape(
                ((plan.fold - low) // 16,) + TILE
            )
        spare = plan.att_blocks - at - plan.fold // 16
        if spare:
            att_part[number, plan.att_blocks - spare :] = jnp.zeros((spare,) + TILE, BF16)

    direct = plan.direct
    routes = [(("core", "pair", "quad"), ("quad", "pair", "core"), "tensor")] * 4
    if direct:
        routes = [(("core", "cross", "quad"), ("quad", "cross", "core"))] * 3
        routes.append((("core", "all"), ("all", "core")))

    att_sums = [
        Reduction(
            links,
            att_part.at[number],
            plan.att_blocks,
            att_arrived.at[number],
            att_full.at[number],
            0,
            *routes[number],
        )
        for number in range(GROUPS + 1)
    ]

    def begin_att(number, now):
        timeline.add(now, att_sums[number].actions(), f"att{number}")

    att_start(0, gm_s[:, wide])
    if not plan.solo:
        begin_att(0, now)
        timeline.point(now)

    def weight_grad(g):
        def joined(w):
            parts = [
                qkv[w, pl.ds(pl.multiple_of(part * D + g * (D // GROUPS), 16), D // GROUPS), :]
                for part in range(3)
            ]
            return jnp.concatenate(parts, axis=0)

        total = dot(ncan[0], joined(0), NT)
        for w in range(1, windows):
            total += dot(ncan[w], joined(w), NT)
        att_start(1 + g, total)

    window_groups = [range(windows)]

    def backward_head(h, carry):
        sig = 1.0 / (1.0 + jnp.exp(-jnp.full((1, TOK), gate_ref[0, h], F32)))
        keep = 1.0 - sig
        factor = keep * SCALE
        sums = [0.0, 0.0]
        gate_row = jnp.zeros((1, TOK), F32)
        for group in window_groups:
            kinds = [window_kind(w) for w in group]
            queries = [qkv[w, head_rows(0, h), :] for w in group]
            keys = [qkv[w, head_rows(1, h), : kind[0]] for w, kind in zip(group, kinds)]
            vals = [qkv[w, head_rows(2, h), : kind[0]] for w, kind in zip(group, kinds)]
            grads = [att_t[w, head_rows(0, h), :] for w in group]
            contents = [kind[2][h, kind[3]].astype(F32) for kind in kinds]
            grad_mixes = [
                kind[5](dot(v, da, TN)) for kind, v, da in zip(kinds, vals, grads)
            ]
            mixtures = [
                kind[6](keep * content + kind[1][h]).astype(BF16)
                for kind, content in zip(kinds, contents)
            ]
            grad_vals = [dot(da, mixture, NT) for da, mixture in zip(grads, mixtures)]
            rows_sum = [
                jnp.sum(content * grad_mix, axis=0, keepdims=True)
                for content, grad_mix in zip(contents, grad_mixes)
            ]
            grad_scores = [
                kind[6](content * (grad_mix - row)).astype(BF16)
                for kind, content, grad_mix, row in zip(kinds, contents, grad_mixes, rows_sum)
            ]
            for w, grad_mix, row in zip(group, grad_mixes, rows_sum):
                sums[w % 3 // 2] += grad_mix
                gate_row -= row
            grad_queries = [dot(k, grad_s) for k, grad_s in zip(keys, grad_scores)]
            grad_keys = [dot(q, grad_s, NT) for q, grad_s in zip(queries, grad_scores)]
            for w, kind, dq, dk, dv in zip(group, kinds, grad_queries, grad_keys, grad_vals):
                qkv[w, head_rows(0, h), :] = (dq * factor).astype(BF16)
                qkv[w, head_rows(1, h), : kind[0]] = (dk * factor[:, : kind[0]]).astype(BF16)
                qkv[w, head_rows(2, h), : kind[0]] = dv.astype(BF16)
        results = [jnp.zeros((1, TOK), F32)] * 3
        for big, pos, grad_mix in ((True, pos_b, sums[0]), (False, pos_s, sums[1])):
            col_off, row_off, dist, _ = offsets(big)
            row = jnp.sum(pos[h] * grad_mix, axis=0, keepdims=True) / sig
            grad_l = pos[h] * (grad_mix - row)
            gate_row += row
            results = [
                old + jnp.sum(grad_l * off, axis=0, keepdims=True)
                for old, off in zip(results, (col_off, row_off, dist))
            ]
        results = jnp.concatenate(results + [gate_row * sig * keep], axis=0)
        column = jnp.sum(results, axis=1, keepdims=True)
        lane = iota((4, LANES), 1)
        small_s[24:28, :] += jnp.where(lane == h, column, 0.0)
        pl.when(h % (HEADS // GROUPS) == HEADS // GROUPS - 1)(
            lambda: weight_grad(h // (HEADS // GROUPS))
        )
        if not plan.solo:
            for k in range(HEADS):
                time = now + HEAD_TIME * (k + 1)
                if k % (HEADS // GROUPS) == HEADS // GROUPS - 1:
                    begin_att(1 + k // (HEADS // GROUPS), time)
                timeline.point(time, h == k)
        return carry

    lax.fori_loop(0, HEADS, backward_head, 0)
    now += HEAD_TIME * HEADS
    if stop == 7:
        return

    att_s[...] = jnp.zeros(att_s.shape, F32)

    for w in range(windows):
        grad = dot(w_s[0], qkv[w, :D, :])
        grad += dot(w_s[1], qkv[w, D : 2 * D, :])
        grad += dot(w_s[2], qkv[w, 2 * D :, :])
        high = grad.astype(BF16)
        low = (grad - high.astype(F32)).astype(BF16)
        att_s[:, window_lanes(w)] += from_grid(high, w) + from_grid(low, w)
        timeline.point(now + WINDOW_TIME * (w + 1))
    now += WINDOW_TIME * windows

    def norm_one_back(at, count):
        scaled, inverse = norm_columns(x_s[:, at].astype(F32))
        grad = att_s[:, at]
        cot_s[:, at] += norm_back(grad, scaled, inverse, spread(GAIN1, count))
        gather_up(4, grad * scaled)
        gather_up(5, grad)

    for_blocks(norm_one_back)
    store_gi = local(cot_s, gi_ref, 9)
    store_gi.start()
    for number in range(6):
        for tile in range(round_up(D, LANES) // LANES):
            turned = jnp.transpose(acc[number, tile * LANES : tile * LANES + LANES, :])
            at = number * 4 + tile
            small_s[at : at + 1, :] = jnp.sum(turned, axis=0, keepdims=True)

    now += NORM_TIME
    small_places = {}

    def small_begin(name):
        size, me, peer = links.group(name)
        first = links.take(size - 1)
        used = sum(size for size, _ in small_places.values())
        small_places[name] = size, first
        small_arrived[used + me] = small_s[...]

        def make(step):
            slot = small_arrived.at[used + me]
            return slot, slot, first + step - 1, peer(lax.rem(me + step, size))

        for step in range(1, size):
            links.put(functools.partial(make, step))

    def small_end(name):
        size, me, peer = links.group(name)
        _, first = small_places[name]
        used = sum(size for size, _ in small_places.values()) - size
        for step in range(1, size):
            source = lax.rem(me + size - step, size)
            ref = small_arrived.at[used + source]
            links.copy(ref, ref, first + step - 1, peer(source)).wait_recv()
        total = small_arrived[used]
        for other in range(1, size):
            total += small_arrived[used + other]
        small_s[...] = total

    names = ("core", "all") if direct else ("core", "tensor", "pair", "quad")
    names = [name for name in names if links.group(name)[0] > 1]
    if names:
        actions = [(functools.partial(small_begin, names[0]), DELAYS[names[0]], None)]
        for before, name in zip(names, names[1:]):

            def turn(before=before, name=name):
                small_end(before)
                small_begin(name)

            actions.append((turn, DELAYS[name], None))
        actions.append((functools.partial(small_end, names[-1]), 0.0, None))
        timeline.add(now, actions, "small")
    timeline.finish(now)
    small_ref[...] = small_s[...]
    stores = [local(mlp_full, mlp_ref, 10), local(att_full, att_ref, 11)]
    for store in stores:
        store.start()
    store_out.wait()
    store_gi.wait()
    if not plan.solo:
        for s in range(plan.steps):
            core_copy(s).wait_send()
            pair_copy(s).wait_send()
        for s, (kind, j, turn) in enumerate(plan.roles):
            if kind == "main" and turn < plan.tensor - 1:
                for half in range(2):
                    links.copy(*tensor_copy(s, half, 2 * j + half, turn)).wait_send()
        if plan.tails:
            for turn in range(plan.tensor - 1):
                owner = lax.rem(t + 1 + turn, plan.tensor)
                links.copy(
                    *tensor_copy(plan.first_tail + owner // 2, owner % 2, plan.tiles - 1, turn)
                ).wait_send()
    links.drain()
    for store in stores:
        store.wait()


def finish_kernel(
    plan,
    out_in,
    gi_in,
    mlp_in,
    att_in,
    small_in,
    out_ref,
    gi_ref,
    dq_ref,
    dk_ref,
    dv_ref,
    dproj_ref,
    dfc1_ref,
    dfc2_ref,
    dfb1_ref,
    pos_ref,
    gate_ref,
    *refs
):
    vector_refs, (mlp_s, att_s, square_s, wide_s, out_s, gi_s, sems) = refs[:6], refs[6:]
    D = plan.width
    copies = [
        pltpu.make_async_copy(source, target, sems.at[number])
        for number, (source, target) in enumerate(
            (
                (mlp_in.at[pl.ds(0, plan.mlp_blocks)], mlp_s.at[0]),
                (mlp_in.at[pl.ds(plan.mlp_blocks, plan.mlp_blocks)], mlp_s.at[1]),
                (att_in, att_s),
                (gi_in, gi_s),
                (out_in, out_s),
                (wide_s.at[0], dfc1_ref),
                (wide_s.at[1], dfc2_ref),
                (square_s.at[0], dproj_ref),
                (square_s.at[1], dq_ref),
                (square_s.at[2], dk_ref),
                (square_s.at[3], dv_ref),
                (gi_s, gi_ref),
                (out_s, out_ref),
            )
        )
    ]
    for copy in copies[:5]:
        copy.start()
    where = {
        tile: (sum(plan.piece_blocks[:number]), plan.piece_blocks[number], at)
        for number, piece in enumerate(plan.pieces)
        for at, tile in enumerate(piece)
    }
    for kind in range(2):
        copies[kind].wait()
        for tile in range(plan.tiles):
            start, size, at = where[tile]
            values = []
            for pair in range(plan.pairs):
                first = start + pair * (size // plan.pairs) + at * plan.pair_rows
                values.append(mlp_s[kind, first : first + plan.pair_rows])
            values = jnp.concatenate(values, axis=0).reshape(plan.tall, LANES).astype(F32)
            low, high = tile * LANES, min(plan.share, tile * LANES + LANES)
            wide_s[kind, :, low:high] = values[:D, : high - low]
            if kind == 0:
                dfb1_ref[low:high] = values[D : D + 1, : high - low].reshape(high - low)
        copies[5 + kind].start()
    copies[2].wait()
    for number in range(2):
        copies[3 + number].wait()
        copies[11 + number].start()
    below = D - plan.fold
    part = D // GROUPS
    for number in range(GROUPS + 1):
        tiles = [
            att_s[number, tile * (D // 16) : (tile + 1) * (D // 16)].reshape(D, LANES).astype(F32)
            for tile in range(plan.width_tiles)
        ]
        at = plan.full_blocks
        folded = att_s[number, at : at + plan.fold // 16].reshape(plan.fold, LANES).astype(F32)
        lower = pltpu.roll(folded, LANES - plan.left_over, 1)[:below]
        edge = jnp.concatenate([folded, lower], axis=0)[:, : plan.left_over]
        total = jnp.concatenate(tiles + [edge], axis=1)
        if number == 0:
            square_s[0] = total
            copies[7].start()
        else:
            to = (number - 1) * part
            for place in range(3):
                square_s[1 + place, :, to : to + part] = total[:, place * part : place * part + part]
    for copy in copies[8:11]:
        copy.start()
    for number, target in enumerate(vector_refs):
        for tile in range(round_up(D, LANES) // LANES):
            low, high = tile * LANES, min(D, tile * LANES + LANES)
            row = number * 4 + tile
            target[:, low:high] = small_in[row : row + 1, : high - low]
    pos_ref[...] = small_in[24:27, :HEADS]
    gate_ref[...] = small_in[27:28, :HEADS].reshape(HEADS)
    for copy in copies[5:]:
        copy.wait()


def local(
    stop,
    dp,
    tensor,
    inputs,
    patch_cells,
    ln1_gain,
    ln1_bias,
    w_query,
    w_key,
    w_value,
    w_proj,
    proj_bias,
    pos_weight,
    gate_param,
    ln2_gain,
    ln2_bias,
    fc1_weight,
    fc1_bias,
    fc2_weight,
    fc2_bias,
    cotangent,
):
    rows, D = inputs.shape
    share = fc1_weight.shape[1]
    plan = Plan(dp, tensor, rows, D, share)
    windows, lanes, steps = plan.windows, plan.lanes, plan.steps

    def vector(values):
        return values.reshape(1, -1)

    vmem = pl.BlockSpec(memory_space=pltpu.VMEM)
    smem = pl.BlockSpec(memory_space=pltpu.SMEM)
    anywhere = pl.BlockSpec(memory_space=pl.ANY)
    params = {} if plan.solo else {"collective_id": 0, "has_side_effects": True}
    slots = plan.cores + plan.tensor + plan.pairs + plan.quads
    if plan.direct:
        slots = plan.cores + tensor * dp // plan.cores
    out, gi, mlp, att, small = pl.pallas_call(
        functools.partial(block_kernel, stop, plan),
        out_shape=(
            jax.ShapeDtypeStruct((D, rows), BF16),
            jax.ShapeDtypeStruct((D, rows), F32),
            jax.ShapeDtypeStruct((2 * plan.mlp_blocks,) + TILE, BF16),
            jax.ShapeDtypeStruct((GROUPS + 1, plan.att_blocks) + TILE, BF16),
            jax.ShapeDtypeStruct((SMALL_ROWS, LANES), F32),
        ),
        in_specs=[anywhere, vmem] + [anywhere] * 6 + [vmem] + [anywhere] + [vmem] * 6 + [smem] * 2,
        out_specs=(anywhere, anywhere, anywhere, anywhere, vmem),
        scratch_shapes=[
            pltpu.VMEM((D, rows), BF16),
            pltpu.VMEM((D, rows), F32),
            pltpu.VMEM((4, D, D), BF16),
            pltpu.VMEM((4, D, D), BF16),
            pltpu.VMEM((2, D, share), BF16),
            pltpu.VMEM((2, plan.tall, plan.hidden), BF16),
            pltpu.VMEM((6, D, LANES), F32),
            pltpu.VMEM((1, lanes), jnp.int32),
            pltpu.VMEM((windows, TOK, WIDE), BF16),
            pltpu.VMEM((D, lanes), BF16),
            pltpu.VMEM((windows, D, TOK), BF16),
            pltpu.VMEM((windows, 3 * D, TOK), BF16),
            pltpu.VMEM((windows, D, TOK), BF16),
            pltpu.VMEM((windows, D, TOK), BF16),
            pltpu.VMEM((HEADS, KEYS_BIG, TOK), F32),
            pltpu.VMEM((HEADS, STRIDE, TOK), F32),
            pltpu.VMEM((HEADS, BIG_CROPS * plan.images, KEYS_BIG, TOK), BF16),
            pltpu.VMEM((HEADS, plan.images, STRIDE, TOK), BF16),
            pltpu.VMEM((D, lanes), F32),
            pltpu.VMEM((D, lanes), F32),
            pltpu.VMEM((plan.tall, rows), BF16),
            pltpu.VMEM((plan.tall, rows), BF16),
            pltpu.VMEM((2, CHUNK, rows), BF16),
            pltpu.VMEM((2, CHUNK, rows), BF16),
            pltpu.VMEM((D, lanes), F32),
            pltpu.VMEM((6, round_up(D, LANES), LANES), F32),
            pltpu.VMEM((2, steps, 2, plan.tile_rows) + TILE, BF16),
            pltpu.VMEM((steps, 2, plan.tile_rows) + TILE, BF16),
            pltpu.VMEM((steps, 2, plan.pair_rows) + TILE, BF16),
            pltpu.VMEM((max(1, tensor - 1), plan.tiles, plan.pair_rows) + TILE, BF16),
            pltpu.VMEM((plan.mlp_blocks // plan.pairs,) + TILE, BF16),
            pltpu.VMEM((plan.mlp_blocks // plan.pairs,) + TILE, BF16),
            pltpu.VMEM((GROUPS + 1, plan.att_blocks) + TILE, BF16),
            pltpu.VMEM((GROUPS + 1, plan.att_arrived) + TILE, BF16),
            pltpu.VMEM((2 * plan.mlp_blocks,) + TILE, BF16),
            pltpu.VMEM((GROUPS + 1, plan.att_blocks) + TILE, BF16),
            pltpu.VMEM((SMALL_ROWS, LANES), F32),
            pltpu.VMEM((slots, SMALL_ROWS, LANES), F32),
            pltpu.SemaphoreType.DMA((12,)),
            pltpu.SemaphoreType.DMA((plan.semaphores,)),
            pltpu.SemaphoreType.DMA((plan.semaphores,)),
        ],
        compiler_params=pltpu.CompilerParams(vmem_limit_bytes=63 * 1024 * 1024, **params),
    )(
        inputs.T,
        patch_cells,
        cotangent.T,
        w_query,
        w_key,
        w_value,
        w_proj,
        fc1_weight,
        fc1_bias,
        fc2_weight.T,
        vector(ln1_gain),
        vector(ln1_bias),
        vector(proj_bias),
        vector(ln2_gain),
        vector(ln2_bias),
        vector(fc2_bias),
        pos_weight,
        vector(gate_param),
    )
    square = jax.ShapeDtypeStruct((D, D), F32)
    wide = jax.ShapeDtypeStruct((D, share), F32)
    results = pl.pallas_call(
        functools.partial(finish_kernel, plan),
        out_shape=(
            jax.ShapeDtypeStruct((D, rows), BF16),
            jax.ShapeDtypeStruct((D, rows), F32),
        )
        + (square,) * 4
        + (wide,) * 2
        + (
            jax.ShapeDtypeStruct((share,), F32),
            jax.ShapeDtypeStruct((3, HEADS), F32),
            jax.ShapeDtypeStruct((HEADS,), F32),
        )
        + (jax.ShapeDtypeStruct((1, D), F32),) * 6,
        in_specs=[anywhere] * 4 + [vmem],
        out_specs=(anywhere,) * 8 + (vmem,) * 9,
        scratch_shapes=[
            pltpu.VMEM((2, plan.mlp_blocks) + TILE, BF16),
            pltpu.VMEM((GROUPS + 1, plan.att_blocks) + TILE, BF16),
            pltpu.VMEM((4, D, D), F32),
            pltpu.VMEM((2, D, share), F32),
            pltpu.VMEM((D, rows), BF16),
            pltpu.VMEM((D, rows), F32),
            pltpu.SemaphoreType.DMA((13,)),
        ],
        compiler_params=pltpu.CompilerParams(vmem_limit_bytes=63 * 1024 * 1024),
    )(out, gi, mlp, att, small)
    out, gi, dq, dk, dv, dproj, dfc1, dfc2, dfb1, pos, gate = results[:11]
    gain2, bias2, pbias, fbias2, gain1, bias1 = (item.reshape(D) for item in results[11:])
    return (
        out.T,
        gi.T,
        gain1,
        bias1,
        dq,
        dk,
        dv,
        dproj,
        pbias,
        pos,
        gate,
        gain2,
        bias2,
        dfc1,
        dfb1,
        dfc2.T,
        fbias2,
    )


def solution(mesh, stop=0):
    both = ("dp", "tensor")
    copied = P()
    in_specs = (
        (P(both, None), P(both))
        + (copied,) * 11
        + (P(None, "tensor"), P("tensor"), P("tensor", None), copied, P(both, None))
    )
    out_specs = (
        (P(both, None), P(both, None))
        + (copied,) * 11
        + (P(None, "tensor"), P("tensor"), P("tensor", None), copied)
    )
    return jax.shard_map(
        functools.partial(local, stop, mesh.shape["dp"], mesh.shape["tensor"]),
        mesh=mesh,
        in_specs=in_specs,
        out_specs=out_specs,
        check_vma=False,
    )
```

```python
import functools

import jax
import jax.numpy as jnp
from jax import lax
from jax.experimental import pallas as pl
from jax.experimental.pallas import tpu as pltpu
from jax.sharding import PartitionSpec as P

MESH = pl.DeviceIdType.MESH

MLP_STEP = 2.3
NORM_TIME = 3.2
GRID_TIME = 0.2
PROJECT_TIME = 0.4
HEAD_TIME = 1.1
GRADIENT_TIME = 1.0
WINDOW_TIME = 1.15
SENT = 5.5
MLP_PACES = (1.2, 1.4, 1.4)
ATT_PACES = (0.9, 0.9, 0.9, 0.9)
BUNDLES = ((0,), (1,), (2,), (3,))

HEADS = 9
HEAD_DIM = 48
BIG_SIDE = 14
SMALL_SIDE = 6
BIG_CROPS = 2
SMALL_CROPS = 6
PER_IMAGE = 608
BIG = BIG_SIDE * BIG_SIDE
SMALL = SMALL_SIDE * SMALL_SIDE
GROUPS = 3

EPS = 1e-06
F32 = jnp.float32
BF16 = jnp.bfloat16
LOG2E = 1.4426950408889634
SCALE = HEAD_DIM ** (-0.5)
FAR = -1e30

NN = (((1,), (0,)), ((), ()))
NT = (((1,), (1,)), ((), ()))
TN = (((0,), (0,)), ((), ()))

LANES = 128
TOK = 256
KEYS_BIG = 208
STRIDE = 40
KEYS_SMALL = SMALL_CROPS * STRIDE
WIDE = 384
CHUNK = 256
BLOCK = 256
TILE = (16, LANES)
SMALL_ROWS = 16
TOGETHER = 3


def dot(left, right, dims=NN):
    return lax.dot_general(left, right, dims, preferred_element_type=F32)


def round_up(count, unit):
    return (count + unit - 1) // unit * unit


def iota(shape, dim):
    return lax.broadcasted_iota(jnp.int32, shape, dim)


def lane_crop():
    token = iota((1, TOK), 1).astype(F32)
    return jnp.floor((token + 0.5) * (1.0 / STRIDE))


def grid_place(cell, side):
    row = jnp.floor((cell + 0.5) * (1.0 / side))
    return row, cell - side * row


def offsets(big):
    keys = KEYS_BIG if big else STRIDE
    side = BIG_SIDE if big else SMALL_SIDE
    key = iota((keys, TOK), 0).astype(F32)
    query = iota((keys, TOK), 1).astype(F32)
    if not big:
        query = query - STRIDE * lane_crop()
    row_j, col_j = grid_place(key, side)
    row_i, col_i = grid_place(query, side)
    col_off = col_j - col_i
    row_off = row_j - row_i
    return col_off, row_off, col_off * col_off + row_off * row_off, key < side * side


def extra_rows(big):
    feature = iota((16, TOK), 0)
    cell = iota((1, TOK), 1).astype(F32)
    if not big:
        cell = cell - STRIDE * lane_crop()
    query = jnp.where(feature == 0, 1.0, 0.0)
    key = jnp.where((feature == 0) & (cell > (BIG if big else SMALL) - 0.5), FAR, 0.0)
    return query.astype(BF16), key.astype(BF16)


def own_crop(full):
    crop = lane_crop()
    result = full[:STRIDE]
    for c in range(1, SMALL_CROPS):
        result = jnp.where(crop == c, full[c * STRIDE : (c + 1) * STRIDE], result)
    return result


def all_crops(own):
    crop = lane_crop()
    return jnp.concatenate([jnp.where(crop == c, own, 0.0) for c in range(SMALL_CROPS)], axis=0)


def whole(values):
    return values


def gelu_parts(before):
    cdf = 0.5 * (1.0 + lax.erf(before * 0.7071067811865476))
    density = jnp.exp(-0.5 * before * before) * 0.3989422804014327
    return before * cdf, cdf + before * density


def norm_columns(values):
    center = values - jnp.mean(values, axis=0, keepdims=True)
    inverse = lax.rsqrt(jnp.mean(center * center, axis=0, keepdims=True) + EPS)
    return center * inverse, inverse


def norm_back(grad_normed, scaled, inverse, gain):
    e = grad_normed * gain
    return inverse * (
        e
        - jnp.mean(e, axis=0, keepdims=True)
        - scaled * jnp.mean(e * scaled, axis=0, keepdims=True)
    )


class Plan:
    def __init__(self, dp, tensor, rows, width, share):
        self.dp, self.tensor = dp, tensor
        self.solo = dp == 1
        self.rows, self.width, self.share = rows, width, share
        self.images = rows // PER_IMAGE
        self.windows = 3 * self.images
        self.lanes = round_up(rows, CHUNK)
        self.padded = round_up(share, LANES)
        self.tiles = self.padded // LANES
        self.mains = self.padded // CHUNK
        self.tails = (self.padded % CHUNK) // LANES * ((tensor + 1) // 2)
        self.own_first = self.mains - 1
        self.roles = [("main", j, tensor - 1) for j in range(self.own_first)]
        self.own_step = list(range(self.own_first))
        self.other_step = []
        for j in range(self.mains):
            if j == self.mains - 1:
                self.first_tail = len(self.roles)
                self.roles += [("tail", m, 0) for m in range(self.tails)]
            self.other_step.append(len(self.roles))
            self.roles += [("main", j, turn) for turn in range(tensor - 1)]
        self.own_step.append(len(self.roles))
        self.roles.append(("main", self.mains - 1, tensor - 1))
        self.steps = len(self.roles)
        self.hidden = CHUNK * self.steps
        self.tall = width + 16
        self.tile_rows = self.tall // 16
        self.cores = 1 if self.solo else 2
        self.pairs = 1 if self.solo else 2
        self.quads = dp // (self.cores * self.pairs)
        self.direct = tensor * dp // self.cores <= 16
        self.pieces = [[2 * j, 2 * j + 1] for j in range(self.mains)]
        if self.tails:
            self.pieces[-1].append(self.tiles - 1)
        self.pair_rows = self.tile_rows // self.pairs
        self.piece_blocks = [
            self.pairs * round_up(len(piece) * self.pair_rows, self.quads) for piece in self.pieces
        ]
        self.mlp_blocks = sum(self.piece_blocks)
        self.width_tiles = width // LANES
        self.left_over = width % LANES
        self.full_blocks = self.width_tiles * (width // 16)
        self.fold = round_up(width // 2, 16)
        whole = self.full_blocks + self.fold // 16
        self.att_blocks = round_up(whole + 1, self.cores * self.pairs * self.quads)
        piece = self.att_blocks // (self.cores * self.pairs * self.quads)
        self.att_arrived = self.att_blocks + tensor * piece
        around = tensor * dp // self.cores if self.direct else tensor + self.pairs + self.quads
        self.sem_weights = 2 * tensor * (self.mains + 1)
        self.sem_steps = 2 * self.steps + (tensor - 1) * self.tiles
        self.semaphores = (
            self.sem_weights
            + self.sem_steps
            + len(self.pieces) * (2 * (self.pairs + dp // self.cores) + 1)
            + 4 * 2 * (1 + around)
            + 1
            + around
        )


class Timeline:
    def __init__(self):
        self.chains = []

    def add(self, ready, actions, label=""):
        self.chains.append([ready, list(actions), label, 0])

    def due(self, now):
        calls = []
        for chain in list(self.chains):
            if chain[1] and chain[0] <= now:
                call, delay, hook = chain[1].pop(0)
                chain[0] = now + delay
                calls.append((call, f"{chain[2]}_{chain[3]}"))
                chain[3] += 1
                if hook:
                    hook(now)
        return calls

    def point(self, now, condition=None):
        calls = self.due(now)
        if not calls:
            return

        def act():
            for call, _ in calls:
                call()

        if condition is None:
            act()
        else:
            pl.when(condition)(act)

    def finish(self, now):
        while any(chain[1] for chain in self.chains):
            self.point(now)
            now += 1.0


class Links:
    def __init__(self, plan, send, recv):
        self.plan, self.send, self.recv = plan, send, recv
        self.next = 0
        self.started = []
        if plan.solo:
            self.d = self.t = self.core = self.pair = self.quad = self.chip = self.place = self.crossed = 0
        else:
            self.d = lax.axis_index("dp")
            self.t = lax.axis_index("tensor")
            self.core = self.d % 2
            self.pair = (self.d // 2) % 2
            self.quad = self.d // 4
            self.chip = self.d // 2
            self.place = self.chip * plan.tensor + self.t
            self.crossed = self.pair * plan.tensor + self.t

    def take(self, count):
        first = self.next
        self.next += count
        return first

    def group(self, name):
        plan, d, t = self.plan, self.d, self.t
        if name == "core":
            return plan.cores, self.core, lambda k: (d - self.core + k, t)
        if name == "tensor":
            return plan.tensor, t, lambda k: (d, k)
        if name == "pair":
            return plan.pairs, self.pair, lambda k: (d + 2 * (k - self.pair), t)
        if name == "quad":
            return plan.quads, self.quad, lambda k: (d + 4 * (k - self.quad), t)
        if name == "cross":
            return (
                plan.pairs * plan.tensor,
                self.crossed,
                lambda k: (d + 2 * (k // plan.tensor - self.pair), k % plan.tensor),
            )
        count = plan.tensor
        return (
            plan.dp // plan.cores * count,
            self.place,
            lambda k: (2 * (k // count) + self.core, k % count),
        )

    def greet(self):
        if self.plan.solo:
            return
        semaphore = pltpu.get_barrier_semaphore()
        self.greeted = 0
        direct = ("core", "all")
        for name in direct if self.plan.direct else ("core", "tensor", "pair", "quad"):
            size, me, peer = self.group(name)
            for step in range(1, size):
                pl.semaphore_signal(
                    semaphore,
                    inc=1,
                    device_id=peer(lax.rem(me + step, size)),
                    device_id_type=MESH,
                )
                self.greeted += 1

    def await_greetings(self):
        if not self.plan.solo:
            pl.semaphore_wait(pltpu.get_barrier_semaphore(), self.greeted)

    def copy(self, source, target, number, device):
        return pltpu.make_async_remote_copy(
            src_ref=source,
            dst_ref=target,
            send_sem=self.send.at[number],
            recv_sem=self.recv.at[number],
            device_id=device,
            device_id_type=MESH,
        )

    def put(self, make):
        self.copy(*make()).start()
        self.started.append(make)

    def drain(self):
        for make in self.started:
            self.copy(*make()).wait_send()


DELAYS = {"core": 1.5, "pair": 4.5, "quad": 4.5, "tensor": 4.5, "cross": 5.0, "all": 6.5}


class Reduction:
    def __init__(self, links, part, length, arrived, full, full_start, groups, gathers, shared=None, held=()):
        self.links, self.part, self.arrived, self.full = links, part, arrived, full
        self.full_start = full_start
        self.length = length
        self.used = 0
        self.terms = [(name, links.group(name)[1], stride, False) for name, stride in held]
        self.stages = []

        def several(name):
            return name and links.group(name)[0] > 1

        groups = [name for name in groups if several(name)]
        gathers = [name for name in gathers if several(name)]
        for at, name in enumerate(groups):
            last = at == len(groups) - 1 and not several(shared)
            self.stages.append((name, self.scatter, functools.partial(self.add, last=last)))
        if several(shared):
            self.stages.append((shared, self.share, self.shared))
        for name in gathers:
            self.stages.append((name, self.gather, self.gathered))

    def actions(self, before=None, pace=1.0):
        calls = []
        for at in range(len(self.stages) + 1):
            todo = []
            if at == 0 and before:
                todo.append(before)
            if at:
                name, _, end = self.stages[at - 1]
                todo.append(functools.partial(end, name))
            if at < len(self.stages):
                name, start, _ = self.stages[at]
                todo.append(functools.partial(start, name))
                delay = DELAYS[name] * pace
            else:
                delay = 0.0
            calls.append((functools.partial(self.run, todo), delay, None))
        return calls

    @staticmethod
    def run(todo):
        for call in todo:
            call()

    def part_place(self):
        return sum(me * stride for _, me, stride, cut in self.terms if cut)

    def full_place(self, terms):
        return self.full_start + sum(me * stride for _, me, stride, _ in terms)

    def scatter(self, name):
        size, me, peer = self.links.group(name)
        piece = self.length // size
        self.first = first = self.links.take(size - 1)
        terms, used = tuple(self.terms), self.used

        def make(step):
            to = lax.rem(me + step, size)
            offset = sum(who * stride for _, who, stride, cut in terms if cut) + to * piece
            return (
                self.part.at[pl.ds(offset, piece)],
                self.arrived.at[pl.ds(used + (step - 1) * piece, piece)],
                first + step - 1,
                peer(to),
            )

        for step in range(1, size):
            self.links.put(functools.partial(make, step))

    def add(self, name, last):
        size, me, peer = self.links.group(name)
        piece = self.length // size
        self.terms.append((name, me, piece, True))
        mine = pl.ds(self.part_place(), piece)
        total = self.part[mine].astype(F32)
        for step in range(1, size):
            slot = pl.ds(self.used + (step - 1) * piece, piece)
            ref = self.arrived.at[slot]
            self.links.copy(
                ref, ref, self.first + step - 1, peer(lax.rem(me + step, size))
            ).wait_recv()
            total += self.arrived[slot].astype(F32)
        self.used += (size - 1) * piece
        self.length = piece
        if last:
            self.full[pl.ds(self.full_place(self.terms), piece)] = total.astype(BF16)
        else:
            self.part[mine] = total.astype(BF16)

    def share(self, name):
        size, me, peer = self.links.group(name)
        self.first = first = self.links.take(size - 1)
        length, used = self.length, self.used
        self.arrived[pl.ds(used + me * length, length)] = self.part[pl.ds(self.part_place(), length)]

        def make(step):
            ref = self.arrived.at[pl.ds(used + me * length, length)]
            return ref, ref, first + step - 1, peer(lax.rem(me + step, size))

        for step in range(1, size):
            self.links.put(functools.partial(make, step))

    def shared(self, name):
        size, me, peer = self.links.group(name)
        for step in range(1, size):
            source = lax.rem(me + size - step, size)
            ref = self.arrived.at[pl.ds(self.used + source * self.length, self.length)]
            self.links.copy(ref, ref, self.first + step - 1, peer(source)).wait_recv()
        total = self.arrived[pl.ds(self.used, self.length)].astype(F32)
        for other in range(1, size):
            total += self.arrived[pl.ds(self.used + other * self.length, self.length)].astype(F32)
        self.full[pl.ds(self.full_place(self.terms), self.length)] = total.astype(BF16)

    def gather(self, name):
        size, me, peer = self.links.group(name)
        self.first = first = self.links.take(size - 1)
        terms, length = tuple(self.terms), self.length

        def make(step):
            mine = self.full.at[pl.ds(self.full_place(terms), length)]
            return mine, mine, first + step - 1, peer(lax.rem(me + step, size))

        for step in range(1, size):
            self.links.put(functools.partial(make, step))

    def gathered(self, name):
        size, me, peer = self.links.group(name)
        stride = [term for term in self.terms if term[0] == name][0][2]
        self.terms = [term for term in self.terms if term[0] != name]
        for step in range(1, size):
            source = lax.rem(me + size - step, size)
            offset = self.full_place(self.terms) + source * stride
            ref = self.full.at[pl.ds(offset, self.length)]
            self.links.copy(ref, ref, self.first + step - 1, peer(source)).wait_recv()
        self.length = self.length * size


def block_kernel(
    stop,
    plan,
    x_ref,
    cells_ref,
    cot_ref,
    wq_ref,
    wk_ref,
    wv_ref,
    wp_ref,
    fc1_ref,
    fb1_ref,
    fc2_ref,
    g1_ref,
    b1_ref,
    pb_ref,
    g2_ref,
    b2_ref,
    fb2_ref,
    posw_ref,
    gate_ref,
    out_ref,
    gi_ref,
    mlp_ref,
    att_ref,
    small_ref,
    x_s,
    cot_s,
    w_s,
    w_t,
    share_s,
    fc_s,
    vec_s,
    cells_s,
    hot,
    norm_s,
    ncan,
    qkv,
    att_t,
    gcan,
    pos_b,
    pos_s,
    con_b,
    con_s,
    att_s,
    mid_s,
    n2_s,
    cb_s,
    hid,
    dbef,
    gm_s,
    acc,
    mlp_part,
    mlp_core,
    mlp_pair,
    mlp_tensor,
    mlp_sum,
    mlp_arrived,
    att_part,
    att_arrived,
    mlp_full,
    att_full,
    small_s,
    small_arrived,
    local_sem,
    send_sem,
    recv_sem,
):
    D, rows, lanes = plan.width, plan.rows, plan.lanes
    windows = plan.windows
    links = Links(plan, send_sem, recv_sem)
    t, core = links.t, links.core
    other_core = (links.d + 1 - 2 * core, t)

    def local(source, target, number):
        return pltpu.make_async_copy(source, target, local_sem.at[number])

    loads = [
        local(x_ref, x_s, 0),
        local(fc1_ref, share_s.at[0], 1),
        local(fc2_ref, share_s.at[1], 2),
        local(wq_ref, w_s.at[0], 3),
        local(wk_ref, w_s.at[1], 4),
        local(wv_ref, w_s.at[2], 5),
        local(wp_ref, w_s.at[3], 6),
        local(cot_ref, cot_s, 7),
    ]
    for load in loads:
        load.start()
    links.greet()

    def position(g, carry):
        heads = [g * (HEADS // GROUPS) + i for i in range(HEADS // GROUPS)]
        sigs = [1.0 / (1.0 + jnp.exp(-jnp.full((1, TOK), gate_ref[0, h], F32))) for h in heads]
        for big, store in ((True, pos_b), (False, pos_s)):
            col_off, row_off, dist, live = offsets(big)
            logits = [
                jnp.where(
                    live,
                    posw_ref[0, h] * col_off + posw_ref[1, h] * row_off + posw_ref[2, h] * dist,
                    FAR,
                )
                for h in heads
            ]
            tops = [jnp.max(item, axis=0, keepdims=True) for item in logits]
            exps = [jnp.exp(item - top) for item, top in zip(logits, tops)]
            totals = [sig / jnp.sum(e, axis=0, keepdims=True) for sig, e in zip(sigs, exps)]
            for h, e, total in zip(heads, exps, totals):
                store[h] = e * total
        return carry

    lax.fori_loop(0, GROUPS, position, 0)
    parts = list(range(plan.mains)) + (["tail"] if plan.tails else [])

    def hidden_lanes(owner, holder, part):
        turn = lax.rem(owner - holder - 1 + plan.tensor, plan.tensor)
        if part == "tail":
            start = plan.first_tail * CHUNK + owner * LANES
            return pl.ds(pl.multiple_of(start, LANES), LANES)
        own = turn == plan.tensor - 1
        step = jnp.where(own, plan.own_step[part], plan.other_step[part] + turn)
        return pl.ds(pl.multiple_of(step * CHUNK, CHUNK), CHUNK)

    first_weight = links.take(2 * plan.tensor * len(parts))
    loads[1].wait()
    loads[2].wait()
    for part in parts:
        to = hidden_lanes(t, t, part)
        low = (plan.mains if part == "tail" else part) * CHUNK
        high = min(plan.share, low + to.size)
        for kind in range(2):
            values = share_s[kind, :, low:high]
            if kind == 0:
                bias = fb1_ref[low:high].astype(F32).reshape(1, high - low)
            else:
                bias = jnp.zeros((1, high - low), F32)
            bias = jnp.where(iota((16, high - low), 0) == 0, bias, 0.0).astype(BF16)
            values = jnp.concatenate([values, bias], axis=0)
            if to.size > high - low:
                fill = jnp.zeros((plan.tall, to.size - high + low), BF16)
                values = jnp.concatenate([values, fill], axis=1)
            fc_s[kind, :, to] = values

    def send_weights(step, at):
        to = lax.rem(t + step, plan.tensor)
        return (
            fc_s.at[core, :, hidden_lanes(t, t, parts[at])],
            fc_s.at[core, :, hidden_lanes(t, to, parts[at])],
            first_weight + len(parts) * step + at,
            (links.d, to),
        )

    def arrived_weights(step, at, kind):
        source = lax.rem(t + plan.tensor - step, plan.tensor)
        ref = fc_s.at[kind, :, hidden_lanes(source, t, parts[at])]
        return ref, ref, first_weight + len(parts) * step + at, (links.d, source)

    def handed_weights(step, at, kind):
        ref, _, number, _ = arrived_weights(step, at, kind)
        return links.copy(ref, ref, number + plan.tensor * len(parts), other_core)

    weight_copies = [(step, at) for step in range(1, plan.tensor) for at in range(len(parts))]
    links.await_greetings()
    for step, at in weight_copies:
        links.put(functools.partial(send_weights, step, at))

    def pass_weights():
        for step, at in weight_copies:
            links.copy(*arrived_weights(step, at, core)).wait_recv()
            handed_weights(step, at, core).start()

    def wait_weights():
        for step, at in weight_copies:
            handed_weights(step, at, 1 - core).wait_recv()
            handed_weights(step, at, core).wait_send()

    for number, ref in enumerate((g1_ref, b1_ref, pb_ref, g2_ref, b2_ref, fb2_ref)):
        for tile in range(round_up(D, LANES) // LANES):
            low, high = tile * LANES, min(D, tile * LANES + LANES)
            spread = jnp.broadcast_to(ref[:, low:high], (LANES, high - low))
            vec_s[number, low:high, :] = jnp.transpose(spread)
    GAIN1, BIAS1, PBIAS, GAIN2, BIAS2, FBIAS2 = range(6)

    acc[...] = jnp.zeros(acc.shape, F32)
    small_s[...] = jnp.zeros(small_s.shape, F32)
    for number in range(3, 7):
        loads[number].wait()
    for number in range(4):
        w_t[number] = jnp.transpose(w_s[number])
    if stop == 1:
        return

    loads[0].wait()

    def for_blocks(body, start=None, total=0.0):
        count = round_up(rows, BLOCK) // BLOCK

        def point(k, condition=None):
            if start is not None:
                timeline.point(start + total * (k + 1) / count, condition)

        def one(b, carry):
            body(pl.ds(pl.multiple_of(b * BLOCK, BLOCK), BLOCK), BLOCK)
            for k in range(rows // BLOCK):
                point(k, b == k)
            return carry

        lax.fori_loop(0, rows // BLOCK, one, 0)
        if rows % BLOCK:
            body(pl.ds(rows // BLOCK * BLOCK, rows % BLOCK), rows % BLOCK)
            point(rows // BLOCK)

    def spread(number, count):
        vector = vec_s[number]
        return jnp.concatenate([vector] * (round_up(count, LANES) // LANES), axis=1)[:, :count]

    def gather_up(number, values):
        for low in range(0, values.shape[1], LANES):
            part = values[:, low : low + LANES]
            acc[number, :D, : part.shape[1]] += part

    def norm_one(at, count):
        scaled, _ = norm_columns(x_s[:, at].astype(F32))
        normed = scaled * spread(GAIN1, count) + spread(BIAS1, count)
        norm_s[:, at] = normed.astype(BF16)

    for_blocks(norm_one)
    if rows < lanes:
        norm_s[:, rows:] = jnp.zeros((D, lanes - rows), BF16)

    def window_span(w):
        first = (w // 3) * PER_IMAGE + (w % 3) * BIG
        count = BIG if w % 3 < 2 else SMALL_CROPS * SMALL
        start = first // LANES * LANES
        return first, count, start, round_up(first + count, LANES) - start

    def window_lanes(w):
        _, _, start, width = window_span(w)
        return pl.ds(start, width)

    def one_hot(w):
        first, count, start, width = window_span(w)
        inside = iota((1, width), 1) + (start - first)
        token = cells_s[:, window_lanes(w)]
        if w % 3 == 2:
            crop = jnp.floor((inside.astype(F32) + 0.5) * (1.0 / SMALL)).astype(jnp.int32)
            token = token + crop * STRIDE
        token = jnp.where((inside >= 0) & (inside < count), token, -1)
        return jnp.where(iota((TOK, width), 0) == token, 1.0, 0.0).astype(BF16)

    cells_s[...] = jnp.full(cells_s.shape, -1, jnp.int32)
    cells_s[:, :rows] = cells_ref[...].reshape(1, rows)
    for w in range(windows):
        hot[w, :, : window_span(w)[3]] = one_hot(w)

    def to_grid(w):
        return dot(norm_s[:, window_lanes(w)], hot[w, :, : window_span(w)[3]], NT).astype(BF16)

    def from_grid(values, w):
        return dot(values, hot[w, :, : window_span(w)[3]])

    for w in range(windows):
        ncan[w] = to_grid(w)

    def project(w, carry):
        canonical = ncan[w]
        for part in range(3):
            qkv[w, part * D : part * D + D, :] = dot(w_t[part], canonical).astype(BF16)
        return carry

    lax.fori_loop(0, windows, project, 0)
    if stop == 2:
        return

    extra_b = extra_rows(True)
    extra_s = extra_rows(False)

    def head_rows(part, h):
        return pl.ds(pl.multiple_of(part * D + h * HEAD_DIM, 16), HEAD_DIM)

    def window_kind(w):
        image, slot = w // 3, w % 3
        if slot < 2:
            return KEYS_BIG, pos_b, con_b, image * BIG_CROPS + slot, extra_b, whole, whole
        return KEYS_SMALL, pos_s, con_s, image, extra_s, own_crop, all_crops

    window_groups = [range(windows)]

    def forward_head(h, carry):
        sig = 1.0 / (1.0 + jnp.exp(-jnp.full((1, TOK), gate_ref[0, h], F32)))
        for group in window_groups:
            kinds = [window_kind(w) for w in group]
            scores = []
            for w, kind in zip(group, kinds):
                extra_q, extra_k = kind[4]
                q = jnp.concatenate([qkv[w, head_rows(0, h), :], extra_q], axis=0)
                k = jnp.concatenate([qkv[w, head_rows(1, h), :], extra_k], axis=0)
                scores.append(kind[5](dot(k[:, : kind[0]], q, TN)))
            tops = [jnp.max(s, axis=0, keepdims=True) for s in scores]
            exps = [jnp.exp2((s - top) * (SCALE * LOG2E)) for s, top in zip(scores, tops)]
            totals = [1.0 / jnp.sum(e, axis=0, keepdims=True) for e in exps]
            contents = [e * total for e, total in zip(exps, totals)]
            for kind, content in zip(kinds, contents):
                kind[2][h, kind[3]] = content.astype(BF16)
            mixtures = [
                kind[6]((1.0 - sig) * content + kind[1][h]).astype(BF16)
                for kind, content in zip(kinds, contents)
            ]
            for w, kind, mixture in zip(group, kinds, mixtures):
                v = qkv[w, head_rows(2, h), : kind[0]]
                att_t[w, head_rows(0, h), :] = dot(v, mixture).astype(BF16)
        return carry

    lax.fori_loop(0, HEADS, forward_head, 0)
    if stop == 3:
        return

    att_s[...] = jnp.zeros(att_s.shape, F32)
    for w in range(windows):
        att_s[:, window_lanes(w)] += from_grid(att_t[w], w)

    loads[7].wait()
    def norm_two(at, count):
        values = dot(w_t[3], att_s[:, at].astype(BF16))
        middle = x_s[:, at].astype(F32) + values + spread(PBIAS, count)
        mid_s[:, at] = middle
        scaled, _ = norm_columns(middle)
        n2_s[:D, at] = (scaled * spread(GAIN2, count) + spread(BIAS2, count)).astype(BF16)
        rounded = cot_s[:, at].astype(BF16)
        cb_s[:D, at] = rounded
        gather_up(3, rounded.astype(F32))
        att_s[:, at] = middle + spread(FBIAS2, count)

    for_blocks(norm_two)
    gm_s[...] = jnp.zeros(gm_s.shape, F32)
    if not plan.solo and plan.own_first < 2:
        pass_weights()
        wait_weights()
    n2_s[D:, :] = jnp.where(iota((16, rows), 0) == 0, 1.0, 0.0).astype(BF16)
    cb_s[D:, :] = jnp.zeros((16, rows), BF16)
    if stop == 4:
        return

    spans = [(low, min(CHUNK, rows - low)) for low in range(0, rows, CHUNK)]

    def activate(s, slot):
        cs = pl.ds(pl.multiple_of(s * CHUNK, CHUNK), CHUNK)
        up = jnp.transpose(fc_s[0, :, cs])
        down = jnp.transpose(fc_s[1, :, cs])
        for low, count in spans:
            at = pl.ds(low, count)
            before = dot(up, n2_s[:, at])
            dh = dot(down, cb_s[:, at])
            active, slope = gelu_parts(before)
            hid[slot, :, at] = active.astype(BF16)
            dbef[slot, :, at] = (dh * slope).astype(BF16)

    def consume(s, slot):
        cs = pl.ds(pl.multiple_of(s * CHUNK, CHUNK), CHUNK)
        for kind, left, right in ((0, n2_s, dbef), (1, cb_s, hid)):
            grad = dot(left[...], right[slot], NT).astype(BF16)
            for half in range(2):
                blocks = grad[:, half * LANES : half * LANES + LANES]
                mlp_part[kind, s, half] = blocks.reshape((plan.tile_rows,) + TILE)
        for low, count in spans:
            at = pl.ds(low, count)
            att_s[:, at] += dot(fc_s[1, :D, cs], hid[slot, :, at])
            gm_s[:, at] += dot(fc_s[0, :D, cs], dbef[slot, :, at])

    first_core = links.take(plan.steps)
    first_pair = links.take(plan.steps)
    first_tensor = links.take((plan.tensor - 1) * plan.tiles)
    timeline = Timeline()

    def core_copy(s):
        return links.copy(mlp_part.at[1 - core, s], mlp_core.at[s], first_core + s, other_core)

    rows_here = pl.ds(links.pair * plan.pair_rows, plan.pair_rows)
    rows_there = pl.ds((1 - links.pair) * plan.pair_rows, plan.pair_rows)
    other_pair = (links.d + 2 - 4 * links.pair, t)

    def pair_copy(s):
        source = mlp_part.at[core, s, :, rows_there]
        return links.copy(source, mlp_pair.at[s], first_pair + s, other_pair)

    def tensor_copy(s, half, tile, turn):
        to = lax.rem(t + 1 + turn, plan.tensor)
        return (
            mlp_part.at[core, s, half, rows_here],
            mlp_tensor.at[turn, tile],
            first_tensor + turn * plan.tiles + tile,
            (links.d, to),
        )

    def core_sum(s):
        links.copy(mlp_core.at[s], mlp_core.at[s], first_core + s, other_core).wait_recv()
        total = mlp_part[core, s].astype(F32) + mlp_core[s].astype(F32)
        mlp_part[core, s] = total.astype(BF16)
        pair_copy(s).start()

    def pair_sum(s):
        links.copy(mlp_pair.at[s], mlp_pair.at[s], first_pair + s, other_pair).wait_recv()
        total = mlp_part[core, s, :, rows_here].astype(F32) + mlp_pair[s].astype(F32)
        mlp_part[core, s, :, rows_here] = total.astype(BF16)
        kind, j, turn = plan.roles[s]
        if kind == "main" and turn < plan.tensor - 1:
            for half in range(2):
                links.copy(*tensor_copy(s, half, 2 * j + half, turn)).start()
        if kind == "tail" and plan.tensor > 1:
            for half in range(2):
                turn = lax.rem(2 * j + half - t - 1 + plan.tensor, plan.tensor)

                def send(turn=turn, half=half):
                    links.copy(*tensor_copy(s, half, plan.tiles - 1, turn)).start()

                pl.when(turn < plan.tensor - 1)(send)

    def collect(number):
        start = sum(plan.piece_blocks[:number]) // plan.pairs
        for at, tile in enumerate(plan.pieces[number]):
            for turn in range(plan.tensor - 1):
                ref = mlp_tensor.at[turn, tile]
                source = lax.rem(t - turn - 1 + plan.tensor, plan.tensor)
                links.copy(
                    ref, ref, first_tensor + turn * plan.tiles + tile, (links.d, source)
                ).wait_recv()
            if tile < 2 * plan.mains:
                step, half = plan.own_step[tile // 2], tile % 2
            else:
                step, half = plan.first_tail + t // 2, t % 2
            total = mlp_part[core, step, half, rows_here].astype(F32)
            for turn in range(plan.tensor - 1):
                total += mlp_tensor[turn, tile].astype(F32)
            low = start + at * plan.pair_rows
            mlp_sum[low : low + plan.pair_rows] = total.astype(BF16)
        low = start + len(plan.pieces[number]) * plan.pair_rows
        high = start + plan.piece_blocks[number] // plan.pairs
        if low < high:
            mlp_sum[low:high] = jnp.zeros((high - low,) + TILE, BF16)

    mlp_sums = []
    for number, size in enumerate(plan.piece_blocks):
        start = sum(plan.piece_blocks[:number])
        share = pl.ds(start // plan.pairs, size // plan.pairs)
        mlp_sums.append(
            Reduction(
                links,
                mlp_sum.at[share],
                size // plan.pairs,
                mlp_arrived.at[share],
                mlp_full,
                start,
                ("quad",),
                ("quad", "pair", "core"),
                held=(("pair", size // plan.pairs), ("core", plan.mlp_blocks)),
            )
        )
    summed = {}
    begun = set()

    def needed(number):
        tail = any(tile >= 2 * plan.mains for tile in plan.pieces[number])
        return [
            s
            for s, (kind, j, turn) in enumerate(plan.roles)
            if (kind == "tail" and tail) or (kind == "main" and 2 * j in plan.pieces[number])
        ]

    def step_done(s, now):
        summed[s] = now
        for number in range(len(plan.pieces)):
            steps = needed(number)
            if number in begun or any(step not in summed for step in steps):
                continue
            begun.add(number)
            sent = [
                summed[step]
                for step in steps
                if plan.roles[step][0] == "tail" or plan.roles[step][2] < plan.tensor - 1
            ]
            timeline.add(
                max([now] + [at + SENT for at in sent]),
                mlp_sums[number].actions(functools.partial(collect, number), MLP_PACES[number]),
                f"mlp{number}",
            )

    def begin_step(s, now):
        timeline.add(
            now,
            [
                (lambda: core_copy(s).start(), DELAYS["core"], None),
                (lambda: core_sum(s), DELAYS["pair"], None),
                (lambda: pair_sum(s), 0.0, functools.partial(step_done, s)),
            ],
            f"step{s}",
        )

    activate(0, 0)
    if not plan.solo and plan.own_first >= 2:
        pass_weights()

    def mlp_step(s, carry):
        consume(s - 1, (s - 1) % 2)
        activate(s, s % 2)
        if not plan.solo:
            if plan.own_first >= 2:
                pl.when(s == plan.own_first - 1)(wait_weights)
            for k in range(1, plan.steps):
                begin_step(k - 1, MLP_STEP * k)
                timeline.point(MLP_STEP * k, s == k)
        return carry

    lax.fori_loop(1, plan.steps, mlp_step, 0)
    last = plan.steps - 1
    consume(last, last % 2)
    now = MLP_STEP * plan.steps
    if not plan.solo:
        begin_step(last, now)
        timeline.point(now)
    if stop == 5:
        return

    def norm_two_back(at, count):
        n2_s[:D, at] = att_s[:, at].astype(BF16)
        grad = gm_s[:, at]
        scaled, inverse = norm_columns(mid_s[:, at])
        back = norm_back(grad, scaled, inverse, spread(GAIN2, count))
        grad_middle = cot_s[:, at] + back
        cot_s[:, at] = grad_middle
        branch = grad_middle.astype(BF16)
        norm_s[:, at] = branch
        gather_up(0, grad * scaled)
        gather_up(1, grad)
        gather_up(2, branch.astype(F32))

    for_blocks(norm_two_back, now, NORM_TIME)
    store_out = local(n2_s.at[pl.ds(0, D)], out_ref, 8)
    store_out.start()

    now += NORM_TIME

    wide = pl.ds(round_up(D, LANES), D)
    for w in range(windows):
        gcan[w] = to_grid(w)
        timeline.point(now + GRID_TIME * (w + 1))
    now += GRID_TIME * windows
    gm_s[:, wide] = sum(dot(att_t[w], gcan[w], NT) for w in range(windows))

    def project_back(w, carry):
        att_t[w] = dot(w_s[3], gcan[w]).astype(BF16)
        for k in range(windows):
            timeline.point(now + PROJECT_TIME * (k + 1), w == k)
        return carry

    lax.fori_loop(0, windows, project_back, 0)
    now += PROJECT_TIME * windows
    if stop == 6:
        return

    def att_blocks_at(number, at, count):
        return pl.ds(number * plan.att_blocks + at, count)

    def att_start(number, total):
        gm_s[:, :D] = total
        for tile in range(plan.width_tiles):
            blocks = gm_s[:, tile * LANES : tile * LANES + LANES].astype(BF16)
            at = att_blocks_at(number, tile * (D // 16), D // 16)
            att_part[at] = blocks.reshape((D // 16,) + TILE)
        edge = gm_s[:, plan.width_tiles * LANES : plan.width_tiles * LANES + LANES]
        low = D - plan.fold
        lane = iota((low, LANES), 1)
        folded = jnp.where(
            lane < plan.left_over, edge[:low], pltpu.roll(edge[plan.fold :], plan.left_over, 1)
        )
        folded = jnp.concatenate([folded, edge[low : plan.fold]], axis=0).astype(BF16)
        at = att_blocks_at(number, plan.full_blocks, plan.fold // 16)
        att_part[at] = folded.reshape((plan.fold // 16,) + TILE)
        used = plan.full_blocks + plan.fold // 16
        at = att_blocks_at(number, used, 1)
        att_part[at] = small_s[16:, :].astype(BF16).reshape((1,) + TILE)
        if plan.att_blocks > used + 1:
            spare = plan.att_blocks - used - 1
            at = att_blocks_at(number, used + 1, spare)
            att_part[at] = jnp.zeros((spare,) + TILE, BF16)

    def vector_sums(numbers, row):
        for place, number in enumerate(numbers):
            for tile in range(round_up(D, LANES) // LANES):
                turned = jnp.transpose(acc[number, tile * LANES : tile * LANES + LANES, :])
                at = row + 4 * place + tile
                small_s[at : at + 1, :] = jnp.sum(turned, axis=0, keepdims=True)

    direct = plan.direct
    routes = [(("core", "pair", "quad"), ("quad", "pair", "core"), "tensor")] * len(BUNDLES)
    if direct:
        routes = [(("core", "cross", "quad"), ("quad", "cross", "core"))] * (len(BUNDLES) - 1)
        routes.append((("core", "all"), ("all", "core")))
    att_sums = []
    for bundle, route in zip(BUNDLES, routes):
        start, size = bundle[0] * plan.att_blocks, len(bundle) * plan.att_blocks
        arrived = pl.ds(bundle[0] * plan.att_arrived, len(bundle) * plan.att_arrived)
        att_sums.append(
            Reduction(
                links,
                att_part.at[pl.ds(start, size)],
                size,
                att_arrived.at[arrived],
                att_full,
                start,
                *route,
            )
        )

    def begin_att(number, now):
        for at, bundle in enumerate(BUNDLES):
            if bundle[-1] == number:
                timeline.add(now, att_sums[at].actions(pace=ATT_PACES[at]), f"att{at}")

    vector_sums(range(4), 16)
    att_start(0, gm_s[:, wide])
    if not plan.solo:
        begin_att(0, now)
        timeline.point(now)

    def weight_grad(g):
        def joined(w):
            parts = [
                qkv[w, pl.ds(pl.multiple_of(part * D + g * (D // GROUPS), 16), D // GROUPS), :]
                for part in range(3)
            ]
            return jnp.concatenate(parts, axis=0)

        total = dot(ncan[0], joined(0), NT)
        for w in range(1, windows):
            total += dot(ncan[w], joined(w), NT)
        att_start(1 + g, total)

    window_groups = [range(windows)]

    def backward_head(h, carry):
        sig = 1.0 / (1.0 + jnp.exp(-jnp.full((1, TOK), gate_ref[0, h], F32)))
        keep = 1.0 - sig
        factor = keep * SCALE
        sums = [0.0, 0.0]
        gate_row = jnp.zeros((1, TOK), F32)
        for group in window_groups:
            kinds = [window_kind(w) for w in group]
            queries = [qkv[w, head_rows(0, h), :] for w in group]
            keys = [qkv[w, head_rows(1, h), : kind[0]] for w, kind in zip(group, kinds)]
            vals = [qkv[w, head_rows(2, h), : kind[0]] for w, kind in zip(group, kinds)]
            grads = [att_t[w, head_rows(0, h), :] for w in group]
            contents = [kind[2][h, kind[3]].astype(F32) for kind in kinds]
            grad_mixes = [
                kind[5](dot(v, da, TN)) for kind, v, da in zip(kinds, vals, grads)
            ]
            mixtures = [
                kind[6](keep * content + kind[1][h]).astype(BF16)
                for kind, content in zip(kinds, contents)
            ]
            grad_vals = [dot(da, mixture, NT) for da, mixture in zip(grads, mixtures)]
            rows_sum = [
                jnp.sum(content * grad_mix, axis=0, keepdims=True)
                for content, grad_mix in zip(contents, grad_mixes)
            ]
            grad_scores = [
                kind[6](content * (grad_mix - row)).astype(BF16)
                for kind, content, grad_mix, row in zip(kinds, contents, grad_mixes, rows_sum)
            ]
            for w, grad_mix, row in zip(group, grad_mixes, rows_sum):
                sums[w % 3 // 2] += grad_mix
                gate_row -= row
            grad_queries = [dot(k, grad_s) for k, grad_s in zip(keys, grad_scores)]
            grad_keys = [dot(q, grad_s, NT) for q, grad_s in zip(queries, grad_scores)]
            for w, kind, dq, dk, dv in zip(group, kinds, grad_queries, grad_keys, grad_vals):
                qkv[w, head_rows(0, h), :] = (dq * factor).astype(BF16)
                qkv[w, head_rows(1, h), : kind[0]] = (dk * factor[:, : kind[0]]).astype(BF16)
                qkv[w, head_rows(2, h), : kind[0]] = dv.astype(BF16)
        results = [jnp.zeros((1, TOK), F32)] * 3
        for big, pos, grad_mix in ((True, pos_b, sums[0]), (False, pos_s, sums[1])):
            col_off, row_off, dist, _ = offsets(big)
            row = jnp.sum(pos[h] * grad_mix, axis=0, keepdims=True) / sig
            grad_l = pos[h] * (grad_mix - row)
            gate_row += row
            results = [
                old + jnp.sum(grad_l * off, axis=0, keepdims=True)
                for old, off in zip(results, (col_off, row_off, dist))
            ]
        results = jnp.concatenate(results + [gate_row * sig * keep], axis=0)
        column = jnp.sum(results, axis=1, keepdims=True)
        lane = iota((4, LANES), 1)
        small_s[8:12, :] += jnp.where(lane == h, column, 0.0)
        pl.when(h % (HEADS // GROUPS) == HEADS // GROUPS - 1)(
            lambda: weight_grad(h // (HEADS // GROUPS))
        )
        if not plan.solo:
            for k in range(HEADS):
                time = now + HEAD_TIME * (k + 1) + GRADIENT_TIME * ((k + 1) // (HEADS // GROUPS))
                if k % (HEADS // GROUPS) == HEADS // GROUPS - 1:
                    begin_att(1 + k // (HEADS // GROUPS), time)
                timeline.point(time, h == k)
        return carry

    lax.fori_loop(0, HEADS, backward_head, 0)
    now += HEAD_TIME * HEADS + GRADIENT_TIME * GROUPS
    if stop == 7:
        return

    att_s[...] = jnp.zeros(att_s.shape, F32)

    for first in range(0, windows, TOGETHER):
        group = range(first, min(first + TOGETHER, windows))
        grads = [dot(w_s[0], qkv[w, :D, :]) for w in group]
        grads = [grad + dot(w_s[1], qkv[w, D : 2 * D, :]) for grad, w in zip(grads, group)]
        grads = [grad + dot(w_s[2], qkv[w, 2 * D :, :]) for grad, w in zip(grads, group)]
        highs = [grad.astype(BF16) for grad in grads]
        lows = [(grad - high.astype(F32)).astype(BF16) for grad, high in zip(grads, highs)]
        for w, high, low in zip(group, highs, lows):
            att_s[:, window_lanes(w)] += from_grid(high, w) + from_grid(low, w)
        timeline.point(now + WINDOW_TIME * (group[-1] + 1))
    now += WINDOW_TIME * windows

    def norm_one_back(at, count):
        scaled, inverse = norm_columns(x_s[:, at].astype(F32))
        grad = att_s[:, at]
        cot_s[:, at] += norm_back(grad, scaled, inverse, spread(GAIN1, count))
        gather_up(4, grad * scaled)
        gather_up(5, grad)

    for_blocks(norm_one_back, now, NORM_TIME)
    store_gi = local(cot_s, gi_ref, 9)
    store_gi.start()
    vector_sums((4, 5), 0)

    now += NORM_TIME
    small_places = {}

    def small_begin(name):
        size, me, peer = links.group(name)
        first = links.take(size - 1)
        used = sum(size for size, _ in small_places.values())
        small_places[name] = size, first
        small_arrived[used + me] = small_s[:SMALL_ROWS, :]

        def make(step):
            slot = small_arrived.at[used + me]
            return slot, slot, first + step - 1, peer(lax.rem(me + step, size))

        for step in range(1, size):
            links.put(functools.partial(make, step))

    def small_end(name):
        size, me, peer = links.group(name)
        _, first = small_places[name]
        used = sum(size for size, _ in small_places.values()) - size
        for step in range(1, size):
            source = lax.rem(me + size - step, size)
            ref = small_arrived.at[used + source]
            links.copy(ref, ref, first + step - 1, peer(source)).wait_recv()
        total = small_arrived[used]
        for other in range(1, size):
            total += small_arrived[used + other]
        small_s[:SMALL_ROWS, :] = total

    names = ("core", "all") if direct else ("core", "tensor", "pair", "quad")
    names = [name for name in names if links.group(name)[0] > 1]
    if names:
        actions = [(functools.partial(small_begin, names[0]), DELAYS[names[0]], None)]
        for before, name in zip(names, names[1:]):

            def turn(before=before, name=name):
                small_end(before)
                small_begin(name)

            actions.append((turn, DELAYS[name], None))
        actions.append((functools.partial(small_end, names[-1]), 0.0, None))
        timeline.add(now, actions, "small")
    timeline.finish(now)
    small_ref[...] = small_s[:SMALL_ROWS, :]
    stores = [local(mlp_full, mlp_ref, 10), local(att_full, att_ref, 11)]
    for store in stores:
        store.start()
    store_out.wait()
    store_gi.wait()
    if not plan.solo:
        for s in range(plan.steps):
            core_copy(s).wait_send()
            pair_copy(s).wait_send()
        for s, (kind, j, turn) in enumerate(plan.roles):
            if kind == "main" and turn < plan.tensor - 1:
                for half in range(2):
                    links.copy(*tensor_copy(s, half, 2 * j + half, turn)).wait_send()
        if plan.tails:
            for turn in range(plan.tensor - 1):
                owner = lax.rem(t + 1 + turn, plan.tensor)
                links.copy(
                    *tensor_copy(plan.first_tail + owner // 2, owner % 2, plan.tiles - 1, turn)
                ).wait_send()
    links.drain()
    for store in stores:
        store.wait()


def finish_kernel(
    plan,
    out_in,
    gi_in,
    mlp_in,
    att_in,
    small_in,
    out_ref,
    gi_ref,
    dq_ref,
    dk_ref,
    dv_ref,
    dproj_ref,
    dfc1_ref,
    dfc2_ref,
    dfb1_ref,
    pos_ref,
    gate_ref,
    *refs
):
    vector_refs, (mlp_s, att_s, square_s, wide_s, out_s, gi_s, sems) = refs[:6], refs[6:]
    D = plan.width
    def copy(source, target, number):
        return pltpu.make_async_copy(source, target, sems.at[number])

    size = plan.mlp_blocks
    loads = [copy(mlp_in.at[pl.ds(kind * size, size)], mlp_s.at[kind], kind) for kind in range(2)]
    loads.append(copy(att_in, att_s, 2))
    third = D // 3
    spans = [pl.ds(k * third, third) for k in range(3)]
    through = [(out_in, out_s, out_ref), (gi_in, gi_s, gi_ref)]
    arrive = [
        copy(source.at[span], held.at[span], 3 + 3 * at + k)
        for at, (source, held, _) in enumerate(through)
        for k, span in enumerate(spans)
    ]
    leave = [
        copy(held.at[span], target.at[span], 9 + 3 * at + k)
        for at, (_, held, target) in enumerate(through)
        for k, span in enumerate(spans)
    ]
    for item in loads + arrive:
        item.start()
    stores = []

    def store(source, target):
        stores.append(copy(source, target, 15 + len(stores)))
        stores[-1].start()

    where = {
        tile: (sum(plan.piece_blocks[:number]), plan.piece_blocks[number], at)
        for number, piece in enumerate(plan.pieces)
        for at, tile in enumerate(piece)
    }
    for kind, target in enumerate((dfc1_ref, dfc2_ref)):
        loads[kind].wait()
        for pair in range(plan.pairs):
            top = pair * plan.pair_rows * 16
            bottom = min(D, top + plan.pair_rows * 16)
            for tile in range(plan.tiles):
                start, count, at = where[tile]
                first = start + pair * (count // plan.pairs) + at * plan.pair_rows
                values = mlp_s[kind, first : first + plan.pair_rows]
                values = values.reshape(plan.pair_rows * 16, LANES).astype(F32)
                low, high = tile * LANES, min(plan.share, tile * LANES + LANES)
                wide_s[kind, top:bottom, low:high] = values[: bottom - top, : high - low]
                if kind == 0 and pair == plan.pairs - 1:
                    bias = values[D - top : D - top + 1, : high - low]
                    dfb1_ref[low:high] = bias.reshape(high - low)
            span = pl.ds(top, bottom - top)
            store(wide_s.at[kind, span], target.at[span])
        if kind == 0:
            for item, onward in zip(arrive, leave):
                item.wait()
                onward.start()
    loads[2].wait()
    below = D - plan.fold
    part = D // GROUPS
    for number in range(GROUPS + 1):
        first = number * plan.att_blocks
        tiles = [
            att_s[pl.ds(first + tile * (D // 16), D // 16)].reshape(D, LANES).astype(F32)
            for tile in range(plan.width_tiles)
        ]
        folded = att_s[pl.ds(first + plan.full_blocks, plan.fold // 16)]
        folded = folded.reshape(plan.fold, LANES).astype(F32)
        lower = pltpu.roll(folded, LANES - plan.left_over, 1)[:below]
        edge = jnp.concatenate([folded, lower], axis=0)[:, : plan.left_over]
        total = jnp.concatenate(tiles + [edge], axis=1)
        if number == 0:
            square_s[0] = total
            store(square_s.at[0], dproj_ref)
        else:
            to = (number - 1) * part
            for place in range(3):
                square_s[1 + place, :, to : to + part] = total[:, place * part : place * part + part]
    for place, target in enumerate((dq_ref, dk_ref, dv_ref)):
        store(square_s.at[1 + place], target)
    early = att_s[plan.full_blocks + plan.fold // 16].astype(F32)
    for number, target in enumerate(vector_refs):
        for tile in range(round_up(D, LANES) // LANES):
            low, high = tile * LANES, min(D, tile * LANES + LANES)
            row = number % 4 * 4 + tile
            source = early if number < 4 else small_in[...]
            target[:, low:high] = source[row : row + 1, : high - low]
    pos_ref[...] = small_in[8:11, :HEADS]
    gate_ref[...] = small_in[11:12, :HEADS].reshape(HEADS)
    for item in stores + leave:
        item.wait()


def local(
    stop,
    dp,
    tensor,
    inputs,
    patch_cells,
    ln1_gain,
    ln1_bias,
    w_query,
    w_key,
    w_value,
    w_proj,
    proj_bias,
    pos_weight,
    gate_param,
    ln2_gain,
    ln2_bias,
    fc1_weight,
    fc1_bias,
    fc2_weight,
    fc2_bias,
    cotangent,
):
    rows, D = inputs.shape
    share = fc1_weight.shape[1]
    plan = Plan(dp, tensor, rows, D, share)
    windows, lanes, steps = plan.windows, plan.lanes, plan.steps

    def vector(values):
        return values.reshape(1, -1)

    vmem = pl.BlockSpec(memory_space=pltpu.VMEM)
    smem = pl.BlockSpec(memory_space=pltpu.SMEM)
    anywhere = pl.BlockSpec(memory_space=pl.ANY)
    params = {} if plan.solo else {"collective_id": 0, "has_side_effects": True}
    slots = plan.cores + plan.tensor + plan.pairs + plan.quads
    if plan.direct:
        slots = plan.cores + tensor * dp // plan.cores
    out, gi, mlp, att, small = pl.pallas_call(
        functools.partial(block_kernel, stop, plan),
        out_shape=(
            jax.ShapeDtypeStruct((D, rows), BF16),
            jax.ShapeDtypeStruct((D, rows), F32),
            jax.ShapeDtypeStruct((2 * plan.mlp_blocks,) + TILE, BF16),
            jax.ShapeDtypeStruct(((GROUPS + 1) * plan.att_blocks,) + TILE, BF16),
            jax.ShapeDtypeStruct((SMALL_ROWS, LANES), F32),
        ),
        in_specs=[anywhere, vmem] + [anywhere] * 6 + [vmem] + [anywhere] + [vmem] * 6 + [smem] * 2,
        out_specs=(anywhere, anywhere, anywhere, anywhere, vmem),
        scratch_shapes=[
            pltpu.VMEM((D, rows), BF16),
            pltpu.VMEM((D, rows), F32),
            pltpu.VMEM((4, D, D), BF16),
            pltpu.VMEM((4, D, D), BF16),
            pltpu.VMEM((2, D, share), BF16),
            pltpu.VMEM((2, plan.tall, plan.hidden), BF16),
            pltpu.VMEM((6, D, LANES), F32),
            pltpu.VMEM((1, lanes), jnp.int32),
            pltpu.VMEM((windows, TOK, WIDE), BF16),
            pltpu.VMEM((D, lanes), BF16),
            pltpu.VMEM((windows, D, TOK), BF16),
            pltpu.VMEM((windows, 3 * D, TOK), BF16),
            pltpu.VMEM((windows, D, TOK), BF16),
            pltpu.VMEM((windows, D, TOK), BF16),
            pltpu.VMEM((HEADS, KEYS_BIG, TOK), F32),
            pltpu.VMEM((HEADS, STRIDE, TOK), F32),
            pltpu.VMEM((HEADS, BIG_CROPS * plan.images, KEYS_BIG, TOK), BF16),
            pltpu.VMEM((HEADS, plan.images, STRIDE, TOK), BF16),
            pltpu.VMEM((D, lanes), F32),
            pltpu.VMEM((D, lanes), F32),
            pltpu.VMEM((plan.tall, rows), BF16),
            pltpu.VMEM((plan.tall, rows), BF16),
            pltpu.VMEM((2, CHUNK, rows), BF16),
            pltpu.VMEM((2, CHUNK, rows), BF16),
            pltpu.VMEM((D, lanes), F32),
            pltpu.VMEM((6, round_up(D, LANES), LANES), F32),
            pltpu.VMEM((2, steps, 2, plan.tile_rows) + TILE, BF16),
            pltpu.VMEM((steps, 2, plan.tile_rows) + TILE, BF16),
            pltpu.VMEM((steps, 2, plan.pair_rows) + TILE, BF16),
            pltpu.VMEM((max(1, tensor - 1), plan.tiles, plan.pair_rows) + TILE, BF16),
            pltpu.VMEM((plan.mlp_blocks // plan.pairs,) + TILE, BF16),
            pltpu.VMEM((plan.mlp_blocks // plan.pairs,) + TILE, BF16),
            pltpu.VMEM(((GROUPS + 1) * plan.att_blocks,) + TILE, BF16),
            pltpu.VMEM(((GROUPS + 1) * plan.att_arrived,) + TILE, BF16),
            pltpu.VMEM((2 * plan.mlp_blocks,) + TILE, BF16),
            pltpu.VMEM(((GROUPS + 1) * plan.att_blocks,) + TILE, BF16),
            pltpu.VMEM((2 * SMALL_ROWS, LANES), F32),
            pltpu.VMEM((slots, SMALL_ROWS, LANES), F32),
            pltpu.SemaphoreType.DMA((12,)),
            pltpu.SemaphoreType.DMA((plan.semaphores,)),
            pltpu.SemaphoreType.DMA((plan.semaphores,)),
        ],
        compiler_params=pltpu.CompilerParams(vmem_limit_bytes=63 * 1024 * 1024, **params),
    )(
        inputs.T,
        patch_cells,
        cotangent.T,
        w_query,
        w_key,
        w_value,
        w_proj,
        fc1_weight,
        fc1_bias,
        fc2_weight.T,
        vector(ln1_gain),
        vector(ln1_bias),
        vector(proj_bias),
        vector(ln2_gain),
        vector(ln2_bias),
        vector(fc2_bias),
        pos_weight,
        vector(gate_param),
    )
    square = jax.ShapeDtypeStruct((D, D), F32)
    wide = jax.ShapeDtypeStruct((D, share), F32)
    results = pl.pallas_call(
        functools.partial(finish_kernel, plan),
        out_shape=(
            jax.ShapeDtypeStruct((D, rows), BF16),
            jax.ShapeDtypeStruct((D, rows), F32),
        )
        + (square,) * 4
        + (wide,) * 2
        + (
            jax.ShapeDtypeStruct((share,), F32),
            jax.ShapeDtypeStruct((3, HEADS), F32),
            jax.ShapeDtypeStruct((HEADS,), F32),
        )
        + (jax.ShapeDtypeStruct((1, D), F32),) * 6,
        in_specs=[anywhere] * 4 + [vmem],
        out_specs=(anywhere,) * 8 + (vmem,) * 9,
        scratch_shapes=[
            pltpu.VMEM((2, plan.mlp_blocks) + TILE, BF16),
            pltpu.VMEM(((GROUPS + 1) * plan.att_blocks,) + TILE, BF16),
            pltpu.VMEM((4, D, D), F32),
            pltpu.VMEM((2, D, share), F32),
            pltpu.VMEM((D, rows), BF16),
            pltpu.VMEM((D, rows), F32),
            pltpu.SemaphoreType.DMA((23,)),
        ],
        compiler_params=pltpu.CompilerParams(vmem_limit_bytes=63 * 1024 * 1024),
    )(out, gi, mlp, att, small)
    out, gi, dq, dk, dv, dproj, dfc1, dfc2, dfb1, pos, gate = results[:11]
    gain2, bias2, pbias, fbias2, gain1, bias1 = (item.reshape(D) for item in results[11:])
    return (
        out.T,
        gi.T,
        gain1,
        bias1,
        dq,
        dk,
        dv,
        dproj,
        pbias,
        pos,
        gate,
        gain2,
        bias2,
        dfc1,
        dfb1,
        dfc2.T,
        fbias2,
    )


def solution(mesh, stop=0):
    both = ("dp", "tensor")
    copied = P()
    in_specs = (
        (P(both, None), P(both))
        + (copied,) * 11
        + (P(None, "tensor"), P("tensor"), P("tensor", None), copied, P(both, None))
    )
    out_specs = (
        (P(both, None), P(both, None))
        + (copied,) * 11
        + (P(None, "tensor"), P("tensor"), P("tensor", None), copied)
    )
    return jax.shard_map(
        functools.partial(local, stop, mesh.shape["dp"], mesh.shape["tensor"]),
        mesh=mesh,
        in_specs=in_specs,
        out_specs=out_specs,
        check_vma=False,
    )
```

```python
import functools

import jax
import jax.numpy as jnp
from jax import lax
from jax.experimental import pallas as pl
from jax.experimental.pallas import tpu as pltpu
from jax.sharding import PartitionSpec as P

MESH = pl.DeviceIdType.MESH

MLP_STEP = 2.3
NORM_TIME = 3.2
GRID_TIME = 0.2
PROJECT_TIME = 0.4
HEAD_TIME = 1.1
GRADIENT_TIME = 1.0
WINDOW_TIME = 1.15
SENT = 5.5
MLP_PACES = (1.2, 1.4, 1.4)
ATT_PACES = (0.9, 0.9, 0.9, 0.9)
BUNDLES = ((0,), (1,), (2,), (3,))

HEADS = 9
HEAD_DIM = 48
BIG_SIDE = 14
SMALL_SIDE = 6
BIG_CROPS = 2
SMALL_CROPS = 6
PER_IMAGE = 608
BIG = BIG_SIDE * BIG_SIDE
SMALL = SMALL_SIDE * SMALL_SIDE
GROUPS = 3

EPS = 1e-06
F32 = jnp.float32
BF16 = jnp.bfloat16
LOG2E = 1.4426950408889634
SCALE = HEAD_DIM ** (-0.5)
FAR = -1e30

NN = (((1,), (0,)), ((), ()))
NT = (((1,), (1,)), ((), ()))
TN = (((0,), (0,)), ((), ()))

LANES = 128
TOK = 256
KEYS_BIG = 208
STRIDE = 40
KEYS_SMALL = SMALL_CROPS * STRIDE
WIDE = 384
CHUNK = 256
BLOCK = 256
TILE = (16, LANES)
SMALL_ROWS = 16
TOGETHER = 3


def dot(left, right, dims=NN):
    return lax.dot_general(left, right, dims, preferred_element_type=F32)


def round_up(count, unit):
    return (count + unit - 1) // unit * unit


def iota(shape, dim):
    return lax.broadcasted_iota(jnp.int32, shape, dim)


def lane_crop():
    token = iota((1, TOK), 1).astype(F32)
    return jnp.floor((token + 0.5) * (1.0 / STRIDE))


def grid_place(cell, side):
    row = jnp.floor((cell + 0.5) * (1.0 / side))
    return row, cell - side * row


def offsets(big):
    keys = KEYS_BIG if big else STRIDE
    side = BIG_SIDE if big else SMALL_SIDE
    key = iota((keys, TOK), 0).astype(F32)
    query = iota((keys, TOK), 1).astype(F32)
    if not big:
        query = query - STRIDE * lane_crop()
    row_j, col_j = grid_place(key, side)
    row_i, col_i = grid_place(query, side)
    col_off = col_j - col_i
    row_off = row_j - row_i
    return col_off, row_off, col_off * col_off + row_off * row_off, key < side * side


def extra_rows(big):
    feature = iota((16, TOK), 0)
    cell = iota((1, TOK), 1).astype(F32)
    if not big:
        cell = cell - STRIDE * lane_crop()
    query = jnp.where(feature == 0, 1.0, 0.0)
    key = jnp.where((feature == 0) & (cell > (BIG if big else SMALL) - 0.5), FAR, 0.0)
    return query.astype(BF16), key.astype(BF16)


def own_crop(full):
    crop = lane_crop()
    result = full[:STRIDE]
    for c in range(1, SMALL_CROPS):
        result = jnp.where(crop == c, full[c * STRIDE : (c + 1) * STRIDE], result)
    return result


def all_crops(own):
    crop = lane_crop()
    return jnp.concatenate([jnp.where(crop == c, own, 0.0) for c in range(SMALL_CROPS)], axis=0)


def whole(values):
    return values


def gelu_parts(before):
    cdf = 0.5 * (1.0 + lax.erf(before * 0.7071067811865476))
    density = jnp.exp(-0.5 * before * before) * 0.3989422804014327
    return before * cdf, cdf + before * density


def norm_columns(values):
    center = values - jnp.mean(values, axis=0, keepdims=True)
    inverse = lax.rsqrt(jnp.mean(center * center, axis=0, keepdims=True) + EPS)
    return center * inverse, inverse


def norm_back(grad_normed, scaled, inverse, gain):
    e = grad_normed * gain
    return inverse * (
        e
        - jnp.mean(e, axis=0, keepdims=True)
        - scaled * jnp.mean(e * scaled, axis=0, keepdims=True)
    )


class Plan:
    def __init__(self, dp, tensor, rows, width, share):
        self.dp, self.tensor = dp, tensor
        self.solo = dp == 1
        self.rows, self.width, self.share = rows, width, share
        self.images = rows // PER_IMAGE
        self.windows = 3 * self.images
        self.lanes = round_up(rows, CHUNK)
        self.padded = round_up(share, LANES)
        self.tiles = self.padded // LANES
        self.mains = self.padded // CHUNK
        self.tails = (self.padded % CHUNK) // LANES * ((tensor + 1) // 2)
        self.own_first = self.mains - 1
        self.roles = []
        self.own_step = []
        if self.mains > 1:
            self.own_step.append(0)
            self.roles.append(("main", 0, tensor - 1))
        self.other_step = []
        for j in range(self.mains):
            if j == self.mains - 1:
                self.first_tail = len(self.roles)
                self.roles += [("tail", m, 0) for m in range(self.tails)]
            self.other_step.append(len(self.roles))
            self.roles += [("main", j, turn) for turn in range(tensor - 1)]
            if j or self.mains == 1:
                self.own_step.append(len(self.roles))
                self.roles.append(("main", j, tensor - 1))
        self.steps = len(self.roles)
        self.hidden = CHUNK * self.steps
        self.tall = width + 16
        self.tile_rows = self.tall // 16
        self.cores = 1 if self.solo else 2
        self.pairs = 1 if self.solo else 2
        self.quads = dp // (self.cores * self.pairs)
        self.direct = tensor * dp // self.cores <= 16
        self.pieces = [[2 * j, 2 * j + 1] for j in range(self.mains)]
        if self.tails:
            self.pieces[-1].append(self.tiles - 1)
        self.pair_rows = self.tile_rows // self.pairs
        self.piece_blocks = [
            self.pairs * round_up(len(piece) * self.pair_rows, self.quads) for piece in self.pieces
        ]
        self.mlp_blocks = sum(self.piece_blocks)
        self.width_tiles = width // LANES
        self.left_over = width % LANES
        self.full_blocks = self.width_tiles * (width // 16)
        self.fold = round_up(width // 2, 16)
        whole = self.full_blocks + self.fold // 16
        self.att_blocks = round_up(whole + 1, self.cores * self.pairs * self.quads)
        piece = self.att_blocks // (self.cores * self.pairs * self.quads)
        self.att_arrived = self.att_blocks + tensor * piece
        around = tensor * dp // self.cores if self.direct else tensor + self.pairs + self.quads
        self.sem_weights = 2 * tensor * (self.mains + 1)
        self.sem_steps = 2 * self.steps + (tensor - 1) * self.tiles
        self.semaphores = (
            self.sem_weights
            + self.sem_steps
            + len(self.pieces) * (2 * (self.pairs + dp // self.cores) + 1)
            + 4 * 2 * (1 + around)
            + 1
            + around
        )


class Timeline:
    def __init__(self):
        self.chains = []

    def add(self, ready, actions, label=""):
        self.chains.append([ready, list(actions), label, 0])

    def due(self, now):
        calls = []
        for chain in list(self.chains):
            if chain[1] and chain[0] <= now:
                call, delay, hook = chain[1].pop(0)
                chain[0] = now + delay
                calls.append((call, f"{chain[2]}_{chain[3]}"))
                chain[3] += 1
                if hook:
                    hook(now)
        return calls

    def point(self, now, condition=None):
        calls = self.due(now)
        if not calls:
            return

        def act():
            for call, _ in calls:
                call()

        if condition is None:
            act()
        else:
            pl.when(condition)(act)

    def finish(self, now):
        while any(chain[1] for chain in self.chains):
            self.point(now)
            now += 1.0


class Links:
    def __init__(self, plan, send, recv):
        self.plan, self.send, self.recv = plan, send, recv
        self.next = 0
        self.started = []
        if plan.solo:
            self.d = self.t = self.core = self.pair = self.quad = self.chip = self.place = self.crossed = 0
        else:
            self.d = lax.axis_index("dp")
            self.t = lax.axis_index("tensor")
            self.core = self.d % 2
            self.pair = (self.d // 2) % 2
            self.quad = self.d // 4
            self.chip = self.d // 2
            self.place = self.chip * plan.tensor + self.t
            self.crossed = self.pair * plan.tensor + self.t

    def take(self, count):
        first = self.next
        self.next += count
        return first

    def group(self, name):
        plan, d, t = self.plan, self.d, self.t
        if name == "core":
            return plan.cores, self.core, lambda k: (d - self.core + k, t)
        if name == "tensor":
            return plan.tensor, t, lambda k: (d, k)
        if name == "pair":
            return plan.pairs, self.pair, lambda k: (d + 2 * (k - self.pair), t)
        if name == "quad":
            return plan.quads, self.quad, lambda k: (d + 4 * (k - self.quad), t)
        if name == "cross":
            return (
                plan.pairs * plan.tensor,
                self.crossed,
                lambda k: (d + 2 * (k // plan.tensor - self.pair), k % plan.tensor),
            )
        count = plan.tensor
        return (
            plan.dp // plan.cores * count,
            self.place,
            lambda k: (2 * (k // count) + self.core, k % count),
        )

    def greet(self):
        if self.plan.solo:
            return
        semaphore = pltpu.get_barrier_semaphore()
        self.greeted = 0
        direct = ("core", "all")
        for name in direct if self.plan.direct else ("core", "tensor", "pair", "quad"):
            size, me, peer = self.group(name)
            for step in range(1, size):
                pl.semaphore_signal(
                    semaphore,
                    inc=1,
                    device_id=peer(lax.rem(me + step, size)),
                    device_id_type=MESH,
                )
                self.greeted += 1

    def await_greetings(self):
        if not self.plan.solo:
            pl.semaphore_wait(pltpu.get_barrier_semaphore(), self.greeted)

    def copy(self, source, target, number, device):
        return pltpu.make_async_remote_copy(
            src_ref=source,
            dst_ref=target,
            send_sem=self.send.at[number],
            recv_sem=self.recv.at[number],
            device_id=device,
            device_id_type=MESH,
        )

    def put(self, make):
        self.copy(*make()).start()
        self.started.append(make)

    def drain(self):
        for make in self.started:
            self.copy(*make()).wait_send()


DELAYS = {"core": 1.5, "pair": 4.5, "quad": 4.5, "tensor": 4.5, "cross": 5.0, "all": 6.5}


class Reduction:
    def __init__(self, links, part, length, arrived, full, full_start, groups, gathers, shared=None, held=()):
        self.links, self.part, self.arrived, self.full = links, part, arrived, full
        self.full_start = full_start
        self.length = length
        self.used = 0
        self.terms = [(name, links.group(name)[1], stride, False) for name, stride in held]
        self.stages = []

        def several(name):
            return name and links.group(name)[0] > 1

        groups = [name for name in groups if several(name)]
        gathers = [name for name in gathers if several(name)]
        for at, name in enumerate(groups):
            last = at == len(groups) - 1 and not several(shared)
            self.stages.append((name, self.scatter, functools.partial(self.add, last=last)))
        if several(shared):
            self.stages.append((shared, self.share, self.shared))
        for name in gathers:
            self.stages.append((name, self.gather, self.gathered))

    def actions(self, before=None, pace=1.0):
        calls = []
        for at in range(len(self.stages) + 1):
            todo = []
            if at == 0 and before:
                todo.append(before)
            if at:
                name, _, end = self.stages[at - 1]
                todo.append(functools.partial(end, name))
            if at < len(self.stages):
                name, start, _ = self.stages[at]
                todo.append(functools.partial(start, name))
                delay = DELAYS[name] * pace
            else:
                delay = 0.0
            calls.append((functools.partial(self.run, todo), delay, None))
        return calls

    @staticmethod
    def run(todo):
        for call in todo:
            call()

    def part_place(self):
        return sum(me * stride for _, me, stride, cut in self.terms if cut)

    def full_place(self, terms):
        return self.full_start + sum(me * stride for _, me, stride, _ in terms)

    def scatter(self, name):
        size, me, peer = self.links.group(name)
        piece = self.length // size
        self.first = first = self.links.take(size - 1)
        terms, used = tuple(self.terms), self.used

        def make(step):
            to = lax.rem(me + step, size)
            offset = sum(who * stride for _, who, stride, cut in terms if cut) + to * piece
            return (
                self.part.at[pl.ds(offset, piece)],
                self.arrived.at[pl.ds(used + (step - 1) * piece, piece)],
                first + step - 1,
                peer(to),
            )

        for step in range(1, size):
            self.links.put(functools.partial(make, step))

    def add(self, name, last):
        size, me, peer = self.links.group(name)
        piece = self.length // size
        self.terms.append((name, me, piece, True))
        mine = pl.ds(self.part_place(), piece)
        total = self.part[mine].astype(F32)
        for step in range(1, size):
            slot = pl.ds(self.used + (step - 1) * piece, piece)
            ref = self.arrived.at[slot]
            self.links.copy(
                ref, ref, self.first + step - 1, peer(lax.rem(me + step, size))
            ).wait_recv()
            total += self.arrived[slot].astype(F32)
        self.used += (size - 1) * piece
        self.length = piece
        if last:
            self.full[pl.ds(self.full_place(self.terms), piece)] = total.astype(BF16)
        else:
            self.part[mine] = total.astype(BF16)

    def share(self, name):
        size, me, peer = self.links.group(name)
        self.first = first = self.links.take(size - 1)
        length, used = self.length, self.used
        self.arrived[pl.ds(used + me * length, length)] = self.part[pl.ds(self.part_place(), length)]

        def make(step):
            ref = self.arrived.at[pl.ds(used + me * length, length)]
            return ref, ref, first + step - 1, peer(lax.rem(me + step, size))

        for step in range(1, size):
            self.links.put(functools.partial(make, step))

    def shared(self, name):
        size, me, peer = self.links.group(name)
        for step in range(1, size):
            source = lax.rem(me + size - step, size)
            ref = self.arrived.at[pl.ds(self.used + source * self.length, self.length)]
            self.links.copy(ref, ref, self.first + step - 1, peer(source)).wait_recv()
        total = self.arrived[pl.ds(self.used, self.length)].astype(F32)
        for other in range(1, size):
            total += self.arrived[pl.ds(self.used + other * self.length, self.length)].astype(F32)
        self.full[pl.ds(self.full_place(self.terms), self.length)] = total.astype(BF16)

    def gather(self, name):
        size, me, peer = self.links.group(name)
        self.first = first = self.links.take(size - 1)
        terms, length = tuple(self.terms), self.length

        def make(step):
            mine = self.full.at[pl.ds(self.full_place(terms), length)]
            return mine, mine, first + step - 1, peer(lax.rem(me + step, size))

        for step in range(1, size):
            self.links.put(functools.partial(make, step))

    def gathered(self, name):
        size, me, peer = self.links.group(name)
        stride = [term for term in self.terms if term[0] == name][0][2]
        self.terms = [term for term in self.terms if term[0] != name]
        for step in range(1, size):
            source = lax.rem(me + size - step, size)
            offset = self.full_place(self.terms) + source * stride
            ref = self.full.at[pl.ds(offset, self.length)]
            self.links.copy(ref, ref, self.first + step - 1, peer(source)).wait_recv()
        self.length = self.length * size


def block_kernel(
    stop,
    plan,
    x_ref,
    cells_ref,
    cot_ref,
    wq_ref,
    wk_ref,
    wv_ref,
    wp_ref,
    fc1_ref,
    fb1_ref,
    fc2_ref,
    g1_ref,
    b1_ref,
    pb_ref,
    g2_ref,
    b2_ref,
    fb2_ref,
    posw_ref,
    gate_ref,
    out_ref,
    gi_ref,
    mlp_ref,
    att_ref,
    small_ref,
    x_s,
    cot_s,
    w_s,
    w_t,
    share_s,
    fc_s,
    vec_s,
    cells_s,
    hot,
    norm_s,
    ncan,
    qkv,
    att_t,
    gcan,
    pos_b,
    pos_s,
    con_b,
    con_s,
    att_s,
    mid_s,
    n2_s,
    cb_s,
    hid,
    dbef,
    gm_s,
    acc,
    mlp_part,
    mlp_core,
    mlp_pair,
    mlp_tensor,
    mlp_sum,
    mlp_arrived,
    att_part,
    att_arrived,
    mlp_full,
    att_full,
    small_s,
    small_arrived,
    local_sem,
    send_sem,
    recv_sem,
):
    D, rows, lanes = plan.width, plan.rows, plan.lanes
    windows = plan.windows
    links = Links(plan, send_sem, recv_sem)
    t, core = links.t, links.core
    other_core = (links.d + 1 - 2 * core, t)

    def local(source, target, number):
        return pltpu.make_async_copy(source, target, local_sem.at[number])

    loads = [
        local(x_ref, x_s, 0),
        local(fc1_ref, share_s.at[0], 1),
        local(fc2_ref, share_s.at[1], 2),
        local(wq_ref, w_s.at[0], 3),
        local(wk_ref, w_s.at[1], 4),
        local(wv_ref, w_s.at[2], 5),
        local(wp_ref, w_s.at[3], 6),
        local(cot_ref, cot_s, 7),
    ]
    for load in loads:
        load.start()
    links.greet()

    def position(g, carry):
        heads = [g * (HEADS // GROUPS) + i for i in range(HEADS // GROUPS)]
        sigs = [1.0 / (1.0 + jnp.exp(-jnp.full((1, TOK), gate_ref[0, h], F32))) for h in heads]
        for big, store in ((True, pos_b), (False, pos_s)):
            col_off, row_off, dist, live = offsets(big)
            logits = [
                jnp.where(
                    live,
                    posw_ref[0, h] * col_off + posw_ref[1, h] * row_off + posw_ref[2, h] * dist,
                    FAR,
                )
                for h in heads
            ]
            tops = [jnp.max(item, axis=0, keepdims=True) for item in logits]
            exps = [jnp.exp(item - top) for item, top in zip(logits, tops)]
            totals = [sig / jnp.sum(e, axis=0, keepdims=True) for sig, e in zip(sigs, exps)]
            for h, e, total in zip(heads, exps, totals):
                store[h] = e * total
        return carry

    lax.fori_loop(0, GROUPS, position, 0)
    parts = list(range(plan.mains)) + (["tail"] if plan.tails else [])

    def hidden_lanes(owner, holder, part):
        turn = lax.rem(owner - holder - 1 + plan.tensor, plan.tensor)
        if part == "tail":
            start = plan.first_tail * CHUNK + owner * LANES
            return pl.ds(pl.multiple_of(start, LANES), LANES)
        own = turn == plan.tensor - 1
        step = jnp.where(own, plan.own_step[part], plan.other_step[part] + turn)
        return pl.ds(pl.multiple_of(step * CHUNK, CHUNK), CHUNK)

    first_weight = links.take(2 * plan.tensor * len(parts))
    loads[1].wait()
    loads[2].wait()
    for part in parts:
        to = hidden_lanes(t, t, part)
        low = (plan.mains if part == "tail" else part) * CHUNK
        high = min(plan.share, low + to.size)
        for kind in range(2):
            values = share_s[kind, :, low:high]
            if kind == 0:
                bias = fb1_ref[low:high].astype(F32).reshape(1, high - low)
            else:
                bias = jnp.zeros((1, high - low), F32)
            bias = jnp.where(iota((16, high - low), 0) == 0, bias, 0.0).astype(BF16)
            values = jnp.concatenate([values, bias], axis=0)
            if to.size > high - low:
                fill = jnp.zeros((plan.tall, to.size - high + low), BF16)
                values = jnp.concatenate([values, fill], axis=1)
            fc_s[kind, :, to] = values

    def send_weights(step, at):
        to = lax.rem(t + step, plan.tensor)
        return (
            fc_s.at[core, :, hidden_lanes(t, t, parts[at])],
            fc_s.at[core, :, hidden_lanes(t, to, parts[at])],
            first_weight + len(parts) * step + at,
            (links.d, to),
        )

    def arrived_weights(step, at, kind):
        source = lax.rem(t + plan.tensor - step, plan.tensor)
        ref = fc_s.at[kind, :, hidden_lanes(source, t, parts[at])]
        return ref, ref, first_weight + len(parts) * step + at, (links.d, source)

    def handed_weights(step, at, kind):
        ref, _, number, _ = arrived_weights(step, at, kind)
        return links.copy(ref, ref, number + plan.tensor * len(parts), other_core)

    weight_copies = [(step, at) for step in range(1, plan.tensor) for at in range(len(parts))]
    links.await_greetings()
    for step, at in weight_copies:
        links.put(functools.partial(send_weights, step, at))

    def pass_weights(which=None):
        for step, at in weight_copies:
            if which is not None and at not in which:
                continue
            links.copy(*arrived_weights(step, at, core)).wait_recv()
            handed_weights(step, at, core).start()

    def wait_weights(which=None):
        for step, at in weight_copies:
            if which is not None and at not in which:
                continue
            handed_weights(step, at, 1 - core).wait_recv()
            handed_weights(step, at, core).wait_send()

    for number, ref in enumerate((g1_ref, b1_ref, pb_ref, g2_ref, b2_ref, fb2_ref)):
        for tile in range(round_up(D, LANES) // LANES):
            low, high = tile * LANES, min(D, tile * LANES + LANES)
            spread = jnp.broadcast_to(ref[:, low:high], (LANES, high - low))
            vec_s[number, low:high, :] = jnp.transpose(spread)
    GAIN1, BIAS1, PBIAS, GAIN2, BIAS2, FBIAS2 = range(6)

    acc[...] = jnp.zeros(acc.shape, F32)
    small_s[...] = jnp.zeros(small_s.shape, F32)
    for number in range(3, 7):
        loads[number].wait()
    for number in range(4):
        w_t[number] = jnp.transpose(w_s[number])
    if stop == 1:
        return

    loads[0].wait()

    def for_blocks(body, start=None, total=0.0):
        count = round_up(rows, BLOCK) // BLOCK

        def point(k, condition=None):
            if start is not None:
                timeline.point(start + total * (k + 1) / count, condition)

        def one(b, carry):
            body(pl.ds(pl.multiple_of(b * BLOCK, BLOCK), BLOCK), BLOCK)
            for k in range(rows // BLOCK):
                point(k, b == k)
            return carry

        lax.fori_loop(0, rows // BLOCK, one, 0)
        if rows % BLOCK:
            body(pl.ds(rows // BLOCK * BLOCK, rows % BLOCK), rows % BLOCK)
            point(rows // BLOCK)

    def spread(number, count):
        vector = vec_s[number]
        return jnp.concatenate([vector] * (round_up(count, LANES) // LANES), axis=1)[:, :count]

    def gather_up(number, values):
        for low in range(0, values.shape[1], LANES):
            part = values[:, low : low + LANES]
            acc[number, :D, : part.shape[1]] += part

    def norm_one(at, count):
        scaled, _ = norm_columns(x_s[:, at].astype(F32))
        normed = scaled * spread(GAIN1, count) + spread(BIAS1, count)
        norm_s[:, at] = normed.astype(BF16)

    for_blocks(norm_one)
    if rows < lanes:
        norm_s[:, rows:] = jnp.zeros((D, lanes - rows), BF16)

    def window_span(w):
        first = (w // 3) * PER_IMAGE + (w % 3) * BIG
        count = BIG if w % 3 < 2 else SMALL_CROPS * SMALL
        start = first // LANES * LANES
        return first, count, start, round_up(first + count, LANES) - start

    def window_lanes(w):
        _, _, start, width = window_span(w)
        return pl.ds(start, width)

    def one_hot(w):
        first, count, start, width = window_span(w)
        inside = iota((1, width), 1) + (start - first)
        token = cells_s[:, window_lanes(w)]
        if w % 3 == 2:
            crop = jnp.floor((inside.astype(F32) + 0.5) * (1.0 / SMALL)).astype(jnp.int32)
            token = token + crop * STRIDE
        token = jnp.where((inside >= 0) & (inside < count), token, -1)
        return jnp.where(iota((TOK, width), 0) == token, 1.0, 0.0).astype(BF16)

    cells_s[...] = jnp.full(cells_s.shape, -1, jnp.int32)
    cells_s[:, :rows] = cells_ref[...].reshape(1, rows)
    for w in range(windows):
        hot[w, :, : window_span(w)[3]] = one_hot(w)

    def to_grid(w):
        return dot(norm_s[:, window_lanes(w)], hot[w, :, : window_span(w)[3]], NT).astype(BF16)

    def from_grid(values, w):
        return dot(values, hot[w, :, : window_span(w)[3]])

    for w in range(windows):
        ncan[w] = to_grid(w)

    def project(w, carry):
        canonical = ncan[w]
        for part in range(3):
            qkv[w, part * D : part * D + D, :] = dot(w_t[part], canonical).astype(BF16)
        return carry

    lax.fori_loop(0, windows, project, 0)
    if stop == 2:
        return

    extra_b = extra_rows(True)
    extra_s = extra_rows(False)

    def head_rows(part, h):
        return pl.ds(pl.multiple_of(part * D + h * HEAD_DIM, 16), HEAD_DIM)

    def window_kind(w):
        image, slot = w // 3, w % 3
        if slot < 2:
            return KEYS_BIG, pos_b, con_b, image * BIG_CROPS + slot, extra_b, whole, whole
        return KEYS_SMALL, pos_s, con_s, image, extra_s, own_crop, all_crops

    window_groups = [range(windows)]

    def forward_head(h, carry):
        sig = 1.0 / (1.0 + jnp.exp(-jnp.full((1, TOK), gate_ref[0, h], F32)))
        for group in window_groups:
            kinds = [window_kind(w) for w in group]
            scores = []
            for w, kind in zip(group, kinds):
                extra_q, extra_k = kind[4]
                q = jnp.concatenate([qkv[w, head_rows(0, h), :], extra_q], axis=0)
                k = jnp.concatenate([qkv[w, head_rows(1, h), :], extra_k], axis=0)
                scores.append(kind[5](dot(k[:, : kind[0]], q, TN)))
            tops = [jnp.max(s, axis=0, keepdims=True) for s in scores]
            exps = [jnp.exp2((s - top) * (SCALE * LOG2E)) for s, top in zip(scores, tops)]
            totals = [1.0 / jnp.sum(e, axis=0, keepdims=True) for e in exps]
            contents = [e * total for e, total in zip(exps, totals)]
            for kind, content in zip(kinds, contents):
                kind[2][h, kind[3]] = content.astype(BF16)
            mixtures = [
                kind[6]((1.0 - sig) * content + kind[1][h]).astype(BF16)
                for kind, content in zip(kinds, contents)
            ]
            for w, kind, mixture in zip(group, kinds, mixtures):
                v = qkv[w, head_rows(2, h), : kind[0]]
                att_t[w, head_rows(0, h), :] = dot(v, mixture).astype(BF16)
        return carry

    lax.fori_loop(0, HEADS, forward_head, 0)
    by_parts = not plan.solo and plan.own_first >= 2
    early = list(range(min(2, plan.mains)))
    later = [at for at in range(plan.mains) if at not in early]
    if by_parts:
        pass_weights(early)
    if stop == 3:
        return

    att_s[...] = jnp.zeros(att_s.shape, F32)
    for w in range(windows):
        att_s[:, window_lanes(w)] += from_grid(att_t[w], w)

    loads[7].wait()
    def norm_two(at, count):
        values = dot(w_t[3], att_s[:, at].astype(BF16))
        middle = x_s[:, at].astype(F32) + values + spread(PBIAS, count)
        mid_s[:, at] = middle
        scaled, _ = norm_columns(middle)
        n2_s[:D, at] = (scaled * spread(GAIN2, count) + spread(BIAS2, count)).astype(BF16)
        rounded = cot_s[:, at].astype(BF16)
        cb_s[:D, at] = rounded
        gather_up(3, rounded.astype(F32))
        att_s[:, at] = middle + spread(FBIAS2, count)

    for_blocks(norm_two)
    gm_s[...] = jnp.zeros(gm_s.shape, F32)
    if not plan.solo and plan.own_first < 2:
        pass_weights()
        wait_weights()
    n2_s[D:, :] = jnp.where(iota((16, rows), 0) == 0, 1.0, 0.0).astype(BF16)
    cb_s[D:, :] = jnp.zeros((16, rows), BF16)
    if stop == 4:
        return

    spans = [(low, min(CHUNK, rows - low)) for low in range(0, rows, CHUNK)]

    def activate(s, slot):
        cs = pl.ds(pl.multiple_of(s * CHUNK, CHUNK), CHUNK)
        up = jnp.transpose(fc_s[0, :, cs])
        down = jnp.transpose(fc_s[1, :, cs])
        for low, count in spans:
            at = pl.ds(low, count)
            before = dot(up, n2_s[:, at])
            dh = dot(down, cb_s[:, at])
            active, slope = gelu_parts(before)
            hid[slot, :, at] = active.astype(BF16)
            dbef[slot, :, at] = (dh * slope).astype(BF16)

    def consume(s, slot):
        cs = pl.ds(pl.multiple_of(s * CHUNK, CHUNK), CHUNK)
        for kind, left, right in ((0, n2_s, dbef), (1, cb_s, hid)):
            grad = dot(left[...], right[slot], NT).astype(BF16)
            for half in range(2):
                blocks = grad[:, half * LANES : half * LANES + LANES]
                mlp_part[kind, s, half] = blocks.reshape((plan.tile_rows,) + TILE)
        for low, count in spans:
            at = pl.ds(low, count)
            att_s[:, at] += dot(fc_s[1, :D, cs], hid[slot, :, at])
            gm_s[:, at] += dot(fc_s[0, :D, cs], dbef[slot, :, at])

    first_core = links.take(plan.steps)
    first_pair = links.take(plan.steps)
    first_tensor = links.take((plan.tensor - 1) * plan.tiles)
    timeline = Timeline()

    def core_copy(s):
        return links.copy(mlp_part.at[1 - core, s], mlp_core.at[s], first_core + s, other_core)

    rows_here = pl.ds(links.pair * plan.pair_rows, plan.pair_rows)
    rows_there = pl.ds((1 - links.pair) * plan.pair_rows, plan.pair_rows)
    other_pair = (links.d + 2 - 4 * links.pair, t)

    def pair_copy(s):
        source = mlp_part.at[core, s, :, rows_there]
        return links.copy(source, mlp_pair.at[s], first_pair + s, other_pair)

    def tensor_copy(s, half, tile, turn):
        to = lax.rem(t + 1 + turn, plan.tensor)
        return (
            mlp_part.at[core, s, half, rows_here],
            mlp_tensor.at[turn, tile],
            first_tensor + turn * plan.tiles + tile,
            (links.d, to),
        )

    def core_sum(s):
        links.copy(mlp_core.at[s], mlp_core.at[s], first_core + s, other_core).wait_recv()
        total = mlp_part[core, s].astype(F32) + mlp_core[s].astype(F32)
        mlp_part[core, s] = total.astype(BF16)
        pair_copy(s).start()

    def pair_sum(s):
        links.copy(mlp_pair.at[s], mlp_pair.at[s], first_pair + s, other_pair).wait_recv()
        total = mlp_part[core, s, :, rows_here].astype(F32) + mlp_pair[s].astype(F32)
        mlp_part[core, s, :, rows_here] = total.astype(BF16)
        kind, j, turn = plan.roles[s]
        if kind == "main" and turn < plan.tensor - 1:
            for half in range(2):
                links.copy(*tensor_copy(s, half, 2 * j + half, turn)).start()
        if kind == "tail" and plan.tensor > 1:
            for half in range(2):
                turn = lax.rem(2 * j + half - t - 1 + plan.tensor, plan.tensor)

                def send(turn=turn, half=half):
                    links.copy(*tensor_copy(s, half, plan.tiles - 1, turn)).start()

                pl.when(turn < plan.tensor - 1)(send)

    def collect(number):
        start = sum(plan.piece_blocks[:number]) // plan.pairs
        for at, tile in enumerate(plan.pieces[number]):
            for turn in range(plan.tensor - 1):
                ref = mlp_tensor.at[turn, tile]
                source = lax.rem(t - turn - 1 + plan.tensor, plan.tensor)
                links.copy(
                    ref, ref, first_tensor + turn * plan.tiles + tile, (links.d, source)
                ).wait_recv()
            if tile < 2 * plan.mains:
                step, half = plan.own_step[tile // 2], tile % 2
            else:
                step, half = plan.first_tail + t // 2, t % 2
            total = mlp_part[core, step, half, rows_here].astype(F32)
            for turn in range(plan.tensor - 1):
                total += mlp_tensor[turn, tile].astype(F32)
            low = start + at * plan.pair_rows
            mlp_sum[low : low + plan.pair_rows] = total.astype(BF16)
        low = start + len(plan.pieces[number]) * plan.pair_rows
        high = start + plan.piece_blocks[number] // plan.pairs
        if low < high:
            mlp_sum[low:high] = jnp.zeros((high - low,) + TILE, BF16)

    mlp_sums = []
    for number, size in enumerate(plan.piece_blocks):
        start = sum(plan.piece_blocks[:number])
        share = pl.ds(start // plan.pairs, size // plan.pairs)
        mlp_sums.append(
            Reduction(
                links,
                mlp_sum.at[share],
                size // plan.pairs,
                mlp_arrived.at[share],
                mlp_full,
                start,
                ("quad",),
                ("quad", "pair", "core"),
                held=(("pair", size // plan.pairs), ("core", plan.mlp_blocks)),
            )
        )
    summed = {}
    begun = set()

    def needed(number):
        tail = any(tile >= 2 * plan.mains for tile in plan.pieces[number])
        return [
            s
            for s, (kind, j, turn) in enumerate(plan.roles)
            if (kind == "tail" and tail) or (kind == "main" and 2 * j in plan.pieces[number])
        ]

    def step_done(s, now):
        summed[s] = now
        for number in range(len(plan.pieces)):
            steps = needed(number)
            if number in begun or any(step not in summed for step in steps):
                continue
            begun.add(number)
            sent = [
                summed[step]
                for step in steps
                if plan.roles[step][0] == "tail" or plan.roles[step][2] < plan.tensor - 1
            ]
            timeline.add(
                max([now] + [at + SENT for at in sent]),
                mlp_sums[number].actions(functools.partial(collect, number), MLP_PACES[number]),
                f"mlp{number}",
            )

    def begin_step(s, now):
        timeline.add(
            now,
            [
                (lambda: core_copy(s).start(), DELAYS["core"], None),
                (lambda: core_sum(s), DELAYS["pair"], None),
                (lambda: pair_sum(s), 0.0, functools.partial(step_done, s)),
            ],
            f"step{s}",
        )

    awaited = set()

    def before_step(s):
        if s == 2 and plan.tails:
            pass_weights([plan.mains])
        if s >= plan.steps:
            return
        kind, j, turn = plan.roles[s]
        at = plan.mains if kind == "tail" else j
        if (kind == "tail" or turn < plan.tensor - 1) and at not in awaited:
            awaited.add(at)
            wait_weights([at])

    activate(0, 0)
    if by_parts:
        pass_weights(later)
        before_step(1)

    def mlp_step(s, carry):
        consume(s - 1, (s - 1) % 2)
        activate(s, s % 2)
        if not plan.solo:
            for k in range(1, plan.steps):
                if by_parts:
                    pl.when(s == k)(functools.partial(before_step, k + 1))
                begin_step(k - 1, MLP_STEP * k)
                timeline.point(MLP_STEP * k, s == k)
        return carry

    lax.fori_loop(1, plan.steps, mlp_step, 0)
    last = plan.steps - 1
    consume(last, last % 2)
    now = MLP_STEP * plan.steps
    if not plan.solo:
        begin_step(last, now)
        timeline.point(now)
    if stop == 5:
        return

    def norm_two_back(at, count):
        n2_s[:D, at] = att_s[:, at].astype(BF16)
        grad = gm_s[:, at]
        scaled, inverse = norm_columns(mid_s[:, at])
        back = norm_back(grad, scaled, inverse, spread(GAIN2, count))
        grad_middle = cot_s[:, at] + back
        cot_s[:, at] = grad_middle
        branch = grad_middle.astype(BF16)
        norm_s[:, at] = branch
        gather_up(0, grad * scaled)
        gather_up(1, grad)
        gather_up(2, branch.astype(F32))

    for_blocks(norm_two_back, now, NORM_TIME)
    store_out = local(n2_s.at[pl.ds(0, D)], out_ref, 8)
    store_out.start()

    now += NORM_TIME

    wide = pl.ds(round_up(D, LANES), D)
    for w in range(windows):
        gcan[w] = to_grid(w)
        timeline.point(now + GRID_TIME * (w + 1))
    now += GRID_TIME * windows
    gm_s[:, wide] = sum(dot(att_t[w], gcan[w], NT) for w in range(windows))

    def project_back(w, carry):
        att_t[w] = dot(w_s[3], gcan[w]).astype(BF16)
        for k in range(windows):
            timeline.point(now + PROJECT_TIME * (k + 1), w == k)
        return carry

    lax.fori_loop(0, windows, project_back, 0)
    now += PROJECT_TIME * windows
    if stop == 6:
        return

    def att_blocks_at(number, at, count):
        return pl.ds(number * plan.att_blocks + at, count)

    def att_start(number, total):
        gm_s[:, :D] = total
        for tile in range(plan.width_tiles):
            blocks = gm_s[:, tile * LANES : tile * LANES + LANES].astype(BF16)
            at = att_blocks_at(number, tile * (D // 16), D // 16)
            att_part[at] = blocks.reshape((D // 16,) + TILE)
        edge = gm_s[:, plan.width_tiles * LANES : plan.width_tiles * LANES + LANES]
        low = D - plan.fold
        lane = iota((low, LANES), 1)
        folded = jnp.where(
            lane < plan.left_over, edge[:low], pltpu.roll(edge[plan.fold :], plan.left_over, 1)
        )
        folded = jnp.concatenate([folded, edge[low : plan.fold]], axis=0).astype(BF16)
        at = att_blocks_at(number, plan.full_blocks, plan.fold // 16)
        att_part[at] = folded.reshape((plan.fold // 16,) + TILE)
        used = plan.full_blocks + plan.fold // 16
        at = att_blocks_at(number, used, 1)
        att_part[at] = small_s[16:, :].astype(BF16).reshape((1,) + TILE)
        if plan.att_blocks > used + 1:
            spare = plan.att_blocks - used - 1
            at = att_blocks_at(number, used + 1, spare)
            att_part[at] = jnp.zeros((spare,) + TILE, BF16)

    def vector_sums(numbers, row):
        for place, number in enumerate(numbers):
            for tile in range(round_up(D, LANES) // LANES):
                turned = jnp.transpose(acc[number, tile * LANES : tile * LANES + LANES, :])
                at = row + 4 * place + tile
                small_s[at : at + 1, :] = jnp.sum(turned, axis=0, keepdims=True)

    direct = plan.direct
    routes = [(("core", "pair", "quad"), ("quad", "pair", "core"), "tensor")] * len(BUNDLES)
    if direct:
        routes = [(("core", "cross", "quad"), ("quad", "cross", "core"))] * (len(BUNDLES) - 1)
        routes.append((("core", "all"), ("all", "core")))
    att_sums = []
    for bundle, route in zip(BUNDLES, routes):
        start, size = bundle[0] * plan.att_blocks, len(bundle) * plan.att_blocks
        arrived = pl.ds(bundle[0] * plan.att_arrived, len(bundle) * plan.att_arrived)
        att_sums.append(
            Reduction(
                links,
                att_part.at[pl.ds(start, size)],
                size,
                att_arrived.at[arrived],
                att_full,
                start,
                *route,
            )
        )

    def begin_att(number, now):
        for at, bundle in enumerate(BUNDLES):
            if bundle[-1] == number:
                timeline.add(now, att_sums[at].actions(pace=ATT_PACES[at]), f"att{at}")

    vector_sums(range(4), 16)
    att_start(0, gm_s[:, wide])
    if not plan.solo:
        begin_att(0, now)
        timeline.point(now)

    def weight_grad(g):
        def joined(w):
            parts = [
                qkv[w, pl.ds(pl.multiple_of(part * D + g * (D // GROUPS), 16), D // GROUPS), :]
                for part in range(3)
            ]
            return jnp.concatenate(parts, axis=0)

        total = dot(ncan[0], joined(0), NT)
        for w in range(1, windows):
            total += dot(ncan[w], joined(w), NT)
        att_start(1 + g, total)

    window_groups = [range(windows)]

    def backward_head(h, carry):
        sig = 1.0 / (1.0 + jnp.exp(-jnp.full((1, TOK), gate_ref[0, h], F32)))
        keep = 1.0 - sig
        factor = keep * SCALE
        sums = [0.0, 0.0]
        gate_row = jnp.zeros((1, TOK), F32)
        for group in window_groups:
            kinds = [window_kind(w) for w in group]
            queries = [qkv[w, head_rows(0, h), :] for w in group]
            keys = [qkv[w, head_rows(1, h), : kind[0]] for w, kind in zip(group, kinds)]
            vals = [qkv[w, head_rows(2, h), : kind[0]] for w, kind in zip(group, kinds)]
            grads = [att_t[w, head_rows(0, h), :] for w in group]
            contents = [kind[2][h, kind[3]].astype(F32) for kind in kinds]
            grad_mixes = [
                kind[5](dot(v, da, TN)) for kind, v, da in zip(kinds, vals, grads)
            ]
            mixtures = [
                kind[6](keep * content + kind[1][h]).astype(BF16)
                for kind, content in zip(kinds, contents)
            ]
            grad_vals = [dot(da, mixture, NT) for da, mixture in zip(grads, mixtures)]
            rows_sum = [
                jnp.sum(content * grad_mix, axis=0, keepdims=True)
                for content, grad_mix in zip(contents, grad_mixes)
            ]
            grad_scores = [
                kind[6](content * (grad_mix - row)).astype(BF16)
                for kind, content, grad_mix, row in zip(kinds, contents, grad_mixes, rows_sum)
            ]
            for w, grad_mix, row in zip(group, grad_mixes, rows_sum):
                sums[w % 3 // 2] += grad_mix
                gate_row -= row
            grad_queries = [dot(k, grad_s) for k, grad_s in zip(keys, grad_scores)]
            grad_keys = [dot(q, grad_s, NT) for q, grad_s in zip(queries, grad_scores)]
            for w, kind, dq, dk, dv in zip(group, kinds, grad_queries, grad_keys, grad_vals):
                qkv[w, head_rows(0, h), :] = (dq * factor).astype(BF16)
                qkv[w, head_rows(1, h), : kind[0]] = (dk * factor[:, : kind[0]]).astype(BF16)
                qkv[w, head_rows(2, h), : kind[0]] = dv.astype(BF16)
        results = [jnp.zeros((1, TOK), F32)] * 3
        for big, pos, grad_mix in ((True, pos_b, sums[0]), (False, pos_s, sums[1])):
            col_off, row_off, dist, _ = offsets(big)
            row = jnp.sum(pos[h] * grad_mix, axis=0, keepdims=True) / sig
            grad_l = pos[h] * (grad_mix - row)
            gate_row += row
            results = [
                old + jnp.sum(grad_l * off, axis=0, keepdims=True)
                for old, off in zip(results, (col_off, row_off, dist))
            ]
        results = jnp.concatenate(results + [gate_row * sig * keep], axis=0)
        column = jnp.sum(results, axis=1, keepdims=True)
        lane = iota((4, LANES), 1)
        small_s[8:12, :] += jnp.where(lane == h, column, 0.0)
        pl.when(h % (HEADS // GROUPS) == HEADS // GROUPS - 1)(
            lambda: weight_grad(h // (HEADS // GROUPS))
        )
        if not plan.solo:
            for k in range(HEADS):
                time = now + HEAD_TIME * (k + 1) + GRADIENT_TIME * ((k + 1) // (HEADS // GROUPS))
                if k % (HEADS // GROUPS) == HEADS // GROUPS - 1:
                    begin_att(1 + k // (HEADS // GROUPS), time)
                timeline.point(time, h == k)
        return carry

    lax.fori_loop(0, HEADS, backward_head, 0)
    now += HEAD_TIME * HEADS + GRADIENT_TIME * GROUPS
    if stop == 7:
        return

    att_s[...] = jnp.zeros(att_s.shape, F32)

    for first in range(0, windows, TOGETHER):
        group = range(first, min(first + TOGETHER, windows))
        grads = [dot(w_s[0], qkv[w, :D, :]) for w in group]
        grads = [grad + dot(w_s[1], qkv[w, D : 2 * D, :]) for grad, w in zip(grads, group)]
        grads = [grad + dot(w_s[2], qkv[w, 2 * D :, :]) for grad, w in zip(grads, group)]
        highs = [grad.astype(BF16) for grad in grads]
        lows = [(grad - high.astype(F32)).astype(BF16) for grad, high in zip(grads, highs)]
        for w, high, low in zip(group, highs, lows):
            att_s[:, window_lanes(w)] += from_grid(high, w) + from_grid(low, w)
        timeline.point(now + WINDOW_TIME * (group[-1] + 1))
    now += WINDOW_TIME * windows

    def norm_one_back(at, count):
        scaled, inverse = norm_columns(x_s[:, at].astype(F32))
        grad = att_s[:, at]
        cot_s[:, at] += norm_back(grad, scaled, inverse, spread(GAIN1, count))
        gather_up(4, grad * scaled)
        gather_up(5, grad)

    for_blocks(norm_one_back, now, NORM_TIME)
    store_gi = local(cot_s, gi_ref, 9)
    store_gi.start()
    vector_sums((4, 5), 0)

    now += NORM_TIME
    small_places = {}

    def small_begin(name):
        size, me, peer = links.group(name)
        first = links.take(size - 1)
        used = sum(size for size, _ in small_places.values())
        small_places[name] = size, first
        small_arrived[used + me] = small_s[:SMALL_ROWS, :]

        def make(step):
            slot = small_arrived.at[used + me]
            return slot, slot, first + step - 1, peer(lax.rem(me + step, size))

        for step in range(1, size):
            links.put(functools.partial(make, step))

    def small_end(name):
        size, me, peer = links.group(name)
        _, first = small_places[name]
        used = sum(size for size, _ in small_places.values()) - size
        for step in range(1, size):
            source = lax.rem(me + size - step, size)
            ref = small_arrived.at[used + source]
            links.copy(ref, ref, first + step - 1, peer(source)).wait_recv()
        total = small_arrived[used]
        for other in range(1, size):
            total += small_arrived[used + other]
        small_s[:SMALL_ROWS, :] = total

    names = ("core", "all") if direct else ("core", "tensor", "pair", "quad")
    names = [name for name in names if links.group(name)[0] > 1]
    if names:
        actions = [(functools.partial(small_begin, names[0]), DELAYS[names[0]], None)]
        for before, name in zip(names, names[1:]):

            def turn(before=before, name=name):
                small_end(before)
                small_begin(name)

            actions.append((turn, DELAYS[name], None))
        actions.append((functools.partial(small_end, names[-1]), 0.0, None))
        timeline.add(now, actions, "small")
    timeline.finish(now)
    small_ref[...] = small_s[:SMALL_ROWS, :]
    stores = [local(mlp_full, mlp_ref, 10), local(att_full, att_ref, 11)]
    for store in stores:
        store.start()
    store_out.wait()
    store_gi.wait()
    if not plan.solo:
        for s in range(plan.steps):
            core_copy(s).wait_send()
            pair_copy(s).wait_send()
        for s, (kind, j, turn) in enumerate(plan.roles):
            if kind == "main" and turn < plan.tensor - 1:
                for half in range(2):
                    links.copy(*tensor_copy(s, half, 2 * j + half, turn)).wait_send()
        if plan.tails:
            for turn in range(plan.tensor - 1):
                owner = lax.rem(t + 1 + turn, plan.tensor)
                links.copy(
                    *tensor_copy(plan.first_tail + owner // 2, owner % 2, plan.tiles - 1, turn)
                ).wait_send()
    links.drain()
    for store in stores:
        store.wait()


def finish_kernel(
    plan,
    out_in,
    gi_in,
    mlp_in,
    att_in,
    small_in,
    out_ref,
    gi_ref,
    dq_ref,
    dk_ref,
    dv_ref,
    dproj_ref,
    dfc1_ref,
    dfc2_ref,
    dfb1_ref,
    pos_ref,
    gate_ref,
    *refs
):
    vector_refs, (mlp_s, att_s, square_s, wide_s, out_s, gi_s, sems) = refs[:6], refs[6:]
    D = plan.width
    def copy(source, target, number):
        return pltpu.make_async_copy(source, target, sems.at[number])

    size = plan.mlp_blocks
    loads = [copy(mlp_in.at[pl.ds(kind * size, size)], mlp_s.at[kind], kind) for kind in range(2)]
    loads.append(copy(att_in, att_s, 2))
    third = D // 3
    spans = [pl.ds(k * third, third) for k in range(3)]
    through = [(out_in, out_s, out_ref), (gi_in, gi_s, gi_ref)]
    arrive = [
        copy(source.at[span], held.at[span], 3 + 3 * at + k)
        for at, (source, held, _) in enumerate(through)
        for k, span in enumerate(spans)
    ]
    leave = [
        copy(held.at[span], target.at[span], 9 + 3 * at + k)
        for at, (_, held, target) in enumerate(through)
        for k, span in enumerate(spans)
    ]
    for item in loads + arrive:
        item.start()
    stores = []

    def store(source, target):
        stores.append(copy(source, target, 15 + len(stores)))
        stores[-1].start()

    where = {
        tile: (sum(plan.piece_blocks[:number]), plan.piece_blocks[number], at)
        for number, piece in enumerate(plan.pieces)
        for at, tile in enumerate(piece)
    }
    for kind, target in enumerate((dfc1_ref, dfc2_ref)):
        loads[kind].wait()
        for pair in range(plan.pairs):
            top = pair * plan.pair_rows * 16
            bottom = min(D, top + plan.pair_rows * 16)
            for tile in range(plan.tiles):
                start, count, at = where[tile]
                first = start + pair * (count // plan.pairs) + at * plan.pair_rows
                values = mlp_s[kind, first : first + plan.pair_rows]
                values = values.reshape(plan.pair_rows * 16, LANES).astype(F32)
                low, high = tile * LANES, min(plan.share, tile * LANES + LANES)
                wide_s[kind, top:bottom, low:high] = values[: bottom - top, : high - low]
                if kind == 0 and pair == plan.pairs - 1:
                    bias = values[D - top : D - top + 1, : high - low]
                    dfb1_ref[low:high] = bias.reshape(high - low)
            span = pl.ds(top, bottom - top)
            store(wide_s.at[kind, span], target.at[span])
        if kind == 0:
            for item, onward in zip(arrive, leave):
                item.wait()
                onward.start()
    loads[2].wait()
    below = D - plan.fold
    part = D // GROUPS
    for number in range(GROUPS + 1):
        first = number * plan.att_blocks
        tiles = [
            att_s[pl.ds(first + tile * (D // 16), D // 16)].reshape(D, LANES).astype(F32)
            for tile in range(plan.width_tiles)
        ]
        folded = att_s[pl.ds(first + plan.full_blocks, plan.fold // 16)]
        folded = folded.reshape(plan.fold, LANES).astype(F32)
        lower = pltpu.roll(folded, LANES - plan.left_over, 1)[:below]
        edge = jnp.concatenate([folded, lower], axis=0)[:, : plan.left_over]
        total = jnp.concatenate(tiles + [edge], axis=1)
        if number == 0:
            square_s[0] = total
            store(square_s.at[0], dproj_ref)
        else:
            to = (number - 1) * part
            for place in range(3):
                square_s[1 + place, :, to : to + part] = total[:, place * part : place * part + part]
    for place, target in enumerate((dq_ref, dk_ref, dv_ref)):
        store(square_s.at[1 + place], target)
    early = att_s[plan.full_blocks + plan.fold // 16].astype(F32)
    for number, target in enumerate(vector_refs):
        for tile in range(round_up(D, LANES) // LANES):
            low, high = tile * LANES, min(D, tile * LANES + LANES)
            row = number % 4 * 4 + tile
            source = early if number < 4 else small_in[...]
            target[:, low:high] = source[row : row + 1, : high - low]
    pos_ref[...] = small_in[8:11, :HEADS]
    gate_ref[...] = small_in[11:12, :HEADS].reshape(HEADS)
    for item in stores + leave:
        item.wait()


def local(
    stop,
    dp,
    tensor,
    inputs,
    patch_cells,
    ln1_gain,
    ln1_bias,
    w_query,
    w_key,
    w_value,
    w_proj,
    proj_bias,
    pos_weight,
    gate_param,
    ln2_gain,
    ln2_bias,
    fc1_weight,
    fc1_bias,
    fc2_weight,
    fc2_bias,
    cotangent,
):
    rows, D = inputs.shape
    share = fc1_weight.shape[1]
    plan = Plan(dp, tensor, rows, D, share)
    windows, lanes, steps = plan.windows, plan.lanes, plan.steps

    def vector(values):
        return values.reshape(1, -1)

    vmem = pl.BlockSpec(memory_space=pltpu.VMEM)
    smem = pl.BlockSpec(memory_space=pltpu.SMEM)
    anywhere = pl.BlockSpec(memory_space=pl.ANY)
    params = {} if plan.solo else {"collective_id": 0, "has_side_effects": True}
    slots = plan.cores + plan.tensor + plan.pairs + plan.quads
    if plan.direct:
        slots = plan.cores + tensor * dp // plan.cores
    out, gi, mlp, att, small = pl.pallas_call(
        functools.partial(block_kernel, stop, plan),
        out_shape=(
            jax.ShapeDtypeStruct((D, rows), BF16),
            jax.ShapeDtypeStruct((D, rows), F32),
            jax.ShapeDtypeStruct((2 * plan.mlp_blocks,) + TILE, BF16),
            jax.ShapeDtypeStruct(((GROUPS + 1) * plan.att_blocks,) + TILE, BF16),
            jax.ShapeDtypeStruct((SMALL_ROWS, LANES), F32),
        ),
        in_specs=[anywhere, vmem] + [anywhere] * 6 + [vmem] + [anywhere] + [vmem] * 6 + [smem] * 2,
        out_specs=(anywhere, anywhere, anywhere, anywhere, vmem),
        scratch_shapes=[
            pltpu.VMEM((D, rows), BF16),
            pltpu.VMEM((D, rows), F32),
            pltpu.VMEM((4, D, D), BF16),
            pltpu.VMEM((4, D, D), BF16),
            pltpu.VMEM((2, D, share), BF16),
            pltpu.VMEM((2, plan.tall, plan.hidden), BF16),
            pltpu.VMEM((6, D, LANES), F32),
            pltpu.VMEM((1, lanes), jnp.int32),
            pltpu.VMEM((windows, TOK, WIDE), BF16),
            pltpu.VMEM((D, lanes), BF16),
            pltpu.VMEM((windows, D, TOK), BF16),
            pltpu.VMEM((windows, 3 * D, TOK), BF16),
            pltpu.VMEM((windows, D, TOK), BF16),
            pltpu.VMEM((windows, D, TOK), BF16),
            pltpu.VMEM((HEADS, KEYS_BIG, TOK), F32),
            pltpu.VMEM((HEADS, STRIDE, TOK), F32),
            pltpu.VMEM((HEADS, BIG_CROPS * plan.images, KEYS_BIG, TOK), BF16),
            pltpu.VMEM((HEADS, plan.images, STRIDE, TOK), BF16),
            pltpu.VMEM((D, lanes), F32),
            pltpu.VMEM((D, lanes), F32),
            pltpu.VMEM((plan.tall, rows), BF16),
            pltpu.VMEM((plan.tall, rows), BF16),
            pltpu.VMEM((2, CHUNK, rows), BF16),
            pltpu.VMEM((2, CHUNK, rows), BF16),
            pltpu.VMEM((D, lanes), F32),
            pltpu.VMEM((6, round_up(D, LANES), LANES), F32),
            pltpu.VMEM((2, steps, 2, plan.tile_rows) + TILE, BF16),
            pltpu.VMEM((steps, 2, plan.tile_rows) + TILE, BF16),
            pltpu.VMEM((steps, 2, plan.pair_rows) + TILE, BF16),
            pltpu.VMEM((max(1, tensor - 1), plan.tiles, plan.pair_rows) + TILE, BF16),
            pltpu.VMEM((plan.mlp_blocks // plan.pairs,) + TILE, BF16),
            pltpu.VMEM((plan.mlp_blocks // plan.pairs,) + TILE, BF16),
            pltpu.VMEM(((GROUPS + 1) * plan.att_blocks,) + TILE, BF16),
            pltpu.VMEM(((GROUPS + 1) * plan.att_arrived,) + TILE, BF16),
            pltpu.VMEM((2 * plan.mlp_blocks,) + TILE, BF16),
            pltpu.VMEM(((GROUPS + 1) * plan.att_blocks,) + TILE, BF16),
            pltpu.VMEM((2 * SMALL_ROWS, LANES), F32),
            pltpu.VMEM((slots, SMALL_ROWS, LANES), F32),
            pltpu.SemaphoreType.DMA((12,)),
            pltpu.SemaphoreType.DMA((plan.semaphores,)),
            pltpu.SemaphoreType.DMA((plan.semaphores,)),
        ],
        compiler_params=pltpu.CompilerParams(vmem_limit_bytes=63 * 1024 * 1024, **params),
    )(
        inputs.T,
        patch_cells,
        cotangent.T,
        w_query,
        w_key,
        w_value,
        w_proj,
        fc1_weight,
        fc1_bias,
        fc2_weight.T,
        vector(ln1_gain),
        vector(ln1_bias),
        vector(proj_bias),
        vector(ln2_gain),
        vector(ln2_bias),
        vector(fc2_bias),
        pos_weight,
        vector(gate_param),
    )
    square = jax.ShapeDtypeStruct((D, D), F32)
    wide = jax.ShapeDtypeStruct((D, share), F32)
    results = pl.pallas_call(
        functools.partial(finish_kernel, plan),
        out_shape=(
            jax.ShapeDtypeStruct((D, rows), BF16),
            jax.ShapeDtypeStruct((D, rows), F32),
        )
        + (square,) * 4
        + (wide,) * 2
        + (
            jax.ShapeDtypeStruct((share,), F32),
            jax.ShapeDtypeStruct((3, HEADS), F32),
            jax.ShapeDtypeStruct((HEADS,), F32),
        )
        + (jax.ShapeDtypeStruct((1, D), F32),) * 6,
        in_specs=[anywhere] * 4 + [vmem],
        out_specs=(anywhere,) * 8 + (vmem,) * 9,
        scratch_shapes=[
            pltpu.VMEM((2, plan.mlp_blocks) + TILE, BF16),
            pltpu.VMEM(((GROUPS + 1) * plan.att_blocks,) + TILE, BF16),
            pltpu.VMEM((4, D, D), F32),
            pltpu.VMEM((2, D, share), F32),
            pltpu.VMEM((D, rows), BF16),
            pltpu.VMEM((D, rows), F32),
            pltpu.SemaphoreType.DMA((23,)),
        ],
        compiler_params=pltpu.CompilerParams(vmem_limit_bytes=63 * 1024 * 1024),
    )(out, gi, mlp, att, small)
    out, gi, dq, dk, dv, dproj, dfc1, dfc2, dfb1, pos, gate = results[:11]
    gain2, bias2, pbias, fbias2, gain1, bias1 = (item.reshape(D) for item in results[11:])
    return (
        out.T,
        gi.T,
        gain1,
        bias1,
        dq,
        dk,
        dv,
        dproj,
        pbias,
        pos,
        gate,
        gain2,
        bias2,
        dfc1,
        dfb1,
        dfc2.T,
        fbias2,
    )


def solution(mesh, stop=0):
    both = ("dp", "tensor")
    copied = P()
    in_specs = (
        (P(both, None), P(both))
        + (copied,) * 11
        + (P(None, "tensor"), P("tensor"), P("tensor", None), copied, P(both, None))
    )
    out_specs = (
        (P(both, None), P(both, None))
        + (copied,) * 11
        + (P(None, "tensor"), P("tensor"), P("tensor", None), copied)
    )
    return jax.shard_map(
        functools.partial(local, stop, mesh.shape["dp"], mesh.shape["tensor"]),
        mesh=mesh,
        in_specs=in_specs,
        out_specs=out_specs,
        check_vma=False,
    )
```
